32 devices in a mesh: seq: 8 (over z, x), head: 4 (over y, core).
Axes of the slice: x: 2, y: 2, z: 4, core: 2. Of those that a mesh axis runs over, the one named last changes fastest.
Arguments:
- layer_input: bfloat16 [4096, 4096], P('seq', 'head'), may hold values from -6 to 6
- query_rows: bfloat16 [4096, 4096], P('seq', 'head'), may hold values from -6 to 6
- key_rows: bfloat16 [4096, 4096], P('seq', 'head'), may hold values from -6 to 6
- value_rows: bfloat16 [4096, 4096], P('seq', 'head'), may hold values from -28 to 28
- out_weight: bfloat16 [4096, 4096], P('head'), may hold values from -0.09375 to 0.09375
- norm_gain: float32 [4096], P('head'), may hold values from 0.1 to 1.9
- cotangent: bfloat16 [4096, 4096], P('seq', 'head'), may hold values from -0.125 to 0.125
Outputs:
- projection_gradient: float32 [4096, 3, 4096], P('seq', None, 'head')
- output_gradient: float32 [4096, 4096], P('head', 'seq')
The draws below stay inside these ranges and needn't reach their ends.
All inputs are finite; a program needn't handle non-finite values.
Results may differ from the reference program's by a relative error of at most 0.023.
Values may be sent and summed in bfloat16 or wider, within the bound.
No kernel may reach another device: no remote copies, remote signals or barrier semaphores. Data moves between devices by JAX's collectives and lax.ppermute only.
A program may use at most 192 MiB of HBM per device.

```python
import math
import jax
import jax.numpy as jnp
from jax import lax

D = 4096
HEAD_DIM = 128
TOK_DEV = 512
HEADS = 32
LENGTH = 4096
N_SEQ = 8


def draw_value_rows(key, part):
    first, second = jax.random.split(key, 2)
    column_scale = jnp.exp(jax.random.uniform(second, (1, D), jnp.float32, 0.0, math.log(10.0)))
    base = jnp.clip(jax.random.normal(first, (LENGTH, D), jnp.float32), -6.0, 6.0)
    return (base * column_scale * 0.4).astype(jnp.bfloat16)


def strengthened(result, key, source, target, blocks, factor):
    owner, partner = [(jnp.arange(result.shape[dim]) // (result.shape[dim] // blocks)).reshape([-1 if axis == dim else 1 for axis in range(result.ndim)]) for dim in (source, target)]
    chosen = jax.random.permutation(key, blocks)[partner]
    strong = (owner == chosen) | (owner == (partner + blocks // 2) % blocks)
    return jnp.where(strong, factor * result, result)


def block_scale(own_key, dims, shards, low, largest):
    level = 1.0
    for position, parts in shards:
        steps = jax.random.uniform(jax.random.fold_in(jax.random.fold_in(own_key, 6), position), (parts,), jnp.float32, low / len(shards), largest / len(shards))
        level = level * jnp.repeat(jnp.exp(steps), dims[position] // parts).reshape((-1,) + (1,) * (len(dims) - 1 - position))
    return level


def normal_values(stream_key, dims, width, limit, cuts=(), kind=jnp.bfloat16):
    drawn = width * jax.random.normal(stream_key, dims, jnp.float32)
    if cuts:
        drawn = drawn * block_scale(stream_key, dims, cuts, -0.22, 0.18)
    return jnp.clip(drawn, -limit, limit).astype(kind)


def heavy_noise(stream_key, shape, deviation, most, cuts, heavy, kind=jnp.bfloat16):
    values = deviation * jax.random.normal(stream_key, shape, jnp.float32)
    if cuts:
        values = values * block_scale(stream_key, shape, cuts, -0.22, 0.18)
    return jnp.clip(strengthened(values, jax.random.fold_in(stream_key, 3), *heavy), -most, most).astype(kind)


def setup_inputs(seed: int = 0) -> dict:
    keys = jax.random.split(jax.random.key(seed), 8)
    layer_input = heavy_noise(keys[0], (LENGTH, D), 1.0, 6.0, ((0, 8), (1, 4)), (0, 1, 8, 2.0))
    query_rows = normal_values(keys[1], (LENGTH, D), 1.0, 6.0, ((0, 8), (1, 4)))
    key_rows = normal_values(keys[2], (LENGTH, D), 1.0, 6.0, ((0, 8), (1, 4)))
    value_rows = draw_value_rows(jax.random.fold_in(keys[7], 71), 0)
    out_weight = normal_values(keys[4], (D, D), D ** -0.5, 0.09375, ((0, 4),))
    norm_gain = jnp.clip(1.0 + 0.18 * jax.random.normal(keys[5], (D,), jnp.float32), 0.1, 1.9)
    cotangent = heavy_noise(keys[6], (LENGTH, D), (TOK_DEV * N_SEQ) ** -0.5, 0.125, ((0, 8), (1, 4)), (0, 1, 8, 2.0))
    return {"layer_input": layer_input, "query_rows": query_rows, "key_rows": key_rows, "value_rows": value_rows, "out_weight": out_weight, "norm_gain": norm_gain, "cotangent": cotangent}


def lower_mask(count):
    rows = lax.broadcasted_iota(jnp.int32, (count, count), 0)
    cols = lax.broadcasted_iota(jnp.int32, (count, count), 1)
    return rows >= cols

def reference(layer_input, query_rows, key_rows, value_rows, out_weight, norm_gain, cotangent):
    high = lax.Precision.HIGHEST
    blocks = N_SEQ
    tokens = TOK_DEV

    def split_heads(matrix):
        return matrix.reshape(blocks, tokens, HEADS, HEAD_DIM)
    queries = split_heads(query_rows)
    key_heads = split_heads(key_rows)
    value_heads = split_heads(value_rows)
    gain = norm_gain.reshape(HEADS, HEAD_DIM)
    lower = lower_mask(tokens)[None]
    block_state = jnp.einsum('bthd,bthe->bhde', key_heads.astype(jnp.float32), value_heads.astype(jnp.float32), precision=high)
    state_in = jnp.cumsum(block_state, axis=0) - block_state
    state_low = state_in.astype(jnp.bfloat16)
    gated_grad = jnp.dot(cotangent, out_weight.T, preferred_element_type=jnp.float32)
    gated_grad = gated_grad.reshape(blocks, tokens, HEADS, HEAD_DIM)

    def forward_block(items):
        query_b, key_b, value_b, state_b, upstream = items
        q32 = query_b.astype(jnp.float32)
        k32 = key_b.astype(jnp.float32)
        v32 = value_b.astype(jnp.float32)
        scores = jnp.einsum('thd,shd->hts', q32, k32, precision=high)
        scores = jnp.where(lower, scores, 0.0).astype(jnp.bfloat16)
        attention = jnp.einsum('hts,she->the', scores.astype(jnp.float32), v32, precision=high)
        attention = attention + jnp.einsum('thd,hde->the', q32, state_b.astype(jnp.float32), precision=high)
        rms_value = jnp.sqrt(lax.optimization_barrier(jnp.mean(attention * attention, axis=-1, keepdims=True)) + 1e-05)
        normed = attention / rms_value
        gated = (normed * gain).astype(jnp.bfloat16)
        scaled = upstream * gain
        inner = lax.optimization_barrier(jnp.mean(scaled * normed, axis=-1, keepdims=True))
        pre_grad = ((scaled - normed * inner) / rms_value).astype(jnp.bfloat16)
        p32 = pre_grad.astype(jnp.float32)
        mixing = jnp.einsum('the,she->hts', p32, v32, precision=high)
        mixing = jnp.where(lower, mixing, 0.0).astype(jnp.bfloat16)
        query_grad = jnp.einsum('hts,shd->thd', mixing.astype(jnp.float32), k32, precision=high)
        query_grad = query_grad + jnp.einsum('the,hde->thd', p32, state_b.astype(jnp.float32), precision=high)
        return (gated, pre_grad, query_grad.astype(jnp.bfloat16))
    gated, pre_grad, query_grad = lax.map(forward_block, (queries, key_heads, value_heads, state_low, gated_grad))
    grad_block = jnp.einsum('bthd,bthe->bhde', queries.astype(jnp.float32), pre_grad.astype(jnp.float32), precision=high)
    grad_state = jnp.cumsum(grad_block[::-1], axis=0)[::-1] - grad_block
    grad_low = grad_state.astype(jnp.bfloat16)

    def backward_block(items):
        query_b, key_b, value_b, pre_b, grad_b = items
        q32 = query_b.astype(jnp.float32)
        k32 = key_b.astype(jnp.float32)
        v32 = value_b.astype(jnp.float32)
        p32 = pre_b.astype(jnp.float32)
        g32 = grad_b.astype(jnp.float32)
        scores = jnp.einsum('thd,shd->hts', q32, k32, precision=high)
        scores = jnp.where(lower, scores, 0.0).astype(jnp.bfloat16)
        mixing = jnp.einsum('the,she->hts', p32, v32, precision=high)
        mixing = jnp.where(lower, mixing, 0.0).astype(jnp.bfloat16)
        key_grad = jnp.einsum('hts,thd->shd', mixing.astype(jnp.float32), q32, precision=high)
        key_grad = key_grad + jnp.einsum('she,hde->shd', v32, g32, precision=high)
        value_grad = jnp.einsum('hts,the->she', scores.astype(jnp.float32), p32, precision=high)
        value_grad = value_grad + jnp.einsum('shd,hde->she', k32, g32, precision=high)
        return (key_grad.astype(jnp.bfloat16), value_grad.astype(jnp.bfloat16))
    key_grad, value_grad = lax.map(backward_block, (queries, key_heads, value_heads, pre_grad, grad_low))
    stacked = jnp.concatenate([query_grad.reshape(blocks, tokens, D), key_grad.reshape(blocks, tokens, D), value_grad.reshape(blocks, tokens, D)], axis=2)
    inputs_b = layer_input.reshape(blocks, tokens, D)
    gated_b = gated.reshape(blocks, tokens, D)
    cot_b = cotangent.reshape(blocks, tokens, D)

    def accumulate(carry, items):
        input_block, grad_rows, gated_block, cot_block = items
        term = jnp.dot(input_block.T, grad_rows, preferred_element_type=jnp.float32)
        term = lax.optimization_barrier(term.astype(jnp.bfloat16)).astype(jnp.float32)
        out_term = jnp.dot(gated_block.T, cot_block, preferred_element_type=jnp.float32)
        out_term = lax.optimization_barrier(out_term.astype(jnp.bfloat16)).astype(jnp.float32)
        return ((carry[0] + term, carry[1] + out_term), None)
    start = (jnp.zeros((D, 3 * D), jnp.float32), jnp.zeros((D, D), jnp.float32))
    totals, unused = lax.scan(accumulate, start, (inputs_b, stacked, gated_b, cot_b))
    return (totals[0].reshape(D, 3, D), totals[1])
```

```python
import jax
import jax.numpy as jnp
from jax import lax
from jax.sharding import PartitionSpec as P

HEAD_DIM = 128
F32 = jnp.float32
BF16 = jnp.bfloat16


def flip(array, bit):
    size = lax.axis_size("seq")
    return lax.ppermute(array, "seq", [(i, i ^ (1 << bit)) for i in range(size)])


def entering(block, reverse):
    size, position = lax.axis_size("seq"), lax.axis_index("seq")
    bits = size.bit_length() - 1
    total, before = block, jnp.zeros_like(block)
    for bit in range(bits):
        step = 1 << bit
        if bit < bits - 1:
            new = flip(total.astype(BF16), bit).astype(F32)
            mine = (position >> bit) & 1
            before = before + jnp.where(mine == (0 if reverse else 1), new, 0.0)
            total = total + new
        else:
            pairs = [(i, i ^ step) for i in range(size) if bool(i & step) == reverse]
            before = before + lax.ppermute(total.astype(BF16), "seq", pairs).astype(F32)
    return before


def lower_mask(count):
    rows = lax.broadcasted_iota(jnp.int32, (count, count), 0)
    cols = lax.broadcasted_iota(jnp.int32, (count, count), 1)
    return rows >= cols


def tdot(a, b):
    return lax.dot_general(a, b, (((0,), (0,)), ((), ())), preferred_element_type=F32)


def body(layer_input, query_rows, key_rows, value_rows, out_weight, norm_gain, cotangent):
    size, position = lax.axis_size("seq"), lax.axis_index("seq")
    bits = size.bit_length() - 1
    gather_bit = 1 if bits > 1 else 0
    halving = [bit for bit in range(bits) if bit != gather_bit]
    tokens, width = query_rows.shape
    heads = width // HEAD_DIM
    model = out_weight.shape[1]
    owned = model // size

    gathered_cot = lax.all_gather(cotangent, "head", axis=1, tiled=True)
    gathered_input = lax.all_gather(layer_input, "head", axis=1, tiled=True)

    chunks = 1 << len(halving)
    order = []
    for j in range(chunks):
        toggled = 0
        for i, bit in enumerate(halving):
            if not (j >> (len(halving) - 1 - i)) & 1:
                toggled |= 1 << bit
        order.append(position ^ toggled)

    def pick(array, toggled):
        return jnp.concatenate(
            [lax.dynamic_slice_in_dim(array, (at ^ toggled) * owned, owned, 1) for at in order], axis=1
        )

    def both(array):
        mine = pick(array, 0)
        share = chunks * owned // lax.axis_size("head")
        send = pick(array, 1 << gather_bit)
        send = lax.dynamic_slice_in_dim(send, lax.axis_index("head") * share, share, 1)
        theirs = lax.all_gather(flip(send, gather_bit), "head", axis=1, tiled=True)
        return jnp.concatenate([mine, theirs], axis=0)

    queries = query_rows.reshape(tokens, heads, HEAD_DIM)
    key_heads = key_rows.reshape(tokens, heads, HEAD_DIM)
    value_heads = value_rows.reshape(tokens, heads, HEAD_DIM)
    gain = norm_gain.reshape(heads, HEAD_DIM)
    lower = lower_mask(tokens)[None]
    block_state = jnp.einsum("thd,the->hde", key_heads, value_heads, preferred_element_type=F32)
    state_low = entering(block_state, False).astype(BF16)
    scores = jnp.einsum("thd,shd->hts", queries, key_heads, preferred_element_type=F32)
    scores = jnp.where(lower, scores, 0.0).astype(BF16)
    attention = jnp.einsum("hts,she->the", scores, value_heads, preferred_element_type=F32)
    attention = attention + jnp.einsum("thd,hde->the", queries, state_low, preferred_element_type=F32)
    rms_value = jnp.sqrt(jnp.mean(attention * attention, axis=-1, keepdims=True) + 1e-05)
    normed = attention / rms_value
    gated = (normed * gain).astype(BF16).reshape(tokens, width)
    gated_grad = jnp.einsum("tj,cj->tc", gathered_cot, out_weight, preferred_element_type=F32)
    scaled = gated_grad.reshape(tokens, heads, HEAD_DIM) * gain
    inner = jnp.mean(scaled * normed, axis=-1, keepdims=True)
    pre_grad = ((scaled - normed * inner) / rms_value).astype(BF16)
    grad_block = jnp.einsum("thd,the->hde", queries, pre_grad, preferred_element_type=F32)
    grad_low = entering(grad_block, True).astype(BF16)
    mixing = jnp.einsum("the,she->hts", pre_grad, value_heads, preferred_element_type=F32)
    mixing = jnp.where(lower, mixing, 0.0).astype(BF16)
    query_grad = jnp.einsum("hts,shd->thd", mixing, key_heads, preferred_element_type=F32)
    query_grad = query_grad + jnp.einsum("the,hde->thd", pre_grad, state_low, preferred_element_type=F32)
    query_grad = query_grad.astype(BF16).reshape(tokens, width)
    key_grad = jnp.einsum("hts,thd->shd", mixing, queries, preferred_element_type=F32)
    key_grad = key_grad + jnp.einsum("she,hde->shd", value_heads, grad_low, preferred_element_type=F32)
    value_grad = jnp.einsum("hts,the->she", scores, pre_grad, preferred_element_type=F32)
    value_grad = value_grad + jnp.einsum("shd,hde->she", key_heads, grad_low, preferred_element_type=F32)
    key_grad = key_grad.astype(BF16).reshape(tokens, width)
    value_grad = value_grad.astype(BF16).reshape(tokens, width)

    both_input, both_cot = both(gathered_input), both(gathered_cot)

    def reduced(features, grad, turned):
        grad = jnp.concatenate([grad, flip(grad, gather_bit)], axis=0)

        def term(start, count):
            part = features[:, start * owned : (start + count) * owned]
            return tdot(grad, part) if turned else tdot(part, grad)

        start, count = 0, chunks
        pending = None
        for bit in halving:
            count //= 2
            send = term(start, count)
            if pending is not None:
                send = send + cut(pending, 0, count, turned)
                pending = cut(pending, count, count, turned)
            new = flip(send.astype(BF16), bit).astype(F32)
            pending = new if pending is None else pending + new
            start += count
        return term(start, 1) + pending

    def cut(array, start, count, turned):
        return lax.slice_in_dim(array, start * owned, (start + count) * owned, axis=1 if turned else 0)

    half = width // 2

    def in_halves(features, grad, turned):
        parts = [reduced(features, grad[:, i * half : (i + 1) * half], turned) for i in range(2)]
        return jnp.concatenate(parts, axis=0 if turned else 1)

    output_gradient = in_halves(both_cot, gated, True)
    projected = [in_halves(both_input, grad, False) for grad in (query_grad, key_grad, value_grad)]
    return (jnp.stack(projected, axis=1), output_gradient)


def solution(mesh):
    placed = (
        P("seq", "head"),
        P("seq", "head"),
        P("seq", "head"),
        P("seq", "head"),
        P("head", None),
        P("head"),
        P("seq", "head"),
    )
    return jax.shard_map(
        body,
        mesh=mesh,
        in_specs=placed,
        out_specs=(P("seq", None, "head"), P("head", "seq")),
        check_vma=False,
    )
```

```python
import jax
import jax.numpy as jnp
from jax import lax
from jax.sharding import PartitionSpec as P

HEAD_DIM = 128
F32 = jnp.float32
BF16 = jnp.bfloat16


def flip(array, bit):
    size = lax.axis_size("seq")
    return lax.ppermute(array, "seq", [(i, i ^ (1 << bit)) for i in range(size)])


def entering(block, reverse):
    size, position = lax.axis_size("seq"), lax.axis_index("seq")
    bits = size.bit_length() - 1
    total, before = block, jnp.zeros_like(block)
    for bit in range(bits):
        step = 1 << bit
        if bit < bits - 1:
            new = flip(total.astype(BF16), bit).astype(F32)
            mine = (position >> bit) & 1
            before = before + jnp.where(mine == (0 if reverse else 1), new, 0.0)
            total = total + new
        else:
            pairs = [(i, i ^ step) for i in range(size) if bool(i & step) == reverse]
            before = before + lax.ppermute(total.astype(BF16), "seq", pairs).astype(F32)
    return before


def lower_mask(count):
    rows = lax.broadcasted_iota(jnp.int32, (count, count), 0)
    cols = lax.broadcasted_iota(jnp.int32, (count, count), 1)
    return rows >= cols


def tdot(a, b):
    return lax.dot_general(a, b, (((0,), (0,)), ((), ())), preferred_element_type=F32)


def body(layer_input, query_rows, key_rows, value_rows, out_weight, norm_gain, cotangent):
    size, position = lax.axis_size("seq"), lax.axis_index("seq")
    bits = size.bit_length() - 1
    gather_bit = 1 if bits > 1 else 0
    halving = [bit for bit in range(bits) if bit != gather_bit]
    tokens, width = query_rows.shape
    heads = width // HEAD_DIM
    model = out_weight.shape[1]
    owned = model // size

    gathered_cot = lax.all_gather(cotangent, "head", axis=1, tiled=True)
    layer_input, gathered_cot = lax.optimization_barrier((layer_input, gathered_cot))
    gathered_input = lax.all_gather(layer_input, "head", axis=1, tiled=True)

    chunks = 1 << len(halving)
    order = []
    for j in range(chunks):
        toggled = 0
        for i, bit in enumerate(halving):
            if not (j >> (len(halving) - 1 - i)) & 1:
                toggled |= 1 << bit
        order.append(position ^ toggled)

    def pick(array, toggled):
        return jnp.concatenate(
            [lax.dynamic_slice_in_dim(array, (at ^ toggled) * owned, owned, 1) for at in order], axis=1
        )

    def both(array):
        mine = pick(array, 0)
        share = chunks * owned // lax.axis_size("head")
        send = pick(array, 1 << gather_bit)
        send = lax.dynamic_slice_in_dim(send, lax.axis_index("head") * share, share, 1)
        theirs = lax.all_gather(flip(send, gather_bit), "head", axis=1, tiled=True)
        return mine, theirs

    queries = query_rows.reshape(tokens, heads, HEAD_DIM)
    key_heads = key_rows.reshape(tokens, heads, HEAD_DIM)
    value_heads = value_rows.reshape(tokens, heads, HEAD_DIM)
    gain = norm_gain.reshape(heads, HEAD_DIM)
    lower = lower_mask(tokens)[None]
    block_state = jnp.einsum("thd,the->hde", key_heads, value_heads, preferred_element_type=F32)
    state_low = entering(block_state, False).astype(BF16)
    scores = jnp.einsum("thd,shd->hts", queries, key_heads, preferred_element_type=F32)
    scores = jnp.where(lower, scores, 0.0).astype(BF16)
    attention = jnp.einsum("hts,she->the", scores, value_heads, preferred_element_type=F32)
    attention = attention + jnp.einsum("thd,hde->the", queries, state_low, preferred_element_type=F32)
    rms_value = jnp.sqrt(jnp.mean(attention * attention, axis=-1, keepdims=True) + 1e-05)
    normed = attention / rms_value
    gated = (normed * gain).astype(BF16).reshape(tokens, width)
    gated_grad = jnp.einsum("tj,cj->tc", gathered_cot, out_weight, preferred_element_type=F32)
    scaled = gated_grad.reshape(tokens, heads, HEAD_DIM) * gain
    inner = jnp.mean(scaled * normed, axis=-1, keepdims=True)
    pre_grad = ((scaled - normed * inner) / rms_value).astype(BF16)
    grad_block = jnp.einsum("thd,the->hde", queries, pre_grad, preferred_element_type=F32)
    grad_low = entering(grad_block, True).astype(BF16)
    mixing = jnp.einsum("the,she->hts", pre_grad, value_heads, preferred_element_type=F32)
    mixing = jnp.where(lower, mixing, 0.0).astype(BF16)
    query_grad = jnp.einsum("hts,shd->thd", mixing, key_heads, preferred_element_type=F32)
    query_grad = query_grad + jnp.einsum("the,hde->thd", pre_grad, state_low, preferred_element_type=F32)
    query_grad = query_grad.astype(BF16).reshape(tokens, width)
    key_grad = jnp.einsum("hts,thd->shd", mixing, queries, preferred_element_type=F32)
    key_grad = key_grad + jnp.einsum("she,hde->shd", value_heads, grad_low, preferred_element_type=F32)
    value_grad = jnp.einsum("hts,the->she", scores, pre_grad, preferred_element_type=F32)
    value_grad = value_grad + jnp.einsum("shd,hde->she", key_heads, grad_low, preferred_element_type=F32)
    key_grad = key_grad.astype(BF16).reshape(tokens, width)
    value_grad = value_grad.astype(BF16).reshape(tokens, width)

    both_input, both_cot = both(gathered_input), both(gathered_cot)

    def cut(array, start, count, turned):
        return lax.slice_in_dim(array, start * owned, (start + count) * owned, axis=1 if turned else 0)

    def term(piece, start, count):
        features, grad, other, turned = piece
        total = 0.0
        for part, rows in zip(features, (grad, other)):
            part = part[:, start * owned : (start + count) * owned]
            total = total + (tdot(rows, part) if turned else tdot(part, rows))
        return total

    half = width // 2
    pieces = []
    for features, grad, turned in (
        (both_cot, gated, True),
        (both_input, query_grad, False),
        (both_input, key_grad, False),
        (both_input, value_grad, False),
    ):
        for i in range(2):
            part = grad[:, i * half : (i + 1) * half]
            pieces.append((features, part, flip(part, gather_bit), turned))

    ready, over, results = [], [], []
    for i, piece in enumerate(pieces):
        turned = piece[3]
        start, count = 0, chunks
        pending = None
        for place, bit in enumerate(halving):
            count //= 2
            send = term(piece, start, count)
            if pending is not None:
                send = send + cut(pending, 0, count, turned)
                pending = cut(pending, count, count, turned)
            send = send.astype(BF16)
            if place == 0:
                if i >= 2:
                    send, ready[i - 2] = lax.optimization_barrier((send, ready[i - 2]))
                if i >= 3:
                    send, over[i - 3] = lax.optimization_barrier((send, over[i - 3]))
            if place == 1:
                ready.append(send)
            new = flip(send, bit)
            if place == 1:
                over.append(new)
            new = new.astype(F32)
            pending = new if pending is None else pending + new
            start += count
        results.append(term(piece, start, 1) + pending)

    output_gradient = jnp.concatenate(results[:2], axis=0)
    projected = [jnp.concatenate(results[2 * i + 2 : 2 * i + 4], axis=1) for i in range(3)]
    return (jnp.stack(projected, axis=1), output_gradient)


def solution(mesh):
    placed = (
        P("seq", "head"),
        P("seq", "head"),
        P("seq", "head"),
        P("seq", "head"),
        P("head", None),
        P("head"),
        P("seq", "head"),
    )
    return jax.shard_map(
        body,
        mesh=mesh,
        in_specs=placed,
        out_specs=(P("seq", None, "head"), P("head", "seq")),
        check_vma=False,
    )
```

```python
import jax
import jax.numpy as jnp
from jax import lax
from jax.experimental import pallas as pl
from jax.sharding import PartitionSpec as P

HEAD_DIM = 128
F32 = jnp.float32
BF16 = jnp.bfloat16


def flip(array, bit):
    size = lax.axis_size("seq")
    return lax.ppermute(array, "seq", [(i, i ^ (1 << bit)) for i in range(size)])


def entering(block, reverse):
    size, position = lax.axis_size("seq"), lax.axis_index("seq")
    bits = size.bit_length() - 1
    total, before = block, jnp.zeros_like(block)
    for bit in range(bits):
        step = 1 << bit
        if bit < bits - 1:
            new = flip(total.astype(BF16), bit).astype(F32)
            mine = (position >> bit) & 1
            before = before + jnp.where(mine == (0 if reverse else 1), new, 0.0)
            total = total + new
        else:
            pairs = [(i, i ^ step) for i in range(size) if bool(i & step) == reverse]
            before = before + lax.ppermute(total.astype(BF16), "seq", pairs).astype(F32)
    return before


def lower_mask(count):
    rows = lax.broadcasted_iota(jnp.int32, (count, count), 0)
    cols = lax.broadcasted_iota(jnp.int32, (count, count), 1)
    return rows >= cols


def tdot(a, b):
    return lax.dot_general(a, b, (((0,), (0,)), ((), ())), preferred_element_type=F32)


def put_kernel(*refs):
    kept, new, out = refs[-3:]
    out[...] = kept[...] + new[...].astype(F32)


def put(target, kept, new, shape, place):
    rows, cols = kept.shape
    tile = min(rows, 256)
    block = (None,) * (len(shape) - 2) + (tile, cols)

    def at(r):
        return (*place[:-2], place[-2] * (rows // tile) + r, place[-1])

    small = pl.BlockSpec((tile, cols), lambda r: (r, 0))
    old = [] if target is None else [target]
    return pl.pallas_call(
        put_kernel,
        grid=(rows // tile,),
        in_specs=[pl.BlockSpec(memory_space=pl.ANY)] * len(old) + [small, small],
        out_specs=pl.BlockSpec(block, at),
        out_shape=jax.ShapeDtypeStruct(shape, F32),
        input_output_aliases={0: 0} if old else {},
        cost_estimate=pl.CostEstimate(flops=rows * cols, bytes_accessed=rows * cols * 10, transcendentals=0),
    )(*old, kept, new)


def body(layer_input, query_rows, key_rows, value_rows, out_weight, norm_gain, cotangent):
    size, position = lax.axis_size("seq"), lax.axis_index("seq")
    bits = size.bit_length() - 1
    gather_bit = 1 if bits > 1 else 0
    halving = [bit for bit in range(bits) if bit != gather_bit]
    tokens, width = query_rows.shape
    heads = width // HEAD_DIM
    model = out_weight.shape[1]
    owned = model // size

    head_size, head_place = lax.axis_size("head"), lax.axis_index("head")
    gathered_cot = lax.all_gather(cotangent, "head", axis=1, tiled=True)

    chunks = 1 << len(halving)
    order = []
    for j in range(chunks):
        toggled = 0
        for i, bit in enumerate(halving):
            if not (j >> (len(halving) - 1 - i)) & 1:
                toggled |= 1 << bit
        order.append(position ^ toggled)

    def pick(array, toggled):
        return jnp.concatenate(
            [lax.dynamic_slice_in_dim(array, (at ^ toggled) * owned, owned, 1) for at in order], axis=1
        )

    def both(gathered):
        share = chunks * owned // head_size
        send = pick(gathered, 1 << gather_bit)
        send = lax.dynamic_slice_in_dim(send, head_place * share, share, 1)
        theirs = lax.all_gather(flip(send, gather_bit), "head", axis=1, tiled=True)
        return pick(gathered, 0), theirs

    paired = gather_bit == 1 and head_size == 4 and width == 2 * owned
    aligned = (head_place & 1) == ((position >> 1) & 1)

    def across(array, seq_toggle, head_toggle):
        pairs = [
            (s * head_size + h, (s ^ seq_toggle) * head_size + (h ^ head_toggle))
            for s in range(size)
            for h in range(head_size)
            if (h ^ (s >> 1)) & 1
        ]
        return lax.ppermute(array, ("seq", "head"), pairs)

    queries = query_rows.reshape(tokens, heads, HEAD_DIM)
    key_heads = key_rows.reshape(tokens, heads, HEAD_DIM)
    value_heads = value_rows.reshape(tokens, heads, HEAD_DIM)
    gain = norm_gain.reshape(heads, HEAD_DIM)
    lower = lower_mask(tokens)[None]
    block_state = jnp.einsum("thd,the->hde", key_heads, value_heads, preferred_element_type=F32)
    if paired:
        same_cot = across(cotangent, 2, 1)
        other_cot = across(same_cot, 0, 2)
        near_cot, far_cot = across(same_cot, 0, 1), across(other_cot, 0, 1)
    state_in = entering(block_state, False)
    if paired:
        layer_input, state_in = lax.optimization_barrier((layer_input, state_in))
        swapped = jnp.where(aligned, layer_input, across(layer_input, 2, 1))
        gathered_input = lax.all_gather(swapped, "head", axis=1, tiled=True)
        both_input = pick(gathered_input, 0), pick(gathered_input, 2)
        near_cot = jnp.where(aligned, near_cot, same_cot)
        far_cot = jnp.where(aligned, far_cot, other_cot)

        def chosen(at):
            near, far = (lax.dynamic_slice_in_dim(a, (at & 1) * owned, owned, 1) for a in (near_cot, far_cot))
            return jnp.where((at >> 2) == (head_place >> 1), near, far)

        both_cot = pick(gathered_cot, 0), jnp.concatenate([chosen(at) for at in order], axis=1)
    else:
        layer_input, gathered_cot = lax.optimization_barrier((layer_input, gathered_cot))
        both_input = both(lax.all_gather(layer_input, "head", axis=1, tiled=True))
        both_cot = both(gathered_cot)
    state_low = state_in.astype(BF16)
    scores = jnp.einsum("thd,shd->hts", queries, key_heads, preferred_element_type=F32)
    scores = jnp.where(lower, scores, 0.0).astype(BF16)
    attention = jnp.einsum("hts,she->the", scores, value_heads, preferred_element_type=F32)
    attention = attention + jnp.einsum("thd,hde->the", queries, state_low, preferred_element_type=F32)
    rms_value = jnp.sqrt(jnp.mean(attention * attention, axis=-1, keepdims=True) + 1e-05)
    normed = attention / rms_value
    gated = (normed * gain).astype(BF16).reshape(tokens, width)
    gated_grad = jnp.einsum("tj,cj->tc", gathered_cot, out_weight, preferred_element_type=F32)
    scaled = gated_grad.reshape(tokens, heads, HEAD_DIM) * gain
    inner = jnp.mean(scaled * normed, axis=-1, keepdims=True)
    pre_grad = ((scaled - normed * inner) / rms_value).astype(BF16)
    grad_block = jnp.einsum("thd,the->hde", queries, pre_grad, preferred_element_type=F32)
    grad_low = entering(grad_block, True).astype(BF16)
    mixing = jnp.einsum("the,she->hts", pre_grad, value_heads, preferred_element_type=F32)
    mixing = jnp.where(lower, mixing, 0.0).astype(BF16)
    query_grad = jnp.einsum("hts,shd->thd", mixing, key_heads, preferred_element_type=F32)
    query_grad = query_grad + jnp.einsum("the,hde->thd", pre_grad, state_low, preferred_element_type=F32)
    query_grad = query_grad.astype(BF16).reshape(tokens, width)
    key_grad = jnp.einsum("hts,thd->shd", mixing, queries, preferred_element_type=F32)
    key_grad = key_grad + jnp.einsum("she,hde->shd", value_heads, grad_low, preferred_element_type=F32)
    value_grad = jnp.einsum("hts,the->she", scores, pre_grad, preferred_element_type=F32)
    value_grad = value_grad + jnp.einsum("shd,hde->she", key_heads, grad_low, preferred_element_type=F32)
    key_grad = key_grad.astype(BF16).reshape(tokens, width)
    value_grad = value_grad.astype(BF16).reshape(tokens, width)

    def cut(array, start, count, turned):
        return lax.slice_in_dim(array, start * owned, (start + count) * owned, axis=1 if turned else 0)

    def term(piece, start, count):
        features, grad, other, turned = piece
        total = 0.0
        for part, rows in zip(features, (grad, other)):
            part = part[:, start * owned : (start + count) * owned]
            total = total + (tdot(rows, part) if turned else tdot(part, rows))
        return total

    half = width // 2
    pieces = []
    output_gradient = projected = None
    for features, grad, turned in (
        (both_cot, gated, True),
        (both_input, query_grad, False),
        (both_input, key_grad, False),
        (both_input, value_grad, False),
    ):
        for i in range(2):
            part = grad[:, i * half : (i + 1) * half]
            pieces.append((features, part, flip(part, gather_bit), turned))

    ready, over = [], []
    for i, piece in enumerate(pieces):
        turned = piece[3]
        start, count = 0, chunks
        pending = None
        for place, bit in enumerate(halving):
            count //= 2
            send = term(piece, start, count)
            if pending is not None:
                send = send + cut(pending, 0, count, turned)
                pending = cut(pending, count, count, turned)
            send = send.astype(BF16)
            if place == 0:
                if i >= 2:
                    send, ready[i - 2] = lax.optimization_barrier((send, ready[i - 2]))
                if i >= 3:
                    send, over[i - 3] = lax.optimization_barrier((send, over[i - 3]))
            if place == 1:
                ready.append(send)
            new = flip(send, bit)
            if place == 1:
                over.append(new)
            start += count
            if place < len(halving) - 1:
                pending = new.astype(F32) if pending is None else pending + new.astype(F32)
        kept = term(piece, start, 1) + pending
        if turned:
            output_gradient = put(output_gradient, kept, new, (width, owned), (i, 0))
        else:
            projected = put(projected, kept, new, (3, owned, width), (i // 2 - 1, 0, i % 2))
    return (projected.transpose(1, 0, 2), output_gradient)


def solution(mesh):
    placed = (
        P("seq", "head"),
        P("seq", "head"),
        P("seq", "head"),
        P("seq", "head"),
        P("head", None),
        P("head"),
        P("seq", "head"),
    )
    return jax.shard_map(
        body,
        mesh=mesh,
        in_specs=placed,
        out_specs=(P("seq", None, "head"), P("head", "seq")),
        check_vma=False,
    )
```

```python
import functools

import jax
import jax.numpy as jnp
from jax import lax
from jax.experimental import pallas as pl
from jax.experimental.pallas import tpu as pltpu
from jax.sharding import PartitionSpec as P

HEAD_DIM = 128
F32 = jnp.float32
BF16 = jnp.bfloat16
PARAMS = pltpu.CompilerParams(vmem_limit_bytes=48 * 1024 * 1024)


def cost(flops, moved):
    return pl.CostEstimate(flops=int(flops), bytes_accessed=int(moved), transcendentals=0)


def after(array, *others):
    return lax.optimization_barrier((array, *others))[0]


def flip(array, bit):
    size = lax.axis_size("seq")
    return lax.ppermute(array, "seq", [(i, i ^ (1 << bit)) for i in range(size)])


def entering(block, low, reverse):
    size, position = lax.axis_size("seq"), lax.axis_index("seq")
    bits = size.bit_length() - 1
    total, before, passed = block, jnp.zeros_like(block), None
    for bit in range(bits):
        step = 1 << bit
        if bit < bits - 1:
            new = flip(low, bit)
            passed = new if bit == 1 or passed is None else passed
            new = new.astype(F32)
            mine = (position >> bit) & 1
            before = before + jnp.where(mine == (0 if reverse else 1), new, 0.0)
            total = total + new
            low = total.astype(BF16)
        else:
            pairs = [(i, i ^ step) for i in range(size) if bool(i & step) == reverse]
            before = before + lax.ppermute(low, "seq", pairs).astype(F32)
    return before.astype(BF16), passed


def mm(a, b):
    return lax.dot_general(a, b, (((1,), (0,)), ((), ())), preferred_element_type=F32)


def mm_t(a, b):
    return lax.dot_general(a, b, (((1,), (1,)), ((), ())), preferred_element_type=F32)


def t_mm(a, b):
    return lax.dot_general(a, b, (((0,), (0,)), ((), ())), preferred_element_type=F32)


def causal(a, b):
    half = a.shape[0] // 2
    rows = lax.broadcasted_iota(jnp.int32, (half, half), 0)
    cols = lax.broadcasted_iota(jnp.int32, (half, half), 1)
    lower = rows >= cols
    a0, a1, b0, b1 = a[:half], a[half:], b[:half], b[half:]
    first = jnp.where(lower, mm_t(a0, b0), 0.0).astype(BF16)
    cross = mm_t(a1, b0).astype(BF16)
    second = jnp.where(lower, mm_t(a1, b1), 0.0).astype(BF16)
    return first, cross, second


def lower_mm(tri, b):
    half = b.shape[0] // 2
    first, cross, second = tri
    return jnp.concatenate([mm(first, b[:half]), mm(cross, b[:half]) + mm(second, b[half:])], axis=0)


def upper_mm(tri, b):
    half = b.shape[0] // 2
    first, cross, second = tri
    return jnp.concatenate([t_mm(first, b[:half]) + t_mm(cross, b[half:]), t_mm(second, b[half:])], axis=0)


def head_slices(ref):
    return [slice(i * HEAD_DIM, (i + 1) * HEAD_DIM) for i in range(ref.shape[1] // HEAD_DIM)]


def state_kernel(k, v, out, low):
    for i, cols in enumerate(head_slices(k)):
        out[i] = t_mm(k[:, cols], v[:, cols])
        low[i] = out[i].astype(BF16)


def local_kernel(q, k, v, out):
    for cols in head_slices(q):
        out[:, cols] = lower_mm(causal(q[:, cols], k[:, cols]), v[:, cols])


def gated_kernel(local, q, state, gain, attention, gated):
    for i, cols in enumerate(head_slices(q)):
        value = local[:, cols] + mm(q[:, cols], state[i])
        attention[:, cols] = value
        rms = jnp.sqrt(jnp.mean(value * value, axis=-1, keepdims=True) + 1e-05)
        gated[:, cols] = (value / rms * gain[:, cols]).astype(BF16)


def pre_kernel(cot, weight, attention, q, gain, pre, out, low):
    gated_grad = mm_t(cot[...], weight[...])
    for i, cols in enumerate(head_slices(q)):
        value = attention[:, cols]
        rms = jnp.sqrt(jnp.mean(value * value, axis=-1, keepdims=True) + 1e-05)
        normed = value / rms
        scaled = gated_grad[:, cols] * gain[:, cols]
        inner = jnp.mean(scaled * normed, axis=-1, keepdims=True)
        grad = ((scaled - normed * inner) / rms).astype(BF16)
        pre[:, cols] = grad
        out[i] = t_mm(q[:, cols], grad)
        low[i] = out[i].astype(BF16)


def query_kernel(pre, q, k, v, state, query_grad, key_local, value_local):
    for i, cols in enumerate(head_slices(q)):
        grad, qh, kh, vh = pre[:, cols], q[:, cols], k[:, cols], v[:, cols]
        mixing = causal(grad, vh)
        query_grad[:, cols] = (lower_mm(mixing, kh) + mm_t(grad, state[i])).astype(BF16)
        key_local[:, cols] = upper_mm(mixing, qh)
        value_local[:, cols] = upper_mm(causal(qh, kh), grad)


def key_value_kernel(key_local, value_local, k, v, state, key_grad, value_grad):
    for i, cols in enumerate(head_slices(k)):
        key_grad[:, cols] = (key_local[:, cols] + mm_t(v[:, cols], state[i])).astype(BF16)
        value_grad[:, cols] = (value_local[:, cols] + mm(k[:, cols], state[i])).astype(BF16)


def by_heads(kernel, args, outs, flops):
    tokens = next(a.shape[0] for kind, a in args if kind == "rows")
    width = next(a.shape[1] for kind, a in args if kind == "rows")
    pair = 2 * HEAD_DIM
    count = width // pair

    def spec(kind, array=None):
        if kind == "rows":
            return pl.BlockSpec((tokens, pair), lambda i: (0, i))
        if kind == "heads":
            return pl.BlockSpec((2, HEAD_DIM, HEAD_DIM), lambda i: (i, 0, 0))
        if kind == "gain":
            return pl.BlockSpec((1, pair), lambda i: (0, i))
        if kind == "weight":
            return pl.BlockSpec((pair, array.shape[1]), lambda i: (i, 0))
        return pl.BlockSpec(array.shape, lambda i: (0, 0))

    shapes = {"rows": (tokens, width), "heads": (2 * count, HEAD_DIM, HEAD_DIM)}
    return pl.pallas_call(
        kernel,
        grid=(count,),
        in_specs=[spec(kind, a) for kind, a in args],
        out_specs=[spec(kind) for kind, _ in outs],
        out_shape=[jax.ShapeDtypeStruct(shapes[kind], dtype) for kind, dtype in outs],
        compiler_params=PARAMS,
        cost_estimate=cost(flops, sum(a.size * a.dtype.itemsize for _, a in args)),
    )(*[a for _, a in args])


def term_kernel(turned, adds, index, mine, theirs, grad, other, *rest):
    out = rest[-1]
    if turned:
        total = t_mm(grad[...], mine[...]) + t_mm(other[...], theirs[...])
    else:
        total = t_mm(mine[...], grad[...]) + t_mm(theirs[...], other[...])
    for ref in rest[:adds]:
        total = total + ref[...].astype(F32)
    out[...] = total.astype(out.dtype)


def term(features, grads, block, cols, turned, owned, start, count, received, target=None):
    mine, theirs, index = features
    grad, other = grads
    tokens, chunks = grad.shape[0], index.shape[0] // 2

    def tile(offset):
        if turned:
            return pl.BlockSpec((cols, owned), lambda r, ix: (0, r + offset))
        return pl.BlockSpec((owned, cols), lambda r, ix: (r + offset, 0))

    rows = pl.BlockSpec((tokens, cols), lambda r, ix: (0, block))
    in_specs = [
        pl.BlockSpec((tokens, owned), lambda r, ix: (0, ix[start + r])),
        pl.BlockSpec((tokens, owned), lambda r, ix: (0, ix[chunks + start + r])),
        rows,
        rows,
    ]
    in_specs += [tile(start - begun) for _, begun in received]
    operands = [index, mine, theirs, grad, other, *[a for a, _ in received]]
    aliases = {}
    if target is None:
        out_spec, dtype = tile(0), BF16
        shape = (cols, count * owned) if turned else (count * owned, cols)
    else:
        old, shape, place = target
        dtype = F32
        out_spec = pl.BlockSpec((None,) * (len(shape) - 2) + ((cols, owned) if turned else (owned, cols)), lambda r, ix: place)
        if old is not None:
            aliases = {len(operands): 0}
            operands.append(old)
            in_specs.append(pl.BlockSpec(memory_space=pl.ANY))
    return pl.pallas_call(
        functools.partial(term_kernel, turned, len(received)),
        grid_spec=pltpu.PrefetchScalarGridSpec(
            num_scalar_prefetch=1, grid=(count,), in_specs=in_specs, out_specs=out_spec
        ),
        out_shape=jax.ShapeDtypeStruct(shape, dtype),
        input_output_aliases=aliases,
        compiler_params=PARAMS,
        cost_estimate=cost(4 * tokens * cols * count * owned, 6 * tokens * count * owned),
    )(*operands)


def body(layer_input, query_rows, key_rows, value_rows, out_weight, norm_gain, cotangent):
    size, position = lax.axis_size("seq"), lax.axis_index("seq")
    head_size, head_place = lax.axis_size("head"), lax.axis_index("head")
    bits = size.bit_length() - 1
    gather_bit = 1
    halving = [bit for bit in range(bits) if bit != gather_bit]
    tokens, width = query_rows.shape
    model = out_weight.shape[1]
    owned = model // size
    work = tokens * width

    chunks = 1 << len(halving)
    order = []
    for j in range(chunks):
        toggled = 0
        for i, bit in enumerate(halving):
            if not (j >> (len(halving) - 1 - i)) & 1:
                toggled |= 1 << bit
        order.append(position ^ toggled)
    there = jnp.stack(order).astype(jnp.int32)
    packed = jnp.arange(chunks, dtype=jnp.int32)

    paired = head_size == 4 and width == 2 * owned
    aligned = (head_place & 1) == ((position >> 1) & 1)

    def across(array, seq_toggle, head_toggle):
        pairs = [
            (s * head_size + h, (s ^ seq_toggle) * head_size + (h ^ head_toggle))
            for s in range(size)
            for h in range(head_size)
            if (h ^ (s >> 1)) & 1
        ]
        return lax.ppermute(array, ("seq", "head"), pairs)

    def both(gathered):
        share = chunks * owned // head_size
        send = jnp.concatenate(
            [lax.dynamic_slice_in_dim(gathered, (at ^ (1 << gather_bit)) * owned, owned, 1) for at in order], axis=1
        )
        send = lax.dynamic_slice_in_dim(send, head_place * share, share, 1)
        theirs = lax.all_gather(flip(send, gather_bit), "head", axis=1, tiled=True)
        return gathered, theirs, jnp.concatenate([there, packed])

    gathered_cot = lax.all_gather(cotangent, "head", axis=1, tiled=True)
    gain = norm_gain.reshape(1, width)
    q, k, v = ("rows", query_rows), ("rows", key_rows), ("rows", value_rows)

    block_state, block_low = by_heads(
        state_kernel, [k, v], [("heads", F32), ("heads", BF16)], 2 * work * HEAD_DIM
    )
    if paired:
        same_cot = across(cotangent, 2, 1)
        other_cot = across(same_cot, 0, 2)
        near_cot, far_cot = across(same_cot, 0, 1), across(other_cot, 0, 1)
    (local,) = by_heads(
        local_kernel, [q, k, ("rows", after(value_rows, block_low))], [("rows", F32)], 3 * work * tokens
    )
    state_low, passed = entering(block_state, block_low, False)
    if paired:
        swapped = jnp.where(aligned, layer_input, across(after(layer_input, passed), 2, 1))
        gathered_input = lax.all_gather(swapped, "head", axis=1, tiled=True)
        both_input = gathered_input, gathered_input, jnp.concatenate([there, there ^ 2])
        near_cot = jnp.where(aligned, near_cot, same_cot)
        far_cot = jnp.where(aligned, far_cot, other_cot)

        def chosen(at):
            near, far = (lax.dynamic_slice_in_dim(a, (at & 1) * owned, owned, 1) for a in (near_cot, far_cot))
            return jnp.where((at >> 2) == (head_place >> 1), near, far)

        partner_cot = jnp.concatenate([chosen(at) for at in order], axis=1)
        both_cot = gathered_cot, partner_cot, jnp.concatenate([there, packed])
    else:
        both_cot = both(gathered_cot)
        both_input = both(lax.all_gather(after(layer_input, gathered_cot), "head", axis=1, tiled=True))

    attention, gated = by_heads(
        gated_kernel,
        [("rows", local), q, ("heads", state_low), ("gain", gain)],
        [("rows", F32), ("rows", BF16)],
        2 * work * HEAD_DIM,
    )
    half = width // 2
    gated_parts = [gated[:, :half], gated[:, half:]]
    gated_parts = [(part, flip(part, gather_bit)) for part in gated_parts]
    pre, grad_block, grad_block_low = by_heads(
        pre_kernel,
        [("whole", gathered_cot), ("weight", out_weight), ("rows", attention), q, ("gain", gain)],
        [("rows", BF16), ("heads", F32), ("heads", BF16)],
        2 * work * (model + HEAD_DIM),
    )
    grad_low, passed = entering(grad_block, grad_block_low, True)
    query_grad, key_local, value_local = by_heads(
        query_kernel,
        [("rows", pre), q, k, v, ("heads", state_low)],
        [("rows", BF16), ("rows", F32), ("rows", F32)],
        8 * work * tokens,
    )
    key_grad, value_grad = by_heads(
        key_value_kernel,
        [("rows", key_local), ("rows", value_local), k, v, ("heads", grad_low)],
        [("rows", BF16), ("rows", BF16)],
        4 * work * HEAD_DIM,
    )

    grads = [(grad, flip(after(grad, passed), gather_bit)) for grad in (query_grad, key_grad, value_grad)]
    pieces = [(both_cot, part, 0, True, (i, 0)) for i, part in enumerate(gated_parts)]
    pieces += [(both_input, pair, i, False, (n, 0, i)) for n, pair in enumerate(grads) for i in range(2)]
    starts = [chunks - (chunks >> i) for i in range(len(halving) + 1)]
    shapes = {True: (width, owned), False: (len(grads), owned, width)}
    targets = {True: None, False: None}
    received = [[] for _ in pieces]
    last = [gated]

    def stage(i, n):
        features, (grad, other), block, turned, place = pieces[i]
        other = after(other, last[0])
        came = received[i]
        if came:
            came[-1] = (after(came[-1][0], last[0]), came[-1][1])
        final = n == len(halving)
        target = (targets[turned], shapes[turned], place) if final else None
        count = 1 if final else chunks >> (n + 1)
        out = term(features, (grad, other), block, half, turned, owned, starts[n], count, came, target)
        last[0] = out
        if final:
            targets[turned] = out
        else:
            came.append((flip(out, halving[n]), starts[n + 1]))

    stages = len(halving) + 1
    for n in range(2):
        stage(n, 0)
    for i in range(len(pieces) + 1):
        for n in range(1, stages - 1):
            if i < len(pieces):
                stage(i, n)
        if i >= 1:
            stage(i - 1, stages - 1)
        if i + 2 < len(pieces):
            stage(i + 2, 0)
    return (targets[False].transpose(1, 0, 2), targets[True])


def solution(mesh):
    placed = (
        P("seq", "head"),
        P("seq", "head"),
        P("seq", "head"),
        P("seq", "head"),
        P("head", None),
        P("head"),
        P("seq", "head"),
    )
    return jax.shard_map(
        body,
        mesh=mesh,
        in_specs=placed,
        out_specs=(P("seq", None, "head"), P("head", "seq")),
        check_vma=False,
    )
```

```python
import functools

import jax
import jax.numpy as jnp
from jax import lax
from jax.experimental import pallas as pl
from jax.experimental.pallas import tpu as pltpu
from jax.sharding import PartitionSpec as P

HEAD_DIM = 128
F32 = jnp.float32
BF16 = jnp.bfloat16
PARAMS = pltpu.CompilerParams(vmem_limit_bytes=48 * 1024 * 1024)


def cost(flops, moved):
    return pl.CostEstimate(flops=int(flops), bytes_accessed=int(moved), transcendentals=0)


def after(array, *others):
    return lax.optimization_barrier((array, *others))[0]


def flip(array, bit):
    size = lax.axis_size("seq")
    return lax.ppermute(array, "seq", [(i, i ^ (1 << bit)) for i in range(size)])


def entering(block, low, reverse, first=()):
    size, position = lax.axis_size("seq"), lax.axis_index("seq")
    bits = size.bit_length() - 1
    total, before, passed = block, jnp.zeros_like(block), None
    for bit in range(bits):
        step = 1 << bit
        if bit < bits - 1:
            new = flip(after(low, *first) if bit == 1 and first else low, bit)
            passed = new if bit == 1 or passed is None else passed
            new = new.astype(F32)
            mine = (position >> bit) & 1
            before = before + jnp.where(mine == (0 if reverse else 1), new, 0.0)
            total = total + new
            low = total.astype(BF16)
        else:
            pairs = [(i, i ^ step) for i in range(size) if bool(i & step) == reverse]
            new = lax.ppermute(low, "seq", pairs)
    return (before, new), passed, low


def mm(a, b):
    return lax.dot_general(a, b, (((1,), (0,)), ((), ())), preferred_element_type=F32)


def mm_t(a, b):
    return lax.dot_general(a, b, (((1,), (1,)), ((), ())), preferred_element_type=F32)


def t_mm(a, b):
    return lax.dot_general(a, b, (((0,), (0,)), ((), ())), preferred_element_type=F32)


def causal(a, b):
    half = a.shape[0] // 2
    rows = lax.broadcasted_iota(jnp.int32, (half, half), 0)
    cols = lax.broadcasted_iota(jnp.int32, (half, half), 1)
    lower = rows >= cols
    a0, a1, b0, b1 = a[:half], a[half:], b[:half], b[half:]
    first = jnp.where(lower, mm_t(a0, b0), 0.0).astype(BF16)
    cross = mm_t(a1, b0).astype(BF16)
    second = jnp.where(lower, mm_t(a1, b1), 0.0).astype(BF16)
    return first, cross, second


def lower_mm(tri, b):
    half = b.shape[0] // 2
    first, cross, second = tri
    return jnp.concatenate([mm(first, b[:half]), mm(cross, b[:half]) + mm(second, b[half:])], axis=0)


def upper_mm(tri, b):
    half = b.shape[0] // 2
    first, cross, second = tri
    return jnp.concatenate([t_mm(first, b[:half]) + t_mm(cross, b[half:]), t_mm(second, b[half:])], axis=0)


def head_slices(ref):
    return [slice(i * HEAD_DIM, (i + 1) * HEAD_DIM) for i in range(ref.shape[1] // HEAD_DIM)]


def state_kernel(k, v, out, low):
    for i, cols in enumerate(head_slices(k)):
        out[i] = t_mm(k[:, cols], v[:, cols])
        low[i] = out[i].astype(BF16)


def local_kernel(q, k, v, out):
    for cols in head_slices(q):
        out[:, cols] = lower_mm(causal(q[:, cols], k[:, cols]), v[:, cols])


def gated_kernel(local, q, state, gain, attention, gated):
    for i, cols in enumerate(head_slices(q)):
        value = local[:, cols] + mm(q[:, cols], state[i])
        attention[:, cols] = value
        rms = jnp.sqrt(jnp.mean(value * value, axis=-1, keepdims=True) + 1e-05)
        gated[:, cols] = (value / rms * gain[:, cols]).astype(BF16)


def pre_kernel(cot, weight, attention, q, gain, pre, out, low):
    gated_grad = mm_t(cot[...], weight[...])
    for i, cols in enumerate(head_slices(q)):
        value = attention[:, cols]
        rms = jnp.sqrt(jnp.mean(value * value, axis=-1, keepdims=True) + 1e-05)
        normed = value / rms
        scaled = gated_grad[:, cols] * gain[:, cols]
        inner = jnp.mean(scaled * normed, axis=-1, keepdims=True)
        grad = ((scaled - normed * inner) / rms).astype(BF16)
        pre[:, cols] = grad
        out[i] = t_mm(q[:, cols], grad)
        low[i] = out[i].astype(BF16)


def query_kernel(pre, q, k, v, state, query_grad, key_local, value_local):
    for i, cols in enumerate(head_slices(q)):
        grad, qh, kh, vh = pre[:, cols], q[:, cols], k[:, cols], v[:, cols]
        mixing = causal(grad, vh)
        query_grad[:, cols] = (lower_mm(mixing, kh) + mm_t(grad, state[i])).astype(BF16)
        key_local[:, cols] = upper_mm(mixing, qh)
        value_local[:, cols] = upper_mm(causal(qh, kh), grad)


def key_value_kernel(key_local, value_local, k, v, state, key_grad, value_grad):
    for i, cols in enumerate(head_slices(k)):
        key_grad[:, cols] = (key_local[:, cols] + mm_t(v[:, cols], state[i])).astype(BF16)
        value_grad[:, cols] = (value_local[:, cols] + mm(k[:, cols], state[i])).astype(BF16)


def by_heads(kernel, args, outs, flops):
    tokens = next(a.shape[0] for kind, a in args if kind == "rows")
    width = next(a.shape[1] for kind, a in args if kind == "rows")
    pair = 2 * HEAD_DIM
    count = width // pair

    def spec(kind, array=None):
        if kind == "rows":
            return pl.BlockSpec((tokens, pair), lambda i: (0, i))
        if kind == "heads":
            return pl.BlockSpec((2, HEAD_DIM, HEAD_DIM), lambda i: (i, 0, 0))
        if kind == "gain":
            return pl.BlockSpec((1, pair), lambda i: (0, i))
        if kind == "weight":
            return pl.BlockSpec((pair, array.shape[1]), lambda i: (i, 0))
        return pl.BlockSpec(array.shape, lambda i: (0, 0))

    shapes = {"rows": (tokens, width), "heads": (2 * count, HEAD_DIM, HEAD_DIM)}
    return pl.pallas_call(
        kernel,
        grid=(count,),
        in_specs=[spec(kind, a) for kind, a in args],
        out_specs=[spec(kind) for kind, _ in outs],
        out_shape=[jax.ShapeDtypeStruct(shapes[kind], dtype) for kind, dtype in outs],
        compiler_params=PARAMS,
        cost_estimate=cost(flops, sum(a.size * a.dtype.itemsize for _, a in args)),
    )(*[a for _, a in args])


def term_kernel(turned, adds, index, mine, theirs, grad, other, *rest):
    out = rest[-1]
    if turned:
        total = t_mm(grad[...], mine[...]) + t_mm(other[...], theirs[...])
    else:
        total = t_mm(mine[...], grad[...]) + t_mm(theirs[...], other[...])
    for ref in rest[:adds]:
        total = total + ref[...].astype(F32)
    out[...] = total.astype(out.dtype)


def term(features, grads, block, cols, turned, owned, start, count, received, target=None):
    mine, theirs, index = features
    grad, other = grads
    tokens, chunks = grad.shape[0], index.shape[0] // 2

    def tile(offset):
        if turned:
            return pl.BlockSpec((cols, owned), lambda r, ix: (0, r + offset))
        return pl.BlockSpec((owned, cols), lambda r, ix: (r + offset, 0))

    rows = pl.BlockSpec((tokens, cols), lambda r, ix: (0, block))
    in_specs = [
        pl.BlockSpec((tokens, owned), lambda r, ix: (0, ix[start + r])),
        pl.BlockSpec((tokens, owned), lambda r, ix: (0, ix[chunks + start + r])),
        rows,
        rows,
    ]
    in_specs += [tile(start - begun) for _, begun in received]
    operands = [index, mine, theirs, grad, other, *[a for a, _ in received]]
    aliases = {}
    if target is None:
        out_spec, dtype = tile(0), BF16
        shape = (cols, count * owned) if turned else (count * owned, cols)
    else:
        old, shape, place = target
        dtype = F32
        out_spec = pl.BlockSpec((None,) * (len(shape) - 2) + ((cols, owned) if turned else (owned, cols)), lambda r, ix: place)
        if old is not None:
            aliases = {len(operands): 0}
            operands.append(old)
            in_specs.append(pl.BlockSpec(memory_space=pl.ANY))
    return pl.pallas_call(
        functools.partial(term_kernel, turned, len(received)),
        grid_spec=pltpu.PrefetchScalarGridSpec(
            num_scalar_prefetch=1, grid=(count,), in_specs=in_specs, out_specs=out_spec
        ),
        out_shape=jax.ShapeDtypeStruct(shape, dtype),
        input_output_aliases=aliases,
        compiler_params=PARAMS,
        cost_estimate=cost(4 * tokens * cols * count * owned, 6 * tokens * count * owned),
    )(*operands)


def body(layer_input, query_rows, key_rows, value_rows, out_weight, norm_gain, cotangent):
    size, position = lax.axis_size("seq"), lax.axis_index("seq")
    head_size, head_place = lax.axis_size("head"), lax.axis_index("head")
    bits = size.bit_length() - 1
    gather_bit = 1
    halving = [bit for bit in range(bits) if bit != gather_bit]
    tokens, width = query_rows.shape
    model = out_weight.shape[1]
    owned = model // size
    work = tokens * width

    chunks = 1 << len(halving)
    order = []
    for j in range(chunks):
        toggled = 0
        for i, bit in enumerate(halving):
            if not (j >> (len(halving) - 1 - i)) & 1:
                toggled |= 1 << bit
        order.append(position ^ toggled)
    there = jnp.stack(order).astype(jnp.int32)
    packed = jnp.arange(chunks, dtype=jnp.int32)

    paired = head_size == 4 and width == 2 * owned
    aligned = (head_place & 1) == ((position >> 1) & 1)

    def across(array, seq_toggle, head_toggle):
        pairs = [
            (s * head_size + h, (s ^ seq_toggle) * head_size + (h ^ head_toggle))
            for s in range(size)
            for h in range(head_size)
            if (h ^ (s >> 1)) & 1
        ]
        return lax.ppermute(array, ("seq", "head"), pairs)

    def both(gathered):
        share = chunks * owned // head_size
        send = jnp.concatenate(
            [lax.dynamic_slice_in_dim(gathered, (at ^ (1 << gather_bit)) * owned, owned, 1) for at in order], axis=1
        )
        send = lax.dynamic_slice_in_dim(send, head_place * share, share, 1)
        theirs = lax.all_gather(flip(send, gather_bit), "head", axis=1, tiled=True)
        return gathered, theirs, jnp.concatenate([there, packed])

    gathered_cot = lax.all_gather(cotangent, "head", axis=1, tiled=True)
    gain = norm_gain.reshape(1, width)
    q, k, v = ("rows", query_rows), ("rows", key_rows), ("rows", value_rows)

    block_state, block_low = by_heads(
        state_kernel, [k, v], [("heads", F32), ("heads", BF16)], 2 * work * HEAD_DIM
    )
    if paired:
        same_cot = across(cotangent, 2, 1)
        other_cot = across(same_cot, 0, 2)
        near_cot = across(same_cot, 0, 1)
    state_parts, passed, last_low = entering(block_state, block_low, False, (same_cot,) if paired else ())
    (local,) = by_heads(
        local_kernel, [q, k, ("rows", after(value_rows, last_low))], [("rows", F32)], 3 * work * tokens
    )
    state_low = (state_parts[0] + after(state_parts[1], local).astype(F32)).astype(BF16)
    if paired:
        swapped = across(after(layer_input, passed), 2, 1)
        swapped = jnp.where(aligned, layer_input, after(swapped, state_low))
        gathered_input = lax.all_gather(swapped, "head", axis=1, tiled=True)
        both_input = gathered_input, gathered_input, jnp.concatenate([there, there ^ 2])
        other_cot = after(other_cot, state_low)
        far_cot = across(other_cot, 0, 1)
    attention, gated = by_heads(
        gated_kernel,
        [("rows", local), q, ("heads", state_low), ("gain", gain)],
        [("rows", F32), ("rows", BF16)],
        2 * work * HEAD_DIM,
    )
    if paired:
        near_cot, far_cot, same_cot, other_cot = lax.optimization_barrier(
            (near_cot, far_cot, same_cot, other_cot, gated)
        )[:4]
        near_cot = jnp.where(aligned, near_cot, same_cot)
        far_cot = jnp.where(aligned, far_cot, other_cot)

        def chosen(at):
            near, far = (lax.dynamic_slice_in_dim(a, (at & 1) * owned, owned, 1) for a in (near_cot, far_cot))
            return jnp.where((at >> 2) == (head_place >> 1), near, far)

        partner_cot = jnp.concatenate([chosen(at) for at in order], axis=1)
        both_cot = gathered_cot, partner_cot, jnp.concatenate([there, packed])
    else:
        both_cot = both(gathered_cot)
        both_input = both(lax.all_gather(after(layer_input, gathered_cot), "head", axis=1, tiled=True))

    half = width // 2
    quarter = half // 2
    pieces = []
    for begin, count in ((0, quarter), (quarter, quarter), (half, half)):
        part = gated[:, begin : begin + count]
        pieces.append((both_cot, (part, flip(part, gather_bit)), count, 0, True, (begin // count, 0)))
    starts = [chunks - (chunks >> i) for i in range(len(halving) + 1)]
    shapes = {True: (width, owned), False: (3, owned, width)}
    targets = {True: None, False: None}
    received = {}
    last = [gated]

    def add_pieces(n, grad, *others):
        pair = grad, flip(after(grad, *others), gather_bit)
        pieces.extend((both_input, pair, half, i, False, (n, 0, i)) for i in range(2))

    def stage(i, n):
        features, (grad, other), cols, block, turned, place = pieces[i]
        other = after(other, last[0])
        came = received.setdefault(i, [])
        if came:
            came[-1] = (after(came[-1][0], last[0]), came[-1][1])
        final = n == len(halving)
        target = (targets[turned], shapes[turned], place) if final else None
        count = 1 if final else chunks >> (n + 1)
        out = term(features, (grad, other), block, cols, turned, owned, starts[n], count, came, target)
        last[0] = out
        if final:
            targets[turned] = out
        else:
            came.append((flip(out, halving[n]), starts[n + 1]))

    stage(0, 0)
    pre, grad_block, grad_block_low = by_heads(
        pre_kernel,
        [("whole", gathered_cot), ("weight", out_weight), ("rows", after(attention, last[0])), q, ("gain", gain)],
        [("rows", BF16), ("heads", F32), ("heads", BF16)],
        2 * work * (model + HEAD_DIM),
    )
    grad_parts, passed, last_low = entering(grad_block, grad_block_low, True)
    last[0] = pre
    stage(1, 0)
    query_grad, key_local, value_local = by_heads(
        query_kernel,
        [("rows", after(pre, last[0])), q, k, v, ("heads", state_low)],
        [("rows", BF16), ("rows", F32), ("rows", F32)],
        8 * work * tokens,
    )
    add_pieces(0, query_grad, passed)
    last[0] = query_grad
    grad_low = (grad_parts[0] + grad_parts[1].astype(F32)).astype(BF16)
    key_grad, value_grad = by_heads(
        key_value_kernel,
        [("rows", key_local), ("rows", value_local), k, v, ("heads", grad_low)],
        [("rows", BF16), ("rows", BF16)],
        4 * work * HEAD_DIM,
    )
    add_pieces(1, key_grad)
    add_pieces(2, value_grad)

    stages = len(halving) + 1
    for i in range(len(pieces) + 2):
        for n in range(1, stages - 1):
            if i < len(pieces):
                stage(i, n)
        if i >= 2:
            stage(i - 2, stages - 1)
        if i + 2 < len(pieces):
            stage(i + 2, 0)
    return (targets[False].transpose(1, 0, 2), targets[True])


def solution(mesh):
    placed = (
        P("seq", "head"),
        P("seq", "head"),
        P("seq", "head"),
        P("seq", "head"),
        P("head", None),
        P("head"),
        P("seq", "head"),
    )
    return jax.shard_map(
        body,
        mesh=mesh,
        in_specs=placed,
        out_specs=(P("seq", None, "head"), P("head", "seq")),
        check_vma=False,
    )
```

```python
import functools

import jax
import jax.numpy as jnp
from jax import lax
from jax.experimental import pallas as pl
from jax.experimental.pallas import tpu as pltpu
from jax.sharding import PartitionSpec as P

HEAD_DIM = 128
F32 = jnp.float32
BF16 = jnp.bfloat16
PARAMS = pltpu.CompilerParams(vmem_limit_bytes=48 * 1024 * 1024)


def cost(flops, moved):
    return pl.CostEstimate(flops=int(flops), bytes_accessed=int(moved), transcendentals=0)


def after(array, *others):
    return lax.optimization_barrier((array, *others))[0]


def flip(array, bit):
    size = lax.axis_size("seq")
    return lax.ppermute(array, "seq", [(i, i ^ (1 << bit)) for i in range(size)])


def entering(block, low, reverse, waits=None):
    size, position = lax.axis_size("seq"), lax.axis_index("seq")
    bits = size.bit_length() - 1
    total, before = block, jnp.zeros_like(block)
    sent, came = [], []
    for bit in range(bits):
        step = 1 << bit
        if waits and bit in waits:
            low = after(low, *waits[bit])
        sent.append(low)
        if bit < bits - 1:
            came.append(flip(low, bit))
            new = came[-1].astype(F32)
            mine = (position >> bit) & 1
            before = before + jnp.where(mine == (0 if reverse else 1), new, 0.0)
            total = total + new
            low = total.astype(BF16)
        else:
            pairs = [(i, i ^ step) for i in range(size) if bool(i & step) == reverse]
            came.append(lax.ppermute(low, "seq", pairs))
    return (before, came[-1]), sent, came


def mm(a, b):
    return lax.dot_general(a, b, (((1,), (0,)), ((), ())), preferred_element_type=F32)


def mm_t(a, b):
    return lax.dot_general(a, b, (((1,), (1,)), ((), ())), preferred_element_type=F32)


def t_mm(a, b):
    return lax.dot_general(a, b, (((0,), (0,)), ((), ())), preferred_element_type=F32)


def causal(a, b):
    half = a.shape[0] // 2
    rows = lax.broadcasted_iota(jnp.int32, (half, half), 0)
    cols = lax.broadcasted_iota(jnp.int32, (half, half), 1)
    lower = rows >= cols
    a0, a1, b0, b1 = a[:half], a[half:], b[:half], b[half:]
    first = jnp.where(lower, mm_t(a0, b0), 0.0).astype(BF16)
    cross = mm_t(a1, b0).astype(BF16)
    second = jnp.where(lower, mm_t(a1, b1), 0.0).astype(BF16)
    return first, cross, second


def lower_mm(tri, b):
    half = b.shape[0] // 2
    first, cross, second = tri
    return jnp.concatenate([mm(first, b[:half]), mm(cross, b[:half]) + mm(second, b[half:])], axis=0)


def upper_mm(tri, b):
    half = b.shape[0] // 2
    first, cross, second = tri
    return jnp.concatenate([t_mm(first, b[:half]) + t_mm(cross, b[half:]), t_mm(second, b[half:])], axis=0)


def head_slices(ref):
    return [slice(i * HEAD_DIM, (i + 1) * HEAD_DIM) for i in range(ref.shape[1] // HEAD_DIM)]


def state_kernel(k, v, out, low):
    for i, cols in enumerate(head_slices(k)):
        out[i] = t_mm(k[:, cols], v[:, cols])
        low[i] = out[i].astype(BF16)


def local_kernel(q, k, v, out):
    for cols in head_slices(q):
        out[:, cols] = lower_mm(causal(q[:, cols], k[:, cols]), v[:, cols])


def gated_kernel(local, q, state, gain, attention, first, second):
    step, steps = pl.program_id(0), pl.num_programs(0)
    parts = []
    for i, cols in enumerate(head_slices(q)):
        value = local[:, cols] + mm(q[:, cols], state[i])
        attention[:, cols] = value
        rms = jnp.sqrt(jnp.mean(value * value, axis=-1, keepdims=True) + 1e-05)
        parts.append((value / rms * gain[:, cols]).astype(BF16))
    found = jnp.concatenate(parts, axis=1)

    @pl.when(step < steps // 2)
    def _():
        first[...] = found

    @pl.when(step >= steps // 2)
    def _():
        second[...] = found


def pre_kernel(blocks, index, *refs):
    cots, weights = refs[:blocks], refs[blocks : 2 * blocks]
    attention, q, gain, pre, out, low = refs[2 * blocks :]
    gated_grad = sum(mm_t(c[...], w[...]) for c, w in zip(cots, weights))
    for i, cols in enumerate(head_slices(q)):
        value = attention[:, cols]
        rms = jnp.sqrt(jnp.mean(value * value, axis=-1, keepdims=True) + 1e-05)
        normed = value / rms
        scaled = gated_grad[:, cols] * gain[:, cols]
        inner = jnp.mean(scaled * normed, axis=-1, keepdims=True)
        grad = ((scaled - normed * inner) / rms).astype(BF16)
        pre[:, cols] = grad
        out[i] = t_mm(q[:, cols], grad)
        low[i] = out[i].astype(BF16)


def pre_grad_of(cots, places, weight, attention, q, gain):
    tokens, width = q.shape
    pair = 2 * HEAD_DIM
    part = cots[0].shape[1]
    blocks = len(cots)
    rows = pl.BlockSpec((tokens, pair), lambda i, ix: (0, i))
    heads = pl.BlockSpec((2, HEAD_DIM, HEAD_DIM), lambda i, ix: (i, 0, 0))
    whole = pl.BlockSpec((tokens, part), lambda i, ix: (0, 0))
    shape = (width // HEAD_DIM, HEAD_DIM, HEAD_DIM)
    return pl.pallas_call(
        functools.partial(pre_kernel, blocks),
        grid_spec=pltpu.PrefetchScalarGridSpec(
            num_scalar_prefetch=1,
            grid=(width // pair,),
            in_specs=[whole] * blocks
            + [pl.BlockSpec((pair, part), lambda i, ix, j=j: (i, ix[j])) for j in range(blocks)]
            + [rows, rows, pl.BlockSpec((1, pair), lambda i, ix: (0, i))],
            out_specs=[rows, heads, heads],
        ),
        out_shape=[
            jax.ShapeDtypeStruct((tokens, width), BF16),
            jax.ShapeDtypeStruct(shape, F32),
            jax.ShapeDtypeStruct(shape, BF16),
        ],
        compiler_params=PARAMS,
        cost_estimate=cost(2 * tokens * width * part * blocks, 2 * (tokens + width) * part * blocks),
    )(places, *cots, *[weight] * blocks, attention, q, gain)


def query_kernel(pre, k, v, state, first, second):
    step, steps = pl.program_id(0), pl.num_programs(0)
    parts = []
    for i, cols in enumerate(head_slices(k)):
        grad = pre[:, cols]
        parts.append((lower_mm(causal(grad, v[:, cols]), k[:, cols]) + mm_t(grad, state[i])).astype(BF16))
    found = jnp.concatenate(parts, axis=1)

    @pl.when(step < steps // 2)
    def _():
        first[...] = found

    @pl.when(step >= steps // 2)
    def _():
        second[...] = found


def own_kernel(pre, q, k, v, key_local, value_local):
    for cols in head_slices(q):
        grad, qh = pre[:, cols], q[:, cols]
        key_local[:, cols] = upper_mm(causal(grad, v[:, cols]), qh)
        value_local[:, cols] = upper_mm(causal(qh, k[:, cols]), grad)


def key_value_kernel(key_local, value_local, k, v, state, key_grad, value_grad):
    for i, cols in enumerate(head_slices(k)):
        key_grad[:, cols] = (key_local[:, cols] + mm_t(v[:, cols], state[i])).astype(BF16)
        value_grad[:, cols] = (value_local[:, cols] + mm(k[:, cols], state[i])).astype(BF16)


def by_heads(kernel, args, outs, flops):
    tokens = next(a.shape[0] for kind, a in args if kind == "rows")
    width = next(a.shape[1] for kind, a in args if kind == "rows")
    pair = 2 * HEAD_DIM
    count = width // pair
    half = count // 2
    specs = {
        "rows": pl.BlockSpec((tokens, pair), lambda i: (0, i)),
        "first": pl.BlockSpec((tokens, pair), lambda i: (0, jnp.minimum(i, half - 1))),
        "second": pl.BlockSpec((tokens, pair), lambda i: (0, jnp.maximum(i - half, 0))),
        "heads": pl.BlockSpec((2, HEAD_DIM, HEAD_DIM), lambda i: (i, 0, 0)),
        "gain": pl.BlockSpec((1, pair), lambda i: (0, i)),
    }
    shapes = {
        "rows": (tokens, width),
        "first": (tokens, width // 2),
        "second": (tokens, width // 2),
        "heads": (2 * count, HEAD_DIM, HEAD_DIM),
    }
    return pl.pallas_call(
        kernel,
        grid=(count,),
        in_specs=[specs[kind] for kind, _ in args],
        out_specs=[specs[kind] for kind, _ in outs],
        out_shape=[jax.ShapeDtypeStruct(shapes[kind], dtype) for kind, dtype in outs],
        compiler_params=PARAMS,
        cost_estimate=cost(flops, sum(a.size * a.dtype.itemsize for _, a in args)),
    )(*[a for _, a in args])


def term_kernel(turned, adds, index, mine, theirs, grad, other, *rest):
    out = rest[-1]
    if turned:
        total = t_mm(grad[...], mine[...]) + t_mm(other[...], theirs[...])
    else:
        total = t_mm(mine[...], grad[...]) + t_mm(theirs[...], other[...])
    for ref in rest[:adds]:
        total = total + ref[...].astype(F32)
    out[...] = total.astype(out.dtype)


def term(features, grads, block, cols, turned, owned, start, count, received, target=None):
    mine, theirs, index = features
    grad, other = grads
    tokens, chunks = grad.shape[0], index.shape[0] // 2

    def tile(offset):
        if turned:
            return pl.BlockSpec((cols, owned), lambda r, ix: (0, r + offset))
        return pl.BlockSpec((owned, cols), lambda r, ix: (r + offset, 0))

    rows = pl.BlockSpec((tokens, cols), lambda r, ix: (0, block))
    in_specs = [
        pl.BlockSpec((tokens, owned), lambda r, ix: (0, ix[start + r])),
        pl.BlockSpec((tokens, owned), lambda r, ix: (0, ix[chunks + start + r])),
        rows,
        rows,
    ]
    in_specs += [tile(start - begun) for _, begun in received]
    operands = [index, mine, theirs, grad, other, *[a for a, _ in received]]
    aliases = {}
    if target is None:
        out_spec, dtype = tile(0), BF16
        shape = (cols, count * owned) if turned else (count * owned, cols)
    else:
        old, shape, place = target
        dtype = F32
        out_spec = pl.BlockSpec((None,) * (len(shape) - 2) + ((cols, owned) if turned else (owned, cols)), lambda r, ix: place)
        if old is not None:
            aliases = {len(operands): 0}
            operands.append(old)
            in_specs.append(pl.BlockSpec(memory_space=pl.ANY))
    return pl.pallas_call(
        functools.partial(term_kernel, turned, len(received)),
        grid_spec=pltpu.PrefetchScalarGridSpec(
            num_scalar_prefetch=1, grid=(count,), in_specs=in_specs, out_specs=out_spec
        ),
        out_shape=jax.ShapeDtypeStruct(shape, dtype),
        input_output_aliases=aliases,
        compiler_params=PARAMS,
        cost_estimate=cost(4 * tokens * cols * count * owned, 6 * tokens * count * owned),
    )(*operands)


def body(layer_input, query_rows, key_rows, value_rows, out_weight, norm_gain, cotangent):
    size, position = lax.axis_size("seq"), lax.axis_index("seq")
    head_size, head_place = lax.axis_size("head"), lax.axis_index("head")
    bits = size.bit_length() - 1
    gather_bit = 1
    halving = [bit for bit in range(bits) if bit != gather_bit]
    tokens, width = query_rows.shape
    model = out_weight.shape[1]
    owned = model // size
    work = tokens * width

    chunks = 1 << len(halving)
    order = []
    for j in range(chunks):
        toggled = 0
        for i, bit in enumerate(halving):
            if not (j >> (len(halving) - 1 - i)) & 1:
                toggled |= 1 << bit
        order.append(position ^ toggled)
    there = jnp.stack(order).astype(jnp.int32)
    packed = jnp.arange(chunks, dtype=jnp.int32)

    paired = head_size == 4 and width == 2 * owned
    aligned = (head_place & 1) == ((position >> 1) & 1)

    def across(array, seq_toggle, head_toggle):
        pairs = [
            (s * head_size + h, (s ^ seq_toggle) * head_size + (h ^ head_toggle))
            for s in range(size)
            for h in range(head_size)
            if (h ^ (s >> 1)) & 1
        ]
        return lax.ppermute(array, ("seq", "head"), pairs)

    def both(gathered):
        share = chunks * owned // head_size
        send = jnp.concatenate(
            [lax.dynamic_slice_in_dim(gathered, (at ^ (1 << gather_bit)) * owned, owned, 1) for at in order], axis=1
        )
        send = lax.dynamic_slice_in_dim(send, head_place * share, share, 1)
        theirs = lax.all_gather(flip(send, gather_bit), "head", axis=1, tiled=True)
        return gathered, theirs, jnp.concatenate([there, packed])

    gain = norm_gain.reshape(1, width)
    q, k, v = ("rows", query_rows), ("rows", key_rows), ("rows", value_rows)

    cots, toggles = [cotangent], [0]
    toggle = head_size // 2
    while toggle:
        pairs = [(h, h ^ toggle) for h in range(head_size)]
        cots += [lax.ppermute(block, "head", pairs) for block in cots]
        toggles += [t ^ toggle for t in toggles]
        toggle //= 2
    places = jnp.stack([head_place ^ t for t in toggles]).astype(jnp.int32)

    block_state, block_low = by_heads(
        state_kernel, [k, v], [("heads", F32), ("heads", BF16)], 2 * work * HEAD_DIM
    )
    waits = {1: [cots[1]]}
    if paired:
        swapped_input = after(across(layer_input, 2, 1), cots[1])
        swapped_input = jnp.where(aligned, layer_input, swapped_input)
    state_parts, sent, came = entering(block_state, block_low, False, waits)
    (local,) = by_heads(
        local_kernel, [q, k, ("rows", after(value_rows, sent[-1]))], [("rows", F32)], 3 * work * tokens
    )
    state_low = (state_parts[0] + after(state_parts[1], local).astype(F32)).astype(BF16)
    attention, *gated = by_heads(
        gated_kernel,
        [("rows", local), q, ("heads", state_low), ("gain", gain)],
        [("rows", F32), ("first", BF16), ("second", BF16)],
        2 * work * HEAD_DIM,
    )
    if paired:
        swapped_cot = across(after(cotangent, came[1]), 2, 1)
        swapped_cot = jnp.where(aligned, cotangent, after(swapped_cot, attention))
        index = jnp.concatenate([there, there ^ 2])
        both_input, both_cot = (
            (gathered, gathered, index)
            for gathered in (lax.all_gather(a, "head", axis=1, tiled=True) for a in (swapped_input, swapped_cot))
        )
    else:
        both_input, both_cot = (
            both(lax.all_gather(a, "head", axis=1, tiled=True)) for a in (layer_input, cotangent)
        )
    gated_first = gated[0], flip(gated[0], gather_bit)

    pre, grad_block, grad_block_low = pre_grad_of(cots, places, out_weight, attention, query_rows, gain)
    grad_parts, sent, came = entering(grad_block, grad_block_low, True)
    pre_then = after(pre, gated_first[1])
    query_grad = by_heads(
        query_kernel,
        [("rows", pre_then), k, v, ("heads", state_low)],
        [("first", BF16), ("second", BF16)],
        4 * work * tokens,
    )
    query_grad = [(part, flip(part, gather_bit)) for part in query_grad]
    key_local, value_local = by_heads(
        own_kernel,
        [("rows", after(pre, query_grad[0][0], sent[1])), q, k, v],
        [("rows", F32), ("rows", F32)],
        6 * work * tokens,
    )
    gated_second = after(gated[1], came[1])
    gated = [gated_first, (gated_second, flip(gated_second, gather_bit))]
    grad_low = (grad_parts[0] + grad_parts[1].astype(F32)).astype(BF16)
    key_grad, value_grad = by_heads(
        key_value_kernel,
        [("rows", key_local), ("rows", value_local), k, v, ("heads", grad_low)],
        [("rows", BF16), ("rows", BF16)],
        4 * work * HEAD_DIM,
    )
    key_grad, value_grad = ((grad, flip(grad, gather_bit)) for grad in (key_grad, value_grad))

    half = width // 2
    pieces = [(both_input, query_grad[i], 0, False, (0, 0, i)) for i in range(2)]
    pieces += [(both_cot, gated[i], 0, True, (i, 0)) for i in range(2)]
    pieces += [(both_input, key_grad, i, False, (1, 0, i)) for i in range(2)]
    pieces += [(both_input, value_grad, i, False, (2, 0, i)) for i in range(2)]
    starts = [chunks - (chunks >> i) for i in range(len(halving) + 1)]
    shapes = {True: (width, owned), False: (3, owned, width)}
    targets = {True: None, False: None}
    received = {}
    last = [key_local]

    def stage(i, n):
        features, (grad, other), block, turned, place = pieces[i]
        other = after(other, last[0])
        came = received.setdefault(i, [])
        if came:
            came[-1] = (after(came[-1][0], last[0]), came[-1][1])
        final = n == len(halving)
        target = (targets[turned], shapes[turned], place) if final else None
        count = 1 if final else chunks >> (n + 1)
        out = term(features, (grad, other), block, half, turned, owned, starts[n], count, came, target)
        last[0] = out
        if final:
            targets[turned] = out
        else:
            came.append((flip(out, halving[n]), starts[n + 1]))

    stages = len(halving) + 1
    last[0] = after(last[0], sent[-1])
    stage(0, 0)
    stage(1, 0)
    last[0] = after(last[0], key_grad[0])
    for i in range(len(pieces) + 1):
        for n in range(1, stages - 1):
            if i < len(pieces):
                stage(i, n)
        if i >= 1:
            stage(i - 1, stages - 1)
        if i + 2 < len(pieces):
            stage(i + 2, 0)
    return (targets[False].transpose(1, 0, 2), targets[True])


def solution(mesh):
    placed = (
        P("seq", "head"),
        P("seq", "head"),
        P("seq", "head"),
        P("seq", "head"),
        P("head", None),
        P("head"),
        P("seq", "head"),
    )
    return jax.shard_map(
        body,
        mesh=mesh,
        in_specs=placed,
        out_specs=(P("seq", None, "head"), P("head", "seq")),
        check_vma=False,
    )
```

```python
import functools

import jax
import jax.numpy as jnp
from jax import lax
from jax.experimental import pallas as pl
from jax.experimental.pallas import tpu as pltpu
from jax.sharding import PartitionSpec as P

HEAD_DIM = 128
F32 = jnp.float32
BF16 = jnp.bfloat16
PARAMS = pltpu.CompilerParams(vmem_limit_bytes=48 * 1024 * 1024)


COST = pl.CostEstimate(flops=10**10, bytes_accessed=1, transcendentals=0)


def after(array, *others):
    return lax.optimization_barrier((array, *others))[0]


def flip(array, bit):
    size = lax.axis_size("seq")
    return lax.ppermute(array, "seq", [(i, i ^ (1 << bit)) for i in range(size)])


def entering(block, low, reverse, waits=None):
    size, position = lax.axis_size("seq"), lax.axis_index("seq")
    bits = size.bit_length() - 1
    total, before = block, jnp.zeros_like(block)
    sent, came = [], []
    for bit in range(bits):
        step = 1 << bit
        if waits and bit in waits:
            low = after(low, *waits[bit](came))
        sent.append(low)
        if bit < bits - 1:
            came.append(flip(low, bit))
            new = came[-1].astype(F32)
            mine = (position >> bit) & 1
            before = before + jnp.where(mine == (0 if reverse else 1), new, 0.0)
            total = total + new
            low = total.astype(BF16)
        else:
            pairs = [(i, i ^ step) for i in range(size) if bool(i & step) == reverse]
            came.append(lax.ppermute(low, "seq", pairs))
    return (before, came[-1]), sent, came


def mm(a, b):
    return lax.dot_general(a, b, (((1,), (0,)), ((), ())), preferred_element_type=F32)


def mm_t(a, b):
    return lax.dot_general(a, b, (((1,), (1,)), ((), ())), preferred_element_type=F32)


def t_mm(a, b):
    return lax.dot_general(a, b, (((0,), (0,)), ((), ())), preferred_element_type=F32)


def causal(a, b):
    half = a.shape[0] // 2
    rows = lax.broadcasted_iota(jnp.int32, (half, half), 0)
    cols = lax.broadcasted_iota(jnp.int32, (half, half), 1)
    lower = rows >= cols
    a0, a1, b0, b1 = a[:half], a[half:], b[:half], b[half:]
    first = jnp.where(lower, mm_t(a0, b0), 0.0).astype(BF16)
    cross = mm_t(a1, b0).astype(BF16)
    second = jnp.where(lower, mm_t(a1, b1), 0.0).astype(BF16)
    return first, cross, second


def lower_mm(tri, b):
    half = b.shape[0] // 2
    first, cross, second = tri
    return jnp.concatenate([mm(first, b[:half]), mm(cross, b[:half]) + mm(second, b[half:])], axis=0)


def upper_mm(tri, b):
    half = b.shape[0] // 2
    first, cross, second = tri
    return jnp.concatenate([t_mm(first, b[:half]) + t_mm(cross, b[half:]), t_mm(second, b[half:])], axis=0)


def head_slices(ref):
    return [slice(i * HEAD_DIM, (i + 1) * HEAD_DIM) for i in range(ref.shape[1] // HEAD_DIM)]


def state_kernel(k, v, out, low):
    for i, cols in enumerate(head_slices(k)):
        out[i] = t_mm(k[:, cols], v[:, cols])
        low[i] = out[i].astype(BF16)


def local_kernel(q, k, v, out):
    for cols in head_slices(q):
        out[:, cols] = lower_mm(causal(q[:, cols], k[:, cols]), v[:, cols])


def gated_kernel(local, q, state, gain, attention, first, second):
    step, steps = pl.program_id(0), pl.num_programs(0)
    parts = []
    for i, cols in enumerate(head_slices(q)):
        value = local[:, cols] + mm(q[:, cols], state[i])
        attention[:, cols] = value
        rms = jnp.sqrt(jnp.mean(value * value, axis=-1, keepdims=True) + 1e-05)
        parts.append((value / rms * gain[:, cols]).astype(BF16))
    found = jnp.concatenate(parts, axis=1)

    @pl.when(step < steps // 2)
    def _():
        first[...] = found

    @pl.when(step >= steps // 2)
    def _():
        second[...] = found


def pre_kernel(cot, weight, attention, q, gain, pre, out, low):
    gated_grad = mm_t(cot[...], weight[...])
    for i, cols in enumerate(head_slices(q)):
        value = attention[:, cols]
        rms = jnp.sqrt(jnp.mean(value * value, axis=-1, keepdims=True) + 1e-05)
        normed = value / rms
        scaled = gated_grad[:, cols] * gain[:, cols]
        inner = jnp.mean(scaled * normed, axis=-1, keepdims=True)
        grad = ((scaled - normed * inner) / rms).astype(BF16)
        pre[:, cols] = grad
        out[i] = t_mm(q[:, cols], grad)
        low[i] = out[i].astype(BF16)


def query_kernel(pre, k, v, state, first, second):
    step, steps = pl.program_id(0), pl.num_programs(0)
    parts = []
    for i, cols in enumerate(head_slices(k)):
        grad = pre[:, cols]
        parts.append((lower_mm(causal(grad, v[:, cols]), k[:, cols]) + mm_t(grad, state[i])).astype(BF16))
    found = jnp.concatenate(parts, axis=1)

    @pl.when(step < steps // 2)
    def _():
        first[...] = found

    @pl.when(step >= steps // 2)
    def _():
        second[...] = found


def own_kernel(pre, q, k, v, key_local, value_local):
    for cols in head_slices(q):
        grad, qh = pre[:, cols], q[:, cols]
        key_local[:, cols] = upper_mm(causal(grad, v[:, cols]), qh)
        value_local[:, cols] = upper_mm(causal(qh, k[:, cols]), grad)


def key_value_kernel(key_local, value_local, k, v, state, key_grad, value_grad):
    for i, cols in enumerate(head_slices(k)):
        key_grad[:, cols] = (key_local[:, cols] + mm_t(v[:, cols], state[i])).astype(BF16)
        value_grad[:, cols] = (value_local[:, cols] + mm(k[:, cols], state[i])).astype(BF16)


def without(kernel, first, count):
    return lambda *refs: kernel(*refs[:first], *refs[first + count :])


def by_heads(kernel, args, outs, waits=()):
    tokens = next(a.shape[0] for kind, a in args if kind == "rows")
    width = next(a.shape[1] for kind, a in args if kind == "rows")
    pair = 2 * HEAD_DIM
    count = width // pair
    half = count // 2
    specs = {
        "rows": pl.BlockSpec((tokens, pair), lambda i: (0, i)),
        "first": pl.BlockSpec((tokens, pair), lambda i: (0, jnp.minimum(i, half - 1))),
        "second": pl.BlockSpec((tokens, pair), lambda i: (0, jnp.maximum(i - half, 0))),
        "heads": pl.BlockSpec((2, HEAD_DIM, HEAD_DIM), lambda i: (i, 0, 0)),
        "gain": pl.BlockSpec((1, pair), lambda i: (0, i)),
    }
    for kind, a in args:
        if kind == "whole":
            specs[kind] = pl.BlockSpec(a.shape, lambda i: (0, 0))
        if kind == "weight":
            specs[kind] = pl.BlockSpec((pair, a.shape[1]), lambda i: (i, 0))
    shapes = {
        "rows": (tokens, width),
        "first": (tokens, width // 2),
        "second": (tokens, width // 2),
        "heads": (2 * count, HEAD_DIM, HEAD_DIM),
    }
    return pl.pallas_call(
        without(kernel, len(args), len(waits)),
        grid=(count,),
        in_specs=[specs[kind] for kind, _ in args] + [pl.BlockSpec(memory_space=pl.ANY)] * len(waits),
        out_specs=[specs[kind] for kind, _ in outs],
        out_shape=[jax.ShapeDtypeStruct(shapes[kind], dtype) for kind, dtype in outs],
        compiler_params=PARAMS,
        cost_estimate=COST,
    )(*[a for _, a in args], *waits)


def term_kernel(turned, adds, index, mine, theirs, grad, other, *rest):
    out = rest[-1]
    if turned:
        total = t_mm(grad[...], mine[...]) + t_mm(other[...], theirs[...])
    else:
        total = t_mm(mine[...], grad[...]) + t_mm(theirs[...], other[...])
    for ref in rest[:adds]:
        total = total + ref[...].astype(F32)
    out[...] = total.astype(out.dtype)


def term(features, grads, block, cols, turned, owned, start, count, received, waits, target=None):
    mine, theirs, index = features
    grad, other = grads
    tokens, chunks = grad.shape[0], index.shape[0] // 2

    def tile(offset):
        if turned:
            return pl.BlockSpec((cols, owned), lambda r, ix: (0, r + offset))
        return pl.BlockSpec((owned, cols), lambda r, ix: (r + offset, 0))

    rows = pl.BlockSpec((tokens, cols), lambda r, ix: (0, block))
    in_specs = [
        pl.BlockSpec((tokens, owned), lambda r, ix: (0, ix[start + r])),
        pl.BlockSpec((tokens, owned), lambda r, ix: (0, ix[chunks + start + r])),
        rows,
        rows,
    ]
    in_specs += [tile(start - begun) for _, begun in received]
    in_specs += [pl.BlockSpec(memory_space=pl.ANY)] * len(waits)
    operands = [index, mine, theirs, grad, other, *[a for a, _ in received], *waits]
    aliases = {}
    if target is None:
        out_spec, dtype = tile(0), BF16
        shape = (cols, count * owned) if turned else (count * owned, cols)
    else:
        old, shape, place = target
        dtype = F32
        out_spec = pl.BlockSpec((None,) * (len(shape) - 2) + ((cols, owned) if turned else (owned, cols)), lambda r, ix: place)
        if old is not None:
            aliases = {len(operands): 0}
            operands.append(old)
            in_specs.append(pl.BlockSpec(memory_space=pl.ANY))
    return pl.pallas_call(
        functools.partial(term_kernel, turned, len(received)),
        grid_spec=pltpu.PrefetchScalarGridSpec(
            num_scalar_prefetch=1, grid=(count,), in_specs=in_specs, out_specs=out_spec
        ),
        out_shape=jax.ShapeDtypeStruct(shape, dtype),
        input_output_aliases=aliases,
        compiler_params=PARAMS,
        cost_estimate=COST,
    )(*operands)


def body(layer_input, query_rows, key_rows, value_rows, out_weight, norm_gain, cotangent):
    size, position = lax.axis_size("seq"), lax.axis_index("seq")
    head_size, head_place = lax.axis_size("head"), lax.axis_index("head")
    bits = size.bit_length() - 1
    gather_bit = 1
    halving = [bit for bit in range(bits) if bit != gather_bit]
    tokens, width = query_rows.shape
    model = out_weight.shape[1]
    owned = model // size

    chunks = 1 << len(halving)
    order = []
    for j in range(chunks):
        toggled = 0
        for i, bit in enumerate(halving):
            if not (j >> (len(halving) - 1 - i)) & 1:
                toggled |= 1 << bit
        order.append(position ^ toggled)
    there = jnp.stack(order).astype(jnp.int32)
    packed = jnp.arange(chunks, dtype=jnp.int32)

    paired = head_size == 4 and width == 2 * owned
    aligned = (head_place & 1) == ((position >> 1) & 1)

    def across(array, seq_toggle, head_toggle):
        pairs = [
            (s * head_size + h, (s ^ seq_toggle) * head_size + (h ^ head_toggle))
            for s in range(size)
            for h in range(head_size)
            if (h ^ (s >> 1)) & 1
        ]
        return lax.ppermute(array, ("seq", "head"), pairs)

    def both(gathered):
        share = chunks * owned // head_size
        send = jnp.concatenate(
            [lax.dynamic_slice_in_dim(gathered, (at ^ (1 << gather_bit)) * owned, owned, 1) for at in order], axis=1
        )
        send = lax.dynamic_slice_in_dim(send, head_place * share, share, 1)
        theirs = lax.all_gather(flip(send, gather_bit), "head", axis=1, tiled=True)
        return gathered, theirs, jnp.concatenate([there, packed])

    gain = norm_gain.reshape(1, width)
    q, k, v = ("rows", query_rows), ("rows", key_rows), ("rows", value_rows)

    gathered_cot = lax.all_gather(cotangent, "head", axis=1, tiled=True)

    block_state, block_low = by_heads(state_kernel, [k, v], [("heads", F32), ("heads", BF16)])
    partner = []

    def partner_shard(came):
        shard = after(across(cotangent, 2, 1), came[0])
        partner.append(jnp.where(aligned, across(shard[:, owned:], 0, 1), shard[:, :owned]))
        return partner

    waits = {2: partner_shard} if paired else {}
    state_parts, sent, came = entering(block_state, block_low, False, waits)
    (local,) = by_heads(local_kernel, [q, k, v], [("rows", F32)], [sent[-1]])
    state_low = (state_parts[0] + after(state_parts[1], local).astype(F32)).astype(BF16)
    attention, *gated = by_heads(
        gated_kernel,
        [("rows", local), q, ("heads", state_low), ("gain", gain)],
        [("rows", F32), ("first", BF16), ("second", BF16)],
    )
    if paired:
        partner_cot = lax.all_gather(partner[0], "head", axis=1, tiled=True)
        side = 1 ^ ((position >> 1) & 1) ^ (there & 1)
        both_cot = gathered_cot, partner_cot, jnp.concatenate([there, (there >> 2) * 2 + side])
        swapped = across(after(layer_input, came[1]), 2, 1)
        swapped = jnp.where(aligned, layer_input, after(swapped, attention))
        gathered_input = lax.all_gather(swapped, "head", axis=1, tiled=True)
        both_input = gathered_input, gathered_input, jnp.concatenate([there, there ^ 2])
    else:
        both_cot = both(gathered_cot)
        both_input = both(lax.all_gather(layer_input, "head", axis=1, tiled=True))
    gated_first = gated[0], flip(gated[0], gather_bit)

    pre, grad_block, grad_block_low = by_heads(
        pre_kernel,
        [("whole", gathered_cot), ("weight", out_weight), ("rows", attention), q, ("gain", gain)],
        [("rows", BF16), ("heads", F32), ("heads", BF16)],
    )
    grad_parts, sent, came = entering(grad_block, grad_block_low, True)
    query_grad = by_heads(
        query_kernel,
        [("rows", pre), k, v, ("heads", state_low)],
        [("first", BF16), ("second", BF16)],
        [gated_first[1]],
    )
    query_grad = [(part, flip(part, gather_bit)) for part in query_grad]
    key_local, value_local = by_heads(
        own_kernel,
        [("rows", pre), q, k, v],
        [("rows", F32), ("rows", F32)],
        [query_grad[0][0], sent[1]],
    )
    gated_second = after(gated[1], came[1])
    gated = [gated_first, (gated_second, flip(gated_second, gather_bit))]
    grad_low = (grad_parts[0] + grad_parts[1].astype(F32)).astype(BF16)
    key_grad, value_grad = by_heads(
        key_value_kernel,
        [("rows", key_local), ("rows", value_local), k, v, ("heads", grad_low)],
        [("rows", BF16), ("rows", BF16)],
    )
    key_grad = key_grad, flip(key_grad, gather_bit)
    value_grad = value_grad, flip(after(value_grad, key_grad[1]), gather_bit)

    half = width // 2
    pieces = [(both_cot, gated[i], 0, True, (i, 0)) for i in range(2)]
    pieces += [(both_input, query_grad[i], 0, False, (0, 0, i)) for i in range(2)]
    pieces += [(both_input, key_grad, i, False, (1, 0, i)) for i in range(2)]
    pieces += [(both_input, value_grad, i, False, (2, 0, i)) for i in range(2)]
    starts = [chunks - (chunks >> i) for i in range(len(halving) + 1)]
    shapes = {True: (width, owned), False: (3, owned, width)}
    targets = {True: None, False: None}
    received = {}
    last = [key_local, sent[-1]]

    def stage(i, n):
        features, (grad, other), block, turned, place = pieces[i]
        came = received.setdefault(i, [])
        final = n == len(halving)
        target = (targets[turned], shapes[turned], place) if final else None
        count = 1 if final else chunks >> (n + 1)
        out = term(features, (grad, other), block, half, turned, owned, starts[n], count, came, last, target)
        last[:] = [out]
        if final:
            targets[turned] = out
        else:
            came.append((flip(out, halving[n]), starts[n + 1]))

    stages = len(halving) + 1
    stage(0, 0)
    stage(1, 0)
    last.append(key_grad[0])
    for i in range(len(pieces)):
        for n in range(1, stages - 1):
            stage(i, n)
        if i + 2 < len(pieces):
            last.extend(([], key_grad[1:], value_grad[1:])[min(i, 2)])
            stage(i + 2, 0)
        if i >= 1:
            stage(i - 1, stages - 1)
    stage(len(pieces) - 1, stages - 1)
    return (targets[False].transpose(1, 0, 2), targets[True])


def solution(mesh):
    placed = (
        P("seq", "head"),
        P("seq", "head"),
        P("seq", "head"),
        P("seq", "head"),
        P("head", None),
        P("head"),
        P("seq", "head"),
    )
    return jax.shard_map(
        body,
        mesh=mesh,
        in_specs=placed,
        out_specs=(P("seq", None, "head"), P("head", "seq")),
        check_vma=False,
    )
```

```python
import functools

import jax
import jax.numpy as jnp
from jax import lax
from jax.experimental import pallas as pl
from jax.experimental.pallas import tpu as pltpu
from jax.sharding import PartitionSpec as P

HEAD_DIM = 128
F32 = jnp.float32
BF16 = jnp.bfloat16
PARAMS = pltpu.CompilerParams(vmem_limit_bytes=60 * 1024 * 1024)


COST = pl.CostEstimate(flops=10**10, bytes_accessed=1, transcendentals=0)


def after(array, *others):
    return lax.optimization_barrier((array, *others))[0]


def flip(array, bit):
    size = lax.axis_size("seq")
    return lax.ppermute(array, "seq", [(i, i ^ (1 << bit)) for i in range(size)])


def entering(block, low, reverse):
    size, position = lax.axis_size("seq"), lax.axis_index("seq")
    bits = size.bit_length() - 1
    total, before = block, jnp.zeros_like(block)
    sent, came = [], []
    for bit in range(bits):
        step = 1 << bit
        sent.append(low)
        if bit < bits - 1:
            came.append(flip(low, bit))
            new = came[-1].astype(F32)
            mine = (position >> bit) & 1
            before = before + jnp.where(mine == (0 if reverse else 1), new, 0.0)
            total = total + new
            low = total.astype(BF16)
        else:
            pairs = [(i, i ^ step) for i in range(size) if bool(i & step) == reverse]
            came.append(lax.ppermute(low, "seq", pairs))
    return (before, came[-1]), sent, came


def mm(a, b):
    return lax.dot_general(a, b, (((1,), (0,)), ((), ())), preferred_element_type=F32)


def mm_t(a, b):
    return lax.dot_general(a, b, (((1,), (1,)), ((), ())), preferred_element_type=F32)


def t_mm(a, b):
    return lax.dot_general(a, b, (((0,), (0,)), ((), ())), preferred_element_type=F32)


def causal(a, b):
    half = a.shape[0] // 2
    rows = lax.broadcasted_iota(jnp.int32, (half, half), 0)
    cols = lax.broadcasted_iota(jnp.int32, (half, half), 1)
    lower = rows >= cols
    a0, a1, b0, b1 = a[:half], a[half:], b[:half], b[half:]
    first = jnp.where(lower, mm_t(a0, b0), 0.0).astype(BF16)
    cross = mm_t(a1, b0).astype(BF16)
    second = jnp.where(lower, mm_t(a1, b1), 0.0).astype(BF16)
    return first, cross, second


def lower_mm(tri, b):
    half = b.shape[0] // 2
    first, cross, second = tri
    return jnp.concatenate([mm(first, b[:half]), mm(cross, b[:half]) + mm(second, b[half:])], axis=0)


def upper_mm(tri, b):
    half = b.shape[0] // 2
    first, cross, second = tri
    return jnp.concatenate([t_mm(first, b[:half]) + t_mm(cross, b[half:]), t_mm(second, b[half:])], axis=0)


def head_slices(ref):
    return [slice(i * HEAD_DIM, (i + 1) * HEAD_DIM) for i in range(ref.shape[1] // HEAD_DIM)]


def state_kernel(k, v, out, low):
    for i, cols in enumerate(head_slices(k)):
        out[i] = t_mm(k[:, cols], v[:, cols])
        low[i] = out[i].astype(BF16)


def local_kernel(q, k, v, out):
    for cols in head_slices(q):
        out[:, cols] = lower_mm(causal(q[:, cols], k[:, cols]), v[:, cols])


def gated_kernel(local, q, state, gain, attention, first, second):
    step, steps = pl.program_id(0), pl.num_programs(0)
    parts = []
    for i, cols in enumerate(head_slices(q)):
        value = local[:, cols] + mm(q[:, cols], state[i])
        attention[:, cols] = value
        rms = jnp.sqrt(jnp.mean(value * value, axis=-1, keepdims=True) + 1e-05)
        parts.append((value / rms * gain[:, cols]).astype(BF16))
    found = jnp.concatenate(parts, axis=1)

    @pl.when(step < steps // 2)
    def _():
        first[...] = found

    @pl.when(step >= steps // 2)
    def _():
        second[...] = found


def pre_kernel(cot, weight, attention, q, gain, pre, out, low):
    gated_grad = mm_t(cot[...], weight[...])
    for i, cols in enumerate(head_slices(q)):
        value = attention[:, cols]
        rms = jnp.sqrt(jnp.mean(value * value, axis=-1, keepdims=True) + 1e-05)
        normed = value / rms
        scaled = gated_grad[:, cols] * gain[:, cols]
        inner = jnp.mean(scaled * normed, axis=-1, keepdims=True)
        grad = ((scaled - normed * inner) / rms).astype(BF16)
        pre[:, cols] = grad
        out[i] = t_mm(q[:, cols], grad)
        low[i] = out[i].astype(BF16)


def query_kernel(pre, k, v, state, first, second):
    step, steps = pl.program_id(0), pl.num_programs(0)
    parts = []
    for i, cols in enumerate(head_slices(k)):
        grad = pre[:, cols]
        parts.append((lower_mm(causal(grad, v[:, cols]), k[:, cols]) + mm_t(grad, state[i])).astype(BF16))
    found = jnp.concatenate(parts, axis=1)

    @pl.when(step < steps // 2)
    def _():
        first[...] = found

    @pl.when(step >= steps // 2)
    def _():
        second[...] = found


def own_kernel(pre, q, k, v, key_local, value_local):
    for cols in head_slices(q):
        grad, qh = pre[:, cols], q[:, cols]
        key_local[:, cols] = upper_mm(causal(grad, v[:, cols]), qh)
        value_local[:, cols] = upper_mm(causal(qh, k[:, cols]), grad)


def key_value_kernel(key_local, value_local, k, v, state, key_grad, value_grad):
    for i, cols in enumerate(head_slices(k)):
        key_grad[:, cols] = (key_local[:, cols] + mm_t(v[:, cols], state[i])).astype(BF16)
        value_grad[:, cols] = (value_local[:, cols] + mm(k[:, cols], state[i])).astype(BF16)


def without(kernel, first, count):
    return lambda *refs: kernel(*refs[:first], *refs[first + count :])


def by_heads(kernel, args, outs, waits=()):
    tokens = next(a.shape[0] for kind, a in args if kind == "rows")
    width = next(a.shape[1] for kind, a in args if kind == "rows")
    pair = 2 * HEAD_DIM
    count = width // pair
    half = count // 2
    specs = {
        "rows": pl.BlockSpec((tokens, pair), lambda i: (0, i)),
        "first": pl.BlockSpec((tokens, pair), lambda i: (0, jnp.minimum(i, half - 1))),
        "second": pl.BlockSpec((tokens, pair), lambda i: (0, jnp.maximum(i - half, 0))),
        "heads": pl.BlockSpec((2, HEAD_DIM, HEAD_DIM), lambda i: (i, 0, 0)),
        "gain": pl.BlockSpec((1, pair), lambda i: (0, i)),
    }
    for kind, a in args:
        if kind == "whole":
            specs[kind] = pl.BlockSpec(a.shape, lambda i: (0, 0))
        if kind == "weight":
            specs[kind] = pl.BlockSpec((pair, a.shape[1]), lambda i: (i, 0))
    shapes = {
        "rows": (tokens, width),
        "first": (tokens, width // 2),
        "second": (tokens, width // 2),
        "heads": (2 * count, HEAD_DIM, HEAD_DIM),
    }
    return pl.pallas_call(
        without(kernel, len(args), len(waits)),
        grid=(count,),
        in_specs=[specs[kind] for kind, _ in args] + [pl.BlockSpec(memory_space=pl.ANY)] * len(waits),
        out_specs=[specs[kind] for kind, _ in outs],
        out_shape=[jax.ShapeDtypeStruct(shapes[kind], dtype) for kind, dtype in outs],
        compiler_params=PARAMS,
        cost_estimate=COST,
    )(*[a for _, a in args], *waits)


def term_kernel(turned, adds, index, mine, theirs, grad, other, *rest):
    out = rest[-1]
    if turned:
        total = t_mm(grad[...], mine[...]) + t_mm(other[...], theirs[...])
    else:
        total = t_mm(mine[...], grad[...]) + t_mm(theirs[...], other[...])
    for ref in rest[:adds]:
        total = total + ref[...].astype(F32)
    out[...] = total.astype(out.dtype)


def term(features, grads, block, cols, turned, owned, start, count, received, waits, target=None):
    mine, theirs, index = features
    grad, other = grads
    tokens, chunks = grad.shape[0], index.shape[0] // 2

    def tile(offset):
        if turned:
            return pl.BlockSpec((cols, owned), lambda r, ix: (0, r + offset))
        return pl.BlockSpec((owned, cols), lambda r, ix: (r + offset, 0))

    rows = pl.BlockSpec((tokens, cols), lambda r, ix: (0, block))
    in_specs = [
        pl.BlockSpec((tokens, owned), lambda r, ix: (0, ix[start + r])),
        pl.BlockSpec((tokens, owned), lambda r, ix: (0, ix[chunks + start + r])),
        rows,
        rows,
    ]
    in_specs += [tile(start - begun) for _, begun in received]
    in_specs += [pl.BlockSpec(memory_space=pl.ANY)] * len(waits)
    operands = [index, mine, theirs, grad, other, *[a for a, _ in received], *waits]
    aliases = {}
    if target is None:
        out_spec, dtype = tile(0), BF16
        shape = (cols, count * owned) if turned else (count * owned, cols)
    else:
        old, shape, place = target
        dtype = F32
        out_spec = pl.BlockSpec((None,) * (len(shape) - 2) + ((cols, owned) if turned else (owned, cols)), lambda r, ix: place)
        if old is not None:
            aliases = {len(operands): 0}
            operands.append(old)
            in_specs.append(pl.BlockSpec(memory_space=pl.ANY))
    return pl.pallas_call(
        functools.partial(term_kernel, turned, len(received)),
        grid_spec=pltpu.PrefetchScalarGridSpec(
            num_scalar_prefetch=1, grid=(count,), in_specs=in_specs, out_specs=out_spec
        ),
        out_shape=jax.ShapeDtypeStruct(shape, dtype),
        input_output_aliases=aliases,
        compiler_params=PARAMS,
        cost_estimate=COST,
    )(*operands)


def body(layer_input, query_rows, key_rows, value_rows, out_weight, norm_gain, cotangent):
    size, position = lax.axis_size("seq"), lax.axis_index("seq")
    head_size, head_place = lax.axis_size("head"), lax.axis_index("head")
    bits = size.bit_length() - 1
    gather_bit = 1
    halving = [bit for bit in range(bits) if bit != gather_bit]
    tokens, width = query_rows.shape
    model = out_weight.shape[1]
    owned = model // size

    chunks = 1 << len(halving)
    order = []
    for j in range(chunks):
        toggled = 0
        for i, bit in enumerate(halving):
            if not (j >> (len(halving) - 1 - i)) & 1:
                toggled |= 1 << bit
        order.append(position ^ toggled)
    there = jnp.stack(order).astype(jnp.int32)
    packed = jnp.arange(chunks, dtype=jnp.int32)

    paired = head_size == 4 and width == 2 * owned
    aligned = (head_place & 1) == ((position >> 1) & 1)

    def across(array, seq_toggle, head_toggle):
        pairs = [
            (s * head_size + h, (s ^ seq_toggle) * head_size + (h ^ head_toggle))
            for s in range(size)
            for h in range(head_size)
            if (h ^ (s >> 1)) & 1
        ]
        return lax.ppermute(array, ("seq", "head"), pairs)

    def both(gathered):
        share = chunks * owned // head_size
        send = jnp.concatenate(
            [lax.dynamic_slice_in_dim(gathered, (at ^ (1 << gather_bit)) * owned, owned, 1) for at in order], axis=1
        )
        send = lax.dynamic_slice_in_dim(send, head_place * share, share, 1)
        theirs = lax.all_gather(flip(send, gather_bit), "head", axis=1, tiled=True)
        return gathered, theirs, jnp.concatenate([there, packed])

    gain = norm_gain.reshape(1, width)
    q, k, v = ("rows", query_rows), ("rows", key_rows), ("rows", value_rows)

    gathered_cot = lax.all_gather(cotangent, "head", axis=1, tiled=True)

    block_state, block_low = by_heads(state_kernel, [k, v], [("heads", F32), ("heads", BF16)])
    state_parts, sent, came = entering(block_state, block_low, False)
    (local,) = by_heads(local_kernel, [q, k, v], [("rows", F32)], [sent[-1]])
    if paired:
        partner = after(across(cotangent, 2, 1), came[1])
        partner_half = after(across(partner[:, owned:], 0, 1), local)
        partner_half = jnp.where(aligned, partner_half, partner[:, :owned])
    state_low = (state_parts[0] + after(state_parts[1], local).astype(F32)).astype(BF16)
    attention, *gated = by_heads(
        gated_kernel,
        [("rows", local), q, ("heads", state_low), ("gain", gain)],
        [("rows", F32), ("first", BF16), ("second", BF16)],
    )
    if paired:
        partner_cot = lax.all_gather(partner_half, "head", axis=1, tiled=True)
        side = 1 ^ ((position >> 1) & 1) ^ (there & 1)
        both_cot = gathered_cot, partner_cot, jnp.concatenate([there, (there >> 2) * 2 + side])
        swapped = across(after(layer_input, came[1]), 2, 1)
        swapped = jnp.where(aligned, layer_input, after(swapped, attention))
        gathered_input = lax.all_gather(swapped, "head", axis=1, tiled=True)
        both_input = gathered_input, gathered_input, jnp.concatenate([there, there ^ 2])
    else:
        both_cot = both(gathered_cot)
        both_input = both(lax.all_gather(layer_input, "head", axis=1, tiled=True))
    gated = [(part, flip(part, gather_bit)) for part in gated]

    pre, grad_block, grad_block_low = by_heads(
        pre_kernel,
        [("whole", gathered_cot), ("weight", out_weight), ("rows", attention), q, ("gain", gain)],
        [("rows", BF16), ("heads", F32), ("heads", BF16)],
    )
    grad_parts, sent, came = entering(grad_block, grad_block_low, True)
    query_grad = by_heads(
        query_kernel,
        [("rows", pre), k, v, ("heads", state_low)],
        [("first", BF16), ("second", BF16)],
        [gated[0][1]],
    )
    query_grad = [(part, flip(after(part, came[1]), gather_bit)) for part in query_grad]
    key_local, value_local = by_heads(
        own_kernel,
        [("rows", pre), q, k, v],
        [("rows", F32), ("rows", F32)],
        [query_grad[0][0], sent[1]],
    )
    grad_low = (grad_parts[0] + grad_parts[1].astype(F32)).astype(BF16)
    key_grad, value_grad = by_heads(
        key_value_kernel,
        [("rows", key_local), ("rows", value_local), k, v, ("heads", grad_low)],
        [("rows", BF16), ("rows", BF16)],
    )
    key_grad = key_grad, flip(key_grad, gather_bit)
    value_grad = value_grad, flip(after(value_grad, key_grad[1]), gather_bit)

    half = width // 2
    pieces = [(both_cot, gated[i], 0, True, (i, 0)) for i in range(2)]
    pieces += [(both_input, query_grad[i], 0, False, (0, 0, i)) for i in range(2)]
    pieces += [(both_input, key_grad, i, False, (1, 0, i)) for i in range(2)]
    pieces += [(both_input, value_grad, i, False, (2, 0, i)) for i in range(2)]
    starts = [chunks - (chunks >> i) for i in range(len(halving) + 1)]
    shapes = {True: (width, owned), False: (3, owned, width)}
    targets = {True: None, False: None}
    received = {}
    last = [key_local, sent[-1]]

    def stage(i, n):
        features, (grad, other), block, turned, place = pieces[i]
        came = received.setdefault(i, [])
        final = n == len(halving)
        target = (targets[turned], shapes[turned], place) if final else None
        count = 1 if final else chunks >> (n + 1)
        out = term(features, (grad, other), block, half, turned, owned, starts[n], count, came, last, target)
        last[:] = [out]
        if final:
            targets[turned] = out
        else:
            came.append((flip(out, halving[n]), starts[n + 1]))

    stages = len(halving) + 1
    stage(0, 0)
    stage(1, 0)
    last.append(key_grad[0])
    for i in range(len(pieces)):
        for n in range(1, stages - 1):
            stage(i, n)
        if i + 2 < len(pieces):
            last.extend(([], key_grad[1:], value_grad[1:])[min(i, 2)])
            stage(i + 2, 0)
        if i >= 1:
            stage(i - 1, stages - 1)
    stage(len(pieces) - 1, stages - 1)
    return (targets[False].transpose(1, 0, 2), targets[True])


def solution(mesh):
    placed = (
        P("seq", "head"),
        P("seq", "head"),
        P("seq", "head"),
        P("seq", "head"),
        P("head", None),
        P("head"),
        P("seq", "head"),
    )
    return jax.shard_map(
        body,
        mesh=mesh,
        in_specs=placed,
        out_specs=(P("seq", None, "head"), P("head", "seq")),
        check_vma=False,
    )
```

```python
import functools

import jax
import jax.numpy as jnp
from jax import lax
from jax.experimental import pallas as pl
from jax.experimental.pallas import tpu as pltpu
from jax.sharding import PartitionSpec as P

HEAD_DIM = 128
F32 = jnp.float32
BF16 = jnp.bfloat16
PARAMS = pltpu.CompilerParams(vmem_limit_bytes=48 * 1024 * 1024)


COST = pl.CostEstimate(flops=10**10, bytes_accessed=1, transcendentals=0)


def after(array, *others):
    return lax.optimization_barrier((array, *others))[0]


def flip(array, bit):
    size = lax.axis_size("seq")
    return lax.ppermute(array, "seq", [(i, i ^ (1 << bit)) for i in range(size)])


def entering(block, low, reverse):
    size, position = lax.axis_size("seq"), lax.axis_index("seq")
    bits = size.bit_length() - 1
    total, before = block, jnp.zeros_like(block)
    sent, came = [], []
    for bit in range(bits):
        step = 1 << bit
        sent.append(low)
        if bit < bits - 1:
            came.append(flip(low, bit))
            new = came[-1].astype(F32)
            mine = (position >> bit) & 1
            before = before + jnp.where(mine == (0 if reverse else 1), new, 0.0)
            total = total + new
            low = total.astype(BF16)
        else:
            pairs = [(i, i ^ step) for i in range(size) if bool(i & step) == reverse]
            came.append(lax.ppermute(low, "seq", pairs))
    return (before, came[-1]), sent, came


def mm(a, b):
    return lax.dot_general(a, b, (((1,), (0,)), ((), ())), preferred_element_type=F32)


def mm_t(a, b):
    return lax.dot_general(a, b, (((1,), (1,)), ((), ())), preferred_element_type=F32)


def t_mm(a, b):
    return lax.dot_general(a, b, (((0,), (0,)), ((), ())), preferred_element_type=F32)


def causal(a, b):
    half = a.shape[0] // 2
    rows = lax.broadcasted_iota(jnp.int32, (half, half), 0)
    cols = lax.broadcasted_iota(jnp.int32, (half, half), 1)
    lower = rows >= cols
    a0, a1, b0, b1 = a[:half], a[half:], b[:half], b[half:]
    first = jnp.where(lower, mm_t(a0, b0), 0.0).astype(BF16)
    cross = mm_t(a1, b0).astype(BF16)
    second = jnp.where(lower, mm_t(a1, b1), 0.0).astype(BF16)
    return first, cross, second


def lower_mm(tri, b):
    half = b.shape[0] // 2
    first, cross, second = tri
    return jnp.concatenate([mm(first, b[:half]), mm(cross, b[:half]) + mm(second, b[half:])], axis=0)


def upper_mm(tri, b):
    half = b.shape[0] // 2
    first, cross, second = tri
    return jnp.concatenate([t_mm(first, b[:half]) + t_mm(cross, b[half:]), t_mm(second, b[half:])], axis=0)


def head_slices(ref):
    return [slice(i * HEAD_DIM, (i + 1) * HEAD_DIM) for i in range(ref.shape[1] // HEAD_DIM)]


def state_kernel(k, v, out, low):
    for i, cols in enumerate(head_slices(k)):
        out[i] = t_mm(k[:, cols], v[:, cols])
        low[i] = out[i].astype(BF16)


def local_kernel(q, k, v, out):
    for cols in head_slices(q):
        out[:, cols] = lower_mm(causal(q[:, cols], k[:, cols]), v[:, cols])


def gated_kernel(local, q, state, gain, attention, first, second):
    step, steps = pl.program_id(0), pl.num_programs(0)
    parts = []
    for i, cols in enumerate(head_slices(q)):
        value = local[:, cols] + mm(q[:, cols], state[i])
        attention[:, cols] = value
        rms = jnp.sqrt(jnp.mean(value * value, axis=-1, keepdims=True) + 1e-05)
        parts.append((value / rms * gain[:, cols]).astype(BF16))
    found = jnp.concatenate(parts, axis=1)

    @pl.when(step < steps // 2)
    def _():
        first[...] = found

    @pl.when(step >= steps // 2)
    def _():
        second[...] = found


def gated_grad_kernel(cot, weight, out):
    out[...] = mm_t(cot[...], weight[...])


def pre_kernel(gated_grad, attention, q, gain, pre, out, low):
    for i, cols in enumerate(head_slices(q)):
        value = attention[:, cols]
        rms = jnp.sqrt(jnp.mean(value * value, axis=-1, keepdims=True) + 1e-05)
        normed = value / rms
        scaled = gated_grad[:, cols] * gain[:, cols]
        inner = jnp.mean(scaled * normed, axis=-1, keepdims=True)
        grad = ((scaled - normed * inner) / rms).astype(BF16)
        pre[:, cols] = grad
        out[i] = t_mm(q[:, cols], grad)
        low[i] = out[i].astype(BF16)


def query_kernel(pre, k, v, state, first, second):
    step, steps = pl.program_id(0), pl.num_programs(0)
    parts = []
    for i, cols in enumerate(head_slices(k)):
        grad = pre[:, cols]
        parts.append((lower_mm(causal(grad, v[:, cols]), k[:, cols]) + mm_t(grad, state[i])).astype(BF16))
    found = jnp.concatenate(parts, axis=1)

    @pl.when(step < steps // 2)
    def _():
        first[...] = found

    @pl.when(step >= steps // 2)
    def _():
        second[...] = found


def own_kernel(pre, q, k, v, key_local, value_local):
    for cols in head_slices(q):
        grad, qh = pre[:, cols], q[:, cols]
        key_local[:, cols] = upper_mm(causal(grad, v[:, cols]), qh)
        value_local[:, cols] = upper_mm(causal(qh, k[:, cols]), grad)


def key_value_kernel(key_local, value_local, k, v, state, key_first, key_second, value_first, value_second):
    step, steps = pl.program_id(0), pl.num_programs(0)
    keys, values = [], []
    for i, cols in enumerate(head_slices(k)):
        keys.append((key_local[:, cols] + mm_t(v[:, cols], state[i])).astype(BF16))
        values.append((value_local[:, cols] + mm(k[:, cols], state[i])).astype(BF16))
    keys, values = jnp.concatenate(keys, axis=1), jnp.concatenate(values, axis=1)

    @pl.when(step < steps // 2)
    def _():
        key_first[...] = keys
        value_first[...] = values

    @pl.when(step >= steps // 2)
    def _():
        key_second[...] = keys
        value_second[...] = values


def without(kernel, first, count):
    return lambda *refs: kernel(*refs[:first], *refs[first + count :])


def by_heads(kernel, args, outs, waits=()):
    tokens = args[0][1].shape[0]
    width = args[1][1].shape[0 if args[1][0] == "weight" else 1]
    pair = 2 * HEAD_DIM
    count = width // pair
    half = count // 2
    specs = {
        "rows": pl.BlockSpec((tokens, pair), lambda i: (0, i)),
        "first": pl.BlockSpec((tokens, pair), lambda i: (0, jnp.minimum(i, half - 1))),
        "second": pl.BlockSpec((tokens, pair), lambda i: (0, jnp.maximum(i - half, 0))),
        "heads": pl.BlockSpec((2, HEAD_DIM, HEAD_DIM), lambda i: (i, 0, 0)),
        "gain": pl.BlockSpec((1, pair), lambda i: (0, i)),
    }
    for kind, a in args:
        if kind == "whole":
            specs[kind] = pl.BlockSpec(a.shape, lambda i: (0, 0))
        if kind == "weight":
            specs[kind] = pl.BlockSpec((pair, a.shape[1]), lambda i: (i, 0))
    shapes = {
        "rows": (tokens, width),
        "first": (tokens, width // 2),
        "second": (tokens, width // 2),
        "heads": (2 * count, HEAD_DIM, HEAD_DIM),
    }
    return pl.pallas_call(
        without(kernel, len(args), len(waits)),
        grid=(count,),
        in_specs=[specs[kind] for kind, _ in args] + [pl.BlockSpec(memory_space=pl.ANY)] * len(waits),
        out_specs=[specs[kind] for kind, _ in outs],
        out_shape=[jax.ShapeDtypeStruct(shapes[kind], dtype) for kind, dtype in outs],
        compiler_params=PARAMS,
        cost_estimate=COST,
    )(*[a for _, a in args], *waits)


def term_kernel(turned, adds, index, mine, theirs, grad, other, *rest):
    out = rest[-1]
    if turned:
        total = t_mm(grad[...], mine[...]) + t_mm(other[...], theirs[...])
    else:
        total = t_mm(mine[...], grad[...]) + t_mm(theirs[...], other[...])
    for ref in rest[:adds]:
        total = total + ref[...].astype(F32)
    out[...] = total.astype(out.dtype)


def term(features, grads, block, cols, turned, owned, start, count, received, waits, target=None):
    mine, theirs, index = features
    grad, other = grads
    tokens, chunks = grad.shape[0], index.shape[0] // 2

    def tile(offset):
        if turned:
            return pl.BlockSpec((cols, owned), lambda r, ix: (0, r + offset))
        return pl.BlockSpec((owned, cols), lambda r, ix: (r + offset, 0))

    rows = pl.BlockSpec((tokens, cols), lambda r, ix: (0, block))
    in_specs = [
        pl.BlockSpec((tokens, owned), lambda r, ix: (0, ix[start + r])),
        pl.BlockSpec((tokens, owned), lambda r, ix: (0, ix[chunks + start + r])),
        rows,
        rows,
    ]
    in_specs += [tile(start - begun) for _, begun in received]
    in_specs += [pl.BlockSpec(memory_space=pl.ANY)] * len(waits)
    operands = [index, mine, theirs, grad, other, *[a for a, _ in received], *waits]
    aliases = {}
    if target is None:
        out_spec, dtype = tile(0), BF16
        shape = (cols, count * owned) if turned else (count * owned, cols)
    else:
        old, shape, place = target
        dtype = F32
        out_spec = pl.BlockSpec((None,) * (len(shape) - 2) + ((cols, owned) if turned else (owned, cols)), lambda r, ix: place)
        if old is not None:
            aliases = {len(operands): 0}
            operands.append(old)
            in_specs.append(pl.BlockSpec(memory_space=pl.ANY))
    return pl.pallas_call(
        functools.partial(term_kernel, turned, len(received)),
        grid_spec=pltpu.PrefetchScalarGridSpec(
            num_scalar_prefetch=1, grid=(count,), in_specs=in_specs, out_specs=out_spec
        ),
        out_shape=jax.ShapeDtypeStruct(shape, dtype),
        input_output_aliases=aliases,
        compiler_params=PARAMS,
        cost_estimate=COST,
    )(*operands)


def body(layer_input, query_rows, key_rows, value_rows, out_weight, norm_gain, cotangent):
    size, position = lax.axis_size("seq"), lax.axis_index("seq")
    head_size, head_place = lax.axis_size("head"), lax.axis_index("head")
    bits = size.bit_length() - 1
    gather_bit = 1
    halving = [bit for bit in range(bits) if bit != gather_bit]
    tokens, width = query_rows.shape
    model = out_weight.shape[1]
    owned = model // size

    chunks = 1 << len(halving)
    order = []
    for j in range(chunks):
        toggled = 0
        for i, bit in enumerate(halving):
            if not (j >> (len(halving) - 1 - i)) & 1:
                toggled |= 1 << bit
        order.append(position ^ toggled)
    there = jnp.stack(order).astype(jnp.int32)
    packed = jnp.arange(chunks, dtype=jnp.int32)

    paired = head_size == 4 and width == 2 * owned
    aligned = (head_place & 1) == ((position >> 1) & 1)

    def across(array, seq_toggle, head_toggle):
        pairs = [
            (s * head_size + h, (s ^ seq_toggle) * head_size + (h ^ head_toggle))
            for s in range(size)
            for h in range(head_size)
            if (h ^ (s >> 1)) & 1
        ]
        return lax.ppermute(array, ("seq", "head"), pairs)

    def both(gathered):
        share = chunks * owned // head_size
        send = jnp.concatenate(
            [lax.dynamic_slice_in_dim(gathered, (at ^ (1 << gather_bit)) * owned, owned, 1) for at in order], axis=1
        )
        send = lax.dynamic_slice_in_dim(send, head_place * share, share, 1)
        theirs = lax.all_gather(flip(send, gather_bit), "head", axis=1, tiled=True)
        return gathered, theirs, jnp.concatenate([there, packed])

    gain = norm_gain.reshape(1, width)
    q, k, v = ("rows", query_rows), ("rows", key_rows), ("rows", value_rows)

    gathered_cot = lax.all_gather(cotangent, "head", axis=1, tiled=True)

    block_state, block_low = by_heads(state_kernel, [k, v], [("heads", F32), ("heads", BF16)])
    state_parts, sent, came = entering(block_state, block_low, False)
    (local,) = by_heads(local_kernel, [q, k, v], [("rows", F32)], [sent[-1]])
    if paired:
        partner = after(across(cotangent, 2, 1), came[1])
        partner_half = across(partner[:, owned:], 0, 1)
    state_low = (state_parts[0] + after(state_parts[1], local).astype(F32)).astype(BF16)
    if paired:
        partner_half = jnp.where(aligned, after(partner_half, state_low), partner[:, :owned])
    attention, *gated = by_heads(
        gated_kernel,
        [("rows", local), q, ("heads", state_low), ("gain", gain)],
        [("rows", F32), ("first", BF16), ("second", BF16)],
    )
    if paired:
        partner_cot = lax.all_gather(partner_half, "head", axis=1, tiled=True)
        side = 1 ^ ((position >> 1) & 1) ^ (there & 1)
        both_cot = gathered_cot, partner_cot, jnp.concatenate([there, (there >> 2) * 2 + side])
        swapped = across(after(layer_input, came[1]), 2, 1)
        swapped = jnp.where(aligned, layer_input, after(swapped, attention))
        gathered_input = lax.all_gather(swapped, "head", axis=1, tiled=True)
        both_input = gathered_input, gathered_input, jnp.concatenate([there, there ^ 2])
    else:
        both_cot = both(gathered_cot)
        both_input = both(lax.all_gather(layer_input, "head", axis=1, tiled=True))
    gated = [(part, flip(part, gather_bit)) for part in gated]

    (gated_grad,) = by_heads(
        gated_grad_kernel, [("whole", gathered_cot), ("weight", out_weight)], [("rows", F32)], [attention]
    )
    pre, grad_block, grad_block_low = by_heads(
        pre_kernel,
        [("rows", gated_grad), ("rows", attention), q, ("gain", gain)],
        [("rows", BF16), ("heads", F32), ("heads", BF16)],
    )
    grad_parts, sent, came = entering(grad_block, grad_block_low, True)
    query_grad = by_heads(
        query_kernel,
        [("rows", pre), k, v, ("heads", state_low)],
        [("first", BF16), ("second", BF16)],
        [gated[0][1]],
    )
    query_grad = [(part, flip(after(part, came[1]), gather_bit)) for part in query_grad]
    key_local, value_local = by_heads(
        own_kernel,
        [("rows", pre), q, k, v],
        [("rows", F32), ("rows", F32)],
        [query_grad[0][0], sent[1]],
    )
    grad_low = (grad_parts[0] + grad_parts[1].astype(F32)).astype(BF16)
    late_grads = by_heads(
        key_value_kernel,
        [("rows", key_local), ("rows", value_local), k, v, ("heads", grad_low)],
        [("first", BF16), ("second", BF16)] * 2,
    )
    chained = []
    for part in late_grads:
        chained.append((part, flip(after(part, chained[-1][1]) if chained else part, gather_bit)))
    late_grads = chained

    half = width // 2
    quarter = half // 2
    pieces = [(both_cot, gated[0], quarter, i, True, (i, 0)) for i in range(2)]
    pieces += [(both_cot, gated[1], half, 0, True, (1, 0))]
    pieces += [(both_input, query_grad[i], half, 0, False, (0, 0, i)) for i in range(2)]
    pieces += [(both_input, late_grads[i], half, 0, False, (1 + i // 2, 0, i % 2)) for i in range(4)]
    starts = [chunks - (chunks >> i) for i in range(len(halving) + 1)]
    shapes = {True: (width, owned), False: (3, owned, width)}
    targets = {True: None, False: None}
    received = {}
    last = [key_local]

    def stage(i, n):
        features, (grad, other), cols, block, turned, place = pieces[i]
        came = received.setdefault(i, [])
        final = n == len(halving)
        target = (targets[turned], shapes[turned], place) if final else None
        count = 1 if final else chunks >> (n + 1)
        waits = [a for a in last if not final or a is not targets[turned]]
        out = term(features, (grad, other), block, cols, turned, owned, starts[n], count, came, waits, target)
        last[:] = [out]
        if final:
            targets[turned] = out
        else:
            came.append((flip(out, halving[n]), starts[n + 1]))

    stages = len(halving) + 1
    stage(0, 0)
    stage(1, 0)
    for i in range(len(pieces)):
        for n in range(1, stages - 1):
            stage(i, n)
        if i + 2 < len(pieces):
            if i == 0:
                last.append(late_grads[0][0])
            if 2 <= i < 6:
                last.append(late_grads[i - 2][1])
            stage(i + 2, 0)
        if i >= 1:
            stage(i - 1, stages - 1)
    stage(len(pieces) - 1, stages - 1)
    return (targets[False].transpose(1, 0, 2), targets[True])


def solution(mesh):
    placed = (
        P("seq", "head"),
        P("seq", "head"),
        P("seq", "head"),
        P("seq", "head"),
        P("head", None),
        P("head"),
        P("seq", "head"),
    )
    return jax.shard_map(
        body,
        mesh=mesh,
        in_specs=placed,
        out_specs=(P("seq", None, "head"), P("head", "seq")),
        check_vma=False,
    )
```

```python
import functools

import jax
import jax.numpy as jnp
from jax import lax
from jax.experimental import pallas as pl
from jax.experimental.pallas import tpu as pltpu
from jax.sharding import PartitionSpec as P

HEAD_DIM = 128
F32 = jnp.float32
BF16 = jnp.bfloat16
PARAMS = pltpu.CompilerParams(vmem_limit_bytes=48 * 1024 * 1024)


COST = pl.CostEstimate(flops=5*10**9, bytes_accessed=1, transcendentals=0)


def after(array, *others):
    return lax.optimization_barrier((array, *others))[0]


def flip(array, bit):
    size = lax.axis_size("seq")
    return lax.ppermute(array, "seq", [(i, i ^ (1 << bit)) for i in range(size)])


def entering(block, low, reverse, last=None):
    size, position = lax.axis_size("seq"), lax.axis_index("seq")
    bits = size.bit_length() - 1
    total, before = block, jnp.zeros_like(block)
    sent, came = [], []
    for bit in range(bits):
        step = 1 << bit
        if bit == bits - 1 and last is not None:
            low = after(low, last(came))
        sent.append(low)
        if bit < bits - 1:
            came.append(flip(low, bit))
            new = came[-1].astype(F32)
            mine = (position >> bit) & 1
            before = before + jnp.where(mine == (0 if reverse else 1), new, 0.0)
            total = total + new
            low = total.astype(BF16)
        else:
            pairs = [(i, i ^ step) for i in range(size) if bool(i & step) == reverse]
            came.append(lax.ppermute(low, "seq", pairs))
    return (before, came[-1]), sent, came


def mm(a, b):
    return lax.dot_general(a, b, (((1,), (0,)), ((), ())), preferred_element_type=F32)


def mm_t(a, b):
    return lax.dot_general(a, b, (((1,), (1,)), ((), ())), preferred_element_type=F32)


def t_mm(a, b):
    return lax.dot_general(a, b, (((0,), (0,)), ((), ())), preferred_element_type=F32)


def causal(a, b):
    half = a.shape[0] // 2
    rows = lax.broadcasted_iota(jnp.int32, (half, half), 0)
    cols = lax.broadcasted_iota(jnp.int32, (half, half), 1)
    lower = rows >= cols
    a0, a1, b0, b1 = a[:half], a[half:], b[:half], b[half:]
    first = jnp.where(lower, mm_t(a0, b0), 0.0).astype(BF16)
    cross = mm_t(a1, b0).astype(BF16)
    second = jnp.where(lower, mm_t(a1, b1), 0.0).astype(BF16)
    return first, cross, second


def lower_mm(tri, b):
    half = b.shape[0] // 2
    first, cross, second = tri
    return jnp.concatenate([mm(first, b[:half]), mm(cross, b[:half]) + mm(second, b[half:])], axis=0)


def upper_mm(tri, b):
    half = b.shape[0] // 2
    first, cross, second = tri
    return jnp.concatenate([t_mm(first, b[:half]) + t_mm(cross, b[half:]), t_mm(second, b[half:])], axis=0)


def head_slices(ref):
    return [slice(i * HEAD_DIM, (i + 1) * HEAD_DIM) for i in range(ref.shape[1] // HEAD_DIM)]


def state_kernel(k, v, out, low):
    for i, cols in enumerate(head_slices(k)):
        out[i] = t_mm(k[:, cols], v[:, cols])
        low[i] = out[i].astype(BF16)


def local_kernel(q, k, v, out):
    for cols in head_slices(q):
        out[:, cols] = lower_mm(causal(q[:, cols], k[:, cols]), v[:, cols])


def gated_kernel(local, q, state, gain, attention, first, second):
    step, steps = pl.program_id(0), pl.num_programs(0)
    parts = []
    for i, cols in enumerate(head_slices(q)):
        value = local[:, cols] + mm(q[:, cols], state[i])
        attention[:, cols] = value
        rms = jnp.sqrt(jnp.mean(value * value, axis=-1, keepdims=True) + 1e-05)
        parts.append((value / rms * gain[:, cols]).astype(BF16))
    found = jnp.concatenate(parts, axis=1)

    @pl.when(step < steps // 2)
    def _():
        first[...] = found

    @pl.when(step >= steps // 2)
    def _():
        second[...] = found


def gated_grad_kernel(cot, weight, out):
    out[...] = mm_t(cot[...], weight[...])


def pre_kernel(gated_grad, attention, q, gain, pre, out, low):
    for i, cols in enumerate(head_slices(q)):
        value = attention[:, cols]
        rms = jnp.sqrt(jnp.mean(value * value, axis=-1, keepdims=True) + 1e-05)
        normed = value / rms
        scaled = gated_grad[:, cols] * gain[:, cols]
        inner = jnp.mean(scaled * normed, axis=-1, keepdims=True)
        grad = ((scaled - normed * inner) / rms).astype(BF16)
        pre[:, cols] = grad
        out[i] = t_mm(q[:, cols], grad)
        low[i] = out[i].astype(BF16)


def query_kernel(pre, k, v, state, first, second):
    step, steps = pl.program_id(0), pl.num_programs(0)
    parts = []
    for i, cols in enumerate(head_slices(k)):
        grad = pre[:, cols]
        parts.append((lower_mm(causal(grad, v[:, cols]), k[:, cols]) + mm_t(grad, state[i])).astype(BF16))
    found = jnp.concatenate(parts, axis=1)

    @pl.when(step < steps // 2)
    def _():
        first[...] = found

    @pl.when(step >= steps // 2)
    def _():
        second[...] = found


def own_kernel(pre, q, k, v, key_local, value_local):
    for cols in head_slices(q):
        grad, qh = pre[:, cols], q[:, cols]
        key_local[:, cols] = upper_mm(causal(grad, v[:, cols]), qh)
        value_local[:, cols] = upper_mm(causal(qh, k[:, cols]), grad)


def key_value_kernel(key_local, value_local, k, v, state, key_grad, value_grad):
    for i, cols in enumerate(head_slices(k)):
        key_grad[:, cols] = (key_local[:, cols] + mm_t(v[:, cols], state[i])).astype(BF16)
        value_grad[:, cols] = (value_local[:, cols] + mm(k[:, cols], state[i])).astype(BF16)


def without(kernel, first, count):
    return lambda *refs: kernel(*refs[:first], *refs[first + count :])


def by_heads(kernel, args, outs, waits=()):
    tokens = args[0][1].shape[0]
    width = args[1][1].shape[0 if args[1][0] == "weight" else 1]
    pair = 2 * HEAD_DIM
    count = width // pair
    half = count // 2
    specs = {
        "rows": pl.BlockSpec((tokens, pair), lambda i: (0, i)),
        "first": pl.BlockSpec((tokens, pair), lambda i: (0, jnp.minimum(i, half - 1))),
        "second": pl.BlockSpec((tokens, pair), lambda i: (0, jnp.maximum(i - half, 0))),
        "heads": pl.BlockSpec((2, HEAD_DIM, HEAD_DIM), lambda i: (i, 0, 0)),
        "gain": pl.BlockSpec((1, pair), lambda i: (0, i)),
    }
    for kind, a in args:
        if kind == "whole":
            specs[kind] = pl.BlockSpec(a.shape, lambda i: (0, 0))
        if kind == "weight":
            specs[kind] = pl.BlockSpec((pair, a.shape[1]), lambda i: (i, 0))
    shapes = {
        "rows": (tokens, width),
        "first": (tokens, width // 2),
        "second": (tokens, width // 2),
        "heads": (2 * count, HEAD_DIM, HEAD_DIM),
    }
    return pl.pallas_call(
        without(kernel, len(args), len(waits)),
        grid=(count,),
        in_specs=[specs[kind] for kind, _ in args] + [pl.BlockSpec(memory_space=pl.ANY)] * len(waits),
        out_specs=[specs[kind] for kind, _ in outs],
        out_shape=[jax.ShapeDtypeStruct(shapes[kind], dtype) for kind, dtype in outs],
        compiler_params=PARAMS,
        cost_estimate=COST,
    )(*[a for _, a in args], *waits)


def term_kernel(turned, adds, index, mine, theirs, grad, other, *rest):
    out = rest[-1]
    if turned:
        total = t_mm(grad[...], mine[...]) + t_mm(other[...], theirs[...])
    else:
        total = t_mm(mine[...], grad[...]) + t_mm(theirs[...], other[...])
    for ref in rest[:adds]:
        total = total + ref[...].astype(F32)
    out[...] = total.astype(out.dtype)


def term(features, grads, block, cols, turned, owned, start, count, received, waits, target=None):
    mine, theirs, index = features
    grad, other = grads
    tokens, chunks = grad.shape[0], index.shape[0] // 2

    def tile(offset):
        if turned:
            return pl.BlockSpec((cols, owned), lambda r, ix: (0, r + offset))
        return pl.BlockSpec((owned, cols), lambda r, ix: (r + offset, 0))

    rows = pl.BlockSpec((tokens, cols), lambda r, ix: (0, block))
    in_specs = [
        pl.BlockSpec((tokens, owned), lambda r, ix: (0, ix[start + r])),
        pl.BlockSpec((tokens, owned), lambda r, ix: (0, ix[chunks + start + r])),
        rows,
        rows,
    ]
    in_specs += [tile(start - begun) for _, begun in received]
    in_specs += [pl.BlockSpec(memory_space=pl.ANY)] * len(waits)
    operands = [index, mine, theirs, grad, other, *[a for a, _ in received], *waits]
    aliases = {}
    if target is None:
        out_spec, dtype = tile(0), BF16
        shape = (cols, count * owned) if turned else (count * owned, cols)
    else:
        old, shape, place = target
        dtype = F32
        out_spec = pl.BlockSpec((None,) * (len(shape) - 2) + ((cols, owned) if turned else (owned, cols)), lambda r, ix: place)
        if old is not None:
            aliases = {len(operands): 0}
            operands.append(old)
            in_specs.append(pl.BlockSpec(memory_space=pl.ANY))
    return pl.pallas_call(
        functools.partial(term_kernel, turned, len(received)),
        grid_spec=pltpu.PrefetchScalarGridSpec(
            num_scalar_prefetch=1, grid=(count,), in_specs=in_specs, out_specs=out_spec
        ),
        out_shape=jax.ShapeDtypeStruct(shape, dtype),
        input_output_aliases=aliases,
        compiler_params=PARAMS,
        cost_estimate=COST,
    )(*operands)


def body(layer_input, query_rows, key_rows, value_rows, out_weight, norm_gain, cotangent):
    size, position = lax.axis_size("seq"), lax.axis_index("seq")
    head_size, head_place = lax.axis_size("head"), lax.axis_index("head")
    bits = size.bit_length() - 1
    gather_bit = 1
    halving = [bit for bit in range(bits) if bit != gather_bit]
    tokens, width = query_rows.shape
    model = out_weight.shape[1]
    owned = model // size

    chunks = 1 << len(halving)
    order = []
    for j in range(chunks):
        toggled = 0
        for i, bit in enumerate(halving):
            if not (j >> (len(halving) - 1 - i)) & 1:
                toggled |= 1 << bit
        order.append(position ^ toggled)
    there = jnp.stack(order).astype(jnp.int32)
    packed = jnp.arange(chunks, dtype=jnp.int32)

    paired = head_size == 4 and width == 2 * owned
    aligned = (head_place & 1) == ((position >> 1) & 1)

    def across(array, seq_toggle, head_toggle):
        pairs = [
            (s * head_size + h, (s ^ seq_toggle) * head_size + (h ^ head_toggle))
            for s in range(size)
            for h in range(head_size)
            if (h ^ (s >> 1)) & 1
        ]
        return lax.ppermute(array, ("seq", "head"), pairs)

    def both(gathered):
        share = chunks * owned // head_size
        send = jnp.concatenate(
            [lax.dynamic_slice_in_dim(gathered, (at ^ (1 << gather_bit)) * owned, owned, 1) for at in order], axis=1
        )
        send = lax.dynamic_slice_in_dim(send, head_place * share, share, 1)
        theirs = lax.all_gather(flip(send, gather_bit), "head", axis=1, tiled=True)
        return gathered, theirs, jnp.concatenate([there, packed])

    gain = norm_gain.reshape(1, width)
    q, k, v = ("rows", query_rows), ("rows", key_rows), ("rows", value_rows)

    gathered_cot = lax.all_gather(cotangent, "head", axis=1, tiled=True)

    block_state, block_low = by_heads(state_kernel, [k, v], [("heads", F32), ("heads", BF16)])
    state_parts, sent, came = entering(block_state, block_low, False)
    (local,) = by_heads(local_kernel, [q, k, v], [("rows", F32)], [sent[-1]])
    if paired:
        partner = after(across(cotangent, 2, 1), came[1])
        partner_half = across(partner[:, owned:], 0, 1)
    state_low = (state_parts[0] + after(state_parts[1], local).astype(F32)).astype(BF16)
    if paired:
        partner_half = jnp.where(aligned, after(partner_half, state_low), partner[:, :owned])
    attention, *gated = by_heads(
        gated_kernel,
        [("rows", local), q, ("heads", state_low), ("gain", gain)],
        [("rows", F32), ("first", BF16), ("second", BF16)],
    )
    if paired:
        partner_cot = lax.all_gather(partner_half, "head", axis=1, tiled=True)
        side = 1 ^ ((position >> 1) & 1) ^ (there & 1)
        both_cot = gathered_cot, partner_cot, jnp.concatenate([there, (there >> 2) * 2 + side])
        swapped = across(after(layer_input, came[1]), 2, 1)
        swapped = jnp.where(aligned, layer_input, after(swapped, attention))
        gathered_input = lax.all_gather(swapped, "head", axis=1, tiled=True)
        both_input = gathered_input, gathered_input, jnp.concatenate([there, there ^ 2])
    else:
        both_cot = both(gathered_cot)
        both_input = both(lax.all_gather(layer_input, "head", axis=1, tiled=True))
    gated = [(part, flip(part, gather_bit)) for part in gated]

    (gated_grad,) = by_heads(
        gated_grad_kernel, [("whole", gathered_cot), ("weight", out_weight)], [("rows", F32)], [attention]
    )
    pre, grad_block, grad_block_low = by_heads(
        pre_kernel,
        [("rows", gated_grad), ("rows", attention), q, ("gain", gain)],
        [("rows", BF16), ("heads", F32), ("heads", BF16)],
    )
    grad_parts, sent, came = entering(grad_block, grad_block_low, True)
    query_grad = by_heads(
        query_kernel,
        [("rows", pre), k, v, ("heads", state_low)],
        [("first", BF16), ("second", BF16)],
    )
    half = width // 2
    quarter = half // 2
    pieces = [(both_cot, gated[i], half, 0, True, (i, 0)) for i in range(2)]
    starts = [chunks - (chunks >> i) for i in range(len(halving) + 1)]
    shapes = {True: (width, owned), False: (3, owned, width)}
    targets = {True: None, False: None}
    received = {}
    last = [query_grad[0]]

    def stage(i, n):
        features, (grad, other), cols, block, turned, place = pieces[i]
        came = received.setdefault(i, [])
        final = n == len(halving)
        target = (targets[turned], shapes[turned], place) if final else None
        count = 1 if final else chunks >> (n + 1)
        waits = [a for a in last if not final or a is not targets[turned]]
        out = term(features, (grad, other), block, cols, turned, owned, starts[n], count, came, waits, target)
        last[:] = [out]
        if final:
            targets[turned] = out
        else:
            came.append((flip(out, halving[n]), starts[n + 1]))

    stages = len(halving) + 1
    stage(0, 0)
    stage(1, 0)
    key_local, value_local = by_heads(
        own_kernel,
        [("rows", pre), q, k, v],
        [("rows", F32), ("rows", F32)],
        [*last, sent[1]],
    )
    last.append(key_local)
    grad_low = (grad_parts[0] + grad_parts[1].astype(F32)).astype(BF16)
    late_grads = by_heads(
        key_value_kernel,
        [("rows", key_local), ("rows", value_local), k, v, ("heads", grad_low)],
        [("rows", BF16)] * 2,
    )
    first = [(part, flip(after(part, came[1]), gather_bit)) for part in query_grad]
    key_grad = late_grads[0], flip(late_grads[0], gather_bit)
    value_grad = late_grads[1], flip(after(late_grads[1], key_grad[1]), gather_bit)
    pieces += [(both_input, first[i], half, 0, False, (0, 0, i)) for i in range(2)]
    pieces += [(both_input, key_grad, half, i, False, (1, 0, i)) for i in range(2)]
    pieces += [(both_input, value_grad, half, i, False, (2, 0, i)) for i in range(2)]
    for i in range(len(pieces)):
        for n in range(1, stages - 1):
            stage(i, n)
        if i + 2 < len(pieces):
            if i == 1:
                last.append(late_grads[0])
            stage(i + 2, 0)
        if i >= 1:
            stage(i - 1, stages - 1)
    stage(len(pieces) - 1, stages - 1)
    return (targets[False].transpose(1, 0, 2), targets[True])


def solution(mesh):
    placed = (
        P("seq", "head"),
        P("seq", "head"),
        P("seq", "head"),
        P("seq", "head"),
        P("head", None),
        P("head"),
        P("seq", "head"),
    )
    return jax.shard_map(
        body,
        mesh=mesh,
        in_specs=placed,
        out_specs=(P("seq", None, "head"), P("head", "seq")),
        check_vma=False,
    )
```

```python
import functools

import jax
import jax.numpy as jnp
from jax import lax
from jax.experimental import pallas as pl
from jax.experimental.pallas import tpu as pltpu
from jax.sharding import PartitionSpec as P

HEAD_DIM = 128
F32 = jnp.float32
BF16 = jnp.bfloat16
PARAMS = pltpu.CompilerParams(vmem_limit_bytes=48 * 1024 * 1024)


COST = pl.CostEstimate(flops=5*10**9, bytes_accessed=1, transcendentals=0)


def after(array, *others):
    return lax.optimization_barrier((array, *others))[0]


def flip(array, bit):
    size = lax.axis_size("seq")
    return lax.ppermute(array, "seq", [(i, i ^ (1 << bit)) for i in range(size)])


def entering(block, low, reverse, last=None):
    size, position = lax.axis_size("seq"), lax.axis_index("seq")
    bits = size.bit_length() - 1
    total, before = block, jnp.zeros_like(block)
    sent, came = [], []
    for bit in range(bits):
        step = 1 << bit
        if bit == bits - 1 and last is not None:
            low = after(low, last(came))
        sent.append(low)
        if bit < bits - 1:
            came.append(flip(low, bit))
            new = came[-1].astype(F32)
            mine = (position >> bit) & 1
            before = before + jnp.where(mine == (0 if reverse else 1), new, 0.0)
            total = total + new
            low = total.astype(BF16)
        else:
            pairs = [(i, i ^ step) for i in range(size) if bool(i & step) == reverse]
            came.append(lax.ppermute(low, "seq", pairs))
    return (before, came[-1]), sent, came


def mm(a, b):
    return lax.dot_general(a, b, (((1,), (0,)), ((), ())), preferred_element_type=F32)


def mm_t(a, b):
    return lax.dot_general(a, b, (((1,), (1,)), ((), ())), preferred_element_type=F32)


def t_mm(a, b):
    return lax.dot_general(a, b, (((0,), (0,)), ((), ())), preferred_element_type=F32)


def causal(a, b):
    half = a.shape[0] // 2
    rows = lax.broadcasted_iota(jnp.int32, (half, half), 0)
    cols = lax.broadcasted_iota(jnp.int32, (half, half), 1)
    lower = rows >= cols
    a0, a1, b0, b1 = a[:half], a[half:], b[:half], b[half:]
    first = jnp.where(lower, mm_t(a0, b0), 0.0).astype(BF16)
    cross = mm_t(a1, b0).astype(BF16)
    second = jnp.where(lower, mm_t(a1, b1), 0.0).astype(BF16)
    return first, cross, second


def lower_mm(tri, b):
    half = b.shape[0] // 2
    first, cross, second = tri
    return jnp.concatenate([mm(first, b[:half]), mm(cross, b[:half]) + mm(second, b[half:])], axis=0)


def upper_mm(tri, b):
    half = b.shape[0] // 2
    first, cross, second = tri
    return jnp.concatenate([t_mm(first, b[:half]) + t_mm(cross, b[half:]), t_mm(second, b[half:])], axis=0)


def head_slices(ref):
    return [slice(i * HEAD_DIM, (i + 1) * HEAD_DIM) for i in range(ref.shape[1] // HEAD_DIM)]


def state_kernel(k, v, out, low):
    for i, cols in enumerate(head_slices(k)):
        out[i] = t_mm(k[:, cols], v[:, cols])
        low[i] = out[i].astype(BF16)


def local_kernel(q, k, v, out):
    for cols in head_slices(q):
        out[:, cols] = lower_mm(causal(q[:, cols], k[:, cols]), v[:, cols])


def gated_kernel(local, q, state, gain, attention, first, second):
    step, steps = pl.program_id(0), pl.num_programs(0)
    parts = []
    for i, cols in enumerate(head_slices(q)):
        value = local[:, cols] + mm(q[:, cols], state[i])
        attention[:, cols] = value
        rms = jnp.sqrt(jnp.mean(value * value, axis=-1, keepdims=True) + 1e-05)
        parts.append((value / rms * gain[:, cols]).astype(BF16))
    found = jnp.concatenate(parts, axis=1)

    @pl.when(step < steps // 2)
    def _():
        first[...] = found

    @pl.when(step >= steps // 2)
    def _():
        second[...] = found


def gated_grad_kernel(cot, weight, out):
    out[...] = mm_t(cot[...], weight[...])


def pre_kernel(gated_grad, attention, q, gain, pre, out, low):
    for i, cols in enumerate(head_slices(q)):
        value = attention[:, cols]
        rms = jnp.sqrt(jnp.mean(value * value, axis=-1, keepdims=True) + 1e-05)
        normed = value / rms
        scaled = gated_grad[:, cols] * gain[:, cols]
        inner = jnp.mean(scaled * normed, axis=-1, keepdims=True)
        grad = ((scaled - normed * inner) / rms).astype(BF16)
        pre[:, cols] = grad
        out[i] = t_mm(q[:, cols], grad)
        low[i] = out[i].astype(BF16)


def query_kernel(pre, k, v, state, first, second):
    step, steps = pl.program_id(0), pl.num_programs(0)
    parts = []
    for i, cols in enumerate(head_slices(k)):
        grad = pre[:, cols]
        parts.append((lower_mm(causal(grad, v[:, cols]), k[:, cols]) + mm_t(grad, state[i])).astype(BF16))
    found = jnp.concatenate(parts, axis=1)

    @pl.when(step < steps // 2)
    def _():
        first[...] = found

    @pl.when(step >= steps // 2)
    def _():
        second[...] = found


def own_kernel(pre, q, k, v, key_local, value_local):
    for cols in head_slices(q):
        grad, qh = pre[:, cols], q[:, cols]
        key_local[:, cols] = upper_mm(causal(grad, v[:, cols]), qh)
        value_local[:, cols] = upper_mm(causal(qh, k[:, cols]), grad)


def key_value_kernel(key_local, value_local, k, v, state, key_grad, value_grad):
    for i, cols in enumerate(head_slices(k)):
        key_grad[:, cols] = (key_local[:, cols] + mm_t(v[:, cols], state[i])).astype(BF16)
        value_grad[:, cols] = (value_local[:, cols] + mm(k[:, cols], state[i])).astype(BF16)


def without(kernel, first, count):
    return lambda *refs: kernel(*refs[:first], *refs[first + count :])


def by_heads(kernel, args, outs, waits=()):
    tokens = args[0][1].shape[0]
    width = args[1][1].shape[0 if args[1][0] == "weight" else 1]
    pair = 2 * HEAD_DIM
    count = width // pair
    half = count // 2
    specs = {
        "rows": pl.BlockSpec((tokens, pair), lambda i: (0, i)),
        "first": pl.BlockSpec((tokens, pair), lambda i: (0, jnp.minimum(i, half - 1))),
        "second": pl.BlockSpec((tokens, pair), lambda i: (0, jnp.maximum(i - half, 0))),
        "heads": pl.BlockSpec((2, HEAD_DIM, HEAD_DIM), lambda i: (i, 0, 0)),
        "gain": pl.BlockSpec((1, pair), lambda i: (0, i)),
    }
    for kind, a in args:
        if kind == "whole":
            specs[kind] = pl.BlockSpec(a.shape, lambda i: (0, 0))
        if kind == "weight":
            specs[kind] = pl.BlockSpec((pair, a.shape[1]), lambda i: (i, 0))
    shapes = {
        "rows": (tokens, width),
        "first": (tokens, width // 2),
        "second": (tokens, width // 2),
        "heads": (2 * count, HEAD_DIM, HEAD_DIM),
    }
    return pl.pallas_call(
        without(kernel, len(args), len(waits)),
        grid=(count,),
        in_specs=[specs[kind] for kind, _ in args] + [pl.BlockSpec(memory_space=pl.ANY)] * len(waits),
        out_specs=[specs[kind] for kind, _ in outs],
        out_shape=[jax.ShapeDtypeStruct(shapes[kind], dtype) for kind, dtype in outs],
        compiler_params=PARAMS,
        cost_estimate=COST,
    )(*[a for _, a in args], *waits)


def term_kernel(turned, adds, index, mine, theirs, grad, other, *rest):
    out = rest[-1]
    if turned:
        total = t_mm(grad[...], mine[...]) + t_mm(other[...], theirs[...])
    else:
        total = t_mm(mine[...], grad[...]) + t_mm(theirs[...], other[...])
    for ref in rest[:adds]:
        total = total + ref[...].astype(F32)
    out[...] = total.astype(out.dtype)


def term(features, grads, block, cols, turned, owned, start, count, received, waits, target=None):
    mine, theirs, index = features
    grad, other = grads
    tokens, chunks = grad.shape[0], index.shape[0] // 2

    def tile(offset):
        if turned:
            return pl.BlockSpec((cols, owned), lambda r, ix: (0, r + offset))
        return pl.BlockSpec((owned, cols), lambda r, ix: (r + offset, 0))

    rows = pl.BlockSpec((tokens, cols), lambda r, ix: (0, block))
    in_specs = [
        pl.BlockSpec((tokens, owned), lambda r, ix: (0, ix[start + r])),
        pl.BlockSpec((tokens, owned), lambda r, ix: (0, ix[chunks + start + r])),
        rows,
        rows,
    ]
    in_specs += [tile(start - begun) for _, begun in received]
    in_specs += [pl.BlockSpec(memory_space=pl.ANY)] * len(waits)
    operands = [index, mine, theirs, grad, other, *[a for a, _ in received], *waits]
    aliases = {}
    if target is None:
        out_spec, dtype = tile(0), BF16
        shape = (cols, count * owned) if turned else (count * owned, cols)
    else:
        old, shape, place = target
        dtype = F32
        out_spec = pl.BlockSpec((None,) * (len(shape) - 2) + ((cols, owned) if turned else (owned, cols)), lambda r, ix: place)
        if old is not None:
            aliases = {len(operands): 0}
            operands.append(old)
            in_specs.append(pl.BlockSpec(memory_space=pl.ANY))
    return pl.pallas_call(
        functools.partial(term_kernel, turned, len(received)),
        grid_spec=pltpu.PrefetchScalarGridSpec(
            num_scalar_prefetch=1, grid=(count,), in_specs=in_specs, out_specs=out_spec
        ),
        out_shape=jax.ShapeDtypeStruct(shape, dtype),
        input_output_aliases=aliases,
        compiler_params=PARAMS,
        cost_estimate=COST,
    )(*operands)


def body(layer_input, query_rows, key_rows, value_rows, out_weight, norm_gain, cotangent):
    size, position = lax.axis_size("seq"), lax.axis_index("seq")
    head_size, head_place = lax.axis_size("head"), lax.axis_index("head")
    bits = size.bit_length() - 1
    gather_bit = 1
    halving = [bit for bit in range(bits) if bit != gather_bit]
    tokens, width = query_rows.shape
    model = out_weight.shape[1]
    owned = model // size

    chunks = 1 << len(halving)
    order = []
    for j in range(chunks):
        toggled = 0
        for i, bit in enumerate(halving):
            if not (j >> (len(halving) - 1 - i)) & 1:
                toggled |= 1 << bit
        order.append(position ^ toggled)
    there = jnp.stack(order).astype(jnp.int32)
    packed = jnp.arange(chunks, dtype=jnp.int32)

    paired = head_size == 4 and width == 2 * owned
    aligned = (head_place & 1) == ((position >> 1) & 1)

    def across(array, seq_toggle, head_toggle):
        pairs = [
            (s * head_size + h, (s ^ seq_toggle) * head_size + (h ^ head_toggle))
            for s in range(size)
            for h in range(head_size)
            if (h ^ (s >> 1)) & 1
        ]
        return lax.ppermute(array, ("seq", "head"), pairs)

    def both(gathered):
        share = chunks * owned // head_size
        send = jnp.concatenate(
            [lax.dynamic_slice_in_dim(gathered, (at ^ (1 << gather_bit)) * owned, owned, 1) for at in order], axis=1
        )
        send = lax.dynamic_slice_in_dim(send, head_place * share, share, 1)
        theirs = lax.all_gather(flip(send, gather_bit), "head", axis=1, tiled=True)
        return gathered, theirs, jnp.concatenate([there, packed])

    gain = norm_gain.reshape(1, width)
    q, k, v = ("rows", query_rows), ("rows", key_rows), ("rows", value_rows)

    gathered_cot = lax.all_gather(cotangent, "head", axis=1, tiled=True)

    block_state, block_low = by_heads(state_kernel, [k, v], [("heads", F32), ("heads", BF16)])
    state_parts, sent, came_in = entering(block_state, block_low, False)
    (local,) = by_heads(local_kernel, [q, k, v], [("rows", F32)], [sent[-1]])
    if paired:
        partner = after(across(cotangent, 2, 1), came_in[1])
        partner_half = across(partner[:, owned:], 0, 1)
    state_low = (state_parts[0] + after(state_parts[1], local).astype(F32)).astype(BF16)
    if paired:
        partner_half = jnp.where(aligned, after(partner_half, state_low), partner[:, :owned])
    attention, *gated = by_heads(
        gated_kernel,
        [("rows", local), q, ("heads", state_low), ("gain", gain)],
        [("rows", F32), ("first", BF16), ("second", BF16)],
    )
    if paired:
        partner_cot = lax.all_gather(partner_half, "head", axis=1, tiled=True)
        side = 1 ^ ((position >> 1) & 1) ^ (there & 1)
        both_cot = gathered_cot, partner_cot, jnp.concatenate([there, (there >> 2) * 2 + side])
    else:
        both_cot = both(gathered_cot)
    gated = [(part, flip(part, gather_bit)) for part in gated]

    (gated_grad,) = by_heads(
        gated_grad_kernel, [("whole", gathered_cot), ("weight", out_weight)], [("rows", F32)], [attention]
    )
    if paired:
        swapped = across(after(layer_input, came_in[1]), 2, 1)
        swapped = jnp.where(aligned, layer_input, after(swapped, gated_grad))
        gathered_input = lax.all_gather(swapped, "head", axis=1, tiled=True)
        both_input = gathered_input, gathered_input, jnp.concatenate([there, there ^ 2])
    else:
        both_input = both(lax.all_gather(layer_input, "head", axis=1, tiled=True))
    pre, grad_block, grad_block_low = by_heads(
        pre_kernel,
        [("rows", gated_grad), ("rows", attention), q, ("gain", gain)],
        [("rows", BF16), ("heads", F32), ("heads", BF16)],
    )
    grad_parts, sent, came = entering(grad_block, grad_block_low, True)
    query_grad = by_heads(
        query_kernel,
        [("rows", pre), k, v, ("heads", state_low)],
        [("first", BF16), ("second", BF16)],
    )
    half = width // 2
    quarter = half // 2
    pieces = [(both_cot, gated[i], half, 0, True, (i, 0)) for i in range(2)]
    starts = [chunks - (chunks >> i) for i in range(len(halving) + 1)]
    shapes = {True: (width, owned), False: (3, owned, width)}
    targets = {True: None, False: None}
    received = {}
    last = [query_grad[0], sent[1]]

    def stage(i, n):
        features, (grad, other), cols, block, turned, place = pieces[i]
        came = received.setdefault(i, [])
        final = n == len(halving)
        target = (targets[turned], shapes[turned], place) if final else None
        count = 1 if final else chunks >> (n + 1)
        waits = [a for a in last if not final or a is not targets[turned]]
        out = term(features, (grad, other), block, cols, turned, owned, starts[n], count, came, waits, target)
        last[:] = [out]
        if final:
            targets[turned] = out
        else:
            came.append((flip(out, halving[n]), starts[n + 1]))

    stages = len(halving) + 1
    stage(0, 0)
    key_local, value_local = by_heads(
        own_kernel,
        [("rows", pre), q, k, v],
        [("rows", F32), ("rows", F32)],
        [*last, sent[1]],
    )
    last.append(key_local)
    stage(1, 0)
    grad_low = (grad_parts[0] + grad_parts[1].astype(F32)).astype(BF16)
    late_grads = by_heads(
        key_value_kernel,
        [("rows", key_local), ("rows", value_local), k, v, ("heads", grad_low)],
        [("rows", BF16)] * 2,
    )
    first = [(part, flip(after(part, sent[1]), gather_bit)) for part in query_grad]
    key_grad = late_grads[0], flip(late_grads[0], gather_bit)
    pieces += [(both_input, first[i], half, 0, False, (0, 0, i)) for i in range(2)]
    pieces += [(both_input, key_grad, half, i, False, (1, 0, i)) for i in range(2)]
    count = 2 * len(gated) + 4
    for i in range(count):
        for n in range(1, stages - 1):
            stage(i, n)
        if i + 2 < count:
            if i == 0:
                last.append(late_grads[0])
            stage(i + 2, 0)
            if i == 2:
                value_grad = late_grads[1], flip(after(late_grads[1], key_grad[1], last[0]), gather_bit)
                pieces += [(both_input, value_grad, half, j, False, (2, 0, j)) for j in range(2)]
        if i >= 1:
            stage(i - 1, stages - 1)
    stage(len(pieces) - 1, stages - 1)
    return (targets[False].transpose(1, 0, 2), targets[True])


def solution(mesh):
    placed = (
        P("seq", "head"),
        P("seq", "head"),
        P("seq", "head"),
        P("seq", "head"),
        P("head", None),
        P("head"),
        P("seq", "head"),
    )
    return jax.shard_map(
        body,
        mesh=mesh,
        in_specs=placed,
        out_specs=(P("seq", None, "head"), P("head", "seq")),
        check_vma=False,
    )
```

```python
import functools

import jax
import jax.numpy as jnp
from jax import lax
from jax.experimental import pallas as pl
from jax.experimental.pallas import tpu as pltpu
from jax.sharding import PartitionSpec as P

HEAD_DIM = 128
F32 = jnp.float32
BF16 = jnp.bfloat16
PARAMS = pltpu.CompilerParams(vmem_limit_bytes=48 * 1024 * 1024)


COST = pl.CostEstimate(flops=5*10**9, bytes_accessed=1, transcendentals=0)


def after(array, *others):
    return lax.optimization_barrier((array, *others))[0]


def flip(array, bit):
    size = lax.axis_size("seq")
    return lax.ppermute(array, "seq", [(i, i ^ (1 << bit)) for i in range(size)])


def entering(block, low, reverse, last=None):
    size, position = lax.axis_size("seq"), lax.axis_index("seq")
    bits = size.bit_length() - 1
    total, before = block, jnp.zeros_like(block)
    sent, came = [], []
    for bit in range(bits):
        step = 1 << bit
        if bit == bits - 1 and last is not None:
            low = after(low, last(came))
        sent.append(low)
        if bit < bits - 1:
            came.append(flip(low, bit))
            new = came[-1].astype(F32)
            mine = (position >> bit) & 1
            before = before + jnp.where(mine == (0 if reverse else 1), new, 0.0)
            total = total + new
            low = total.astype(BF16)
        else:
            pairs = [(i, i ^ step) for i in range(size) if bool(i & step) == reverse]
            came.append(lax.ppermute(low, "seq", pairs))
    return (before, came[-1]), sent, came


def mm(a, b):
    return lax.dot_general(a, b, (((1,), (0,)), ((), ())), preferred_element_type=F32)


def mm_t(a, b):
    return lax.dot_general(a, b, (((1,), (1,)), ((), ())), preferred_element_type=F32)


def t_mm(a, b):
    return lax.dot_general(a, b, (((0,), (0,)), ((), ())), preferred_element_type=F32)


def causal(a, b):
    half = a.shape[0] // 2
    rows = lax.broadcasted_iota(jnp.int32, (half, half), 0)
    cols = lax.broadcasted_iota(jnp.int32, (half, half), 1)
    lower = rows >= cols
    a0, a1, b0, b1 = a[:half], a[half:], b[:half], b[half:]
    first = jnp.where(lower, mm_t(a0, b0), 0.0).astype(BF16)
    cross = mm_t(a1, b0).astype(BF16)
    second = jnp.where(lower, mm_t(a1, b1), 0.0).astype(BF16)
    return first, cross, second


def lower_mm(tri, b):
    half = b.shape[0] // 2
    first, cross, second = tri
    return jnp.concatenate([mm(first, b[:half]), mm(cross, b[:half]) + mm(second, b[half:])], axis=0)


def upper_mm(tri, b):
    half = b.shape[0] // 2
    first, cross, second = tri
    return jnp.concatenate([t_mm(first, b[:half]) + t_mm(cross, b[half:]), t_mm(second, b[half:])], axis=0)


def head_slices(ref):
    return [slice(i * HEAD_DIM, (i + 1) * HEAD_DIM) for i in range(ref.shape[1] // HEAD_DIM)]


def state_kernel(k, v, out, low):
    for i, cols in enumerate(head_slices(k)):
        out[i] = t_mm(k[:, cols], v[:, cols])
        low[i] = out[i].astype(BF16)


def local_kernel(q, k, v, out):
    for cols in head_slices(q):
        out[:, cols] = lower_mm(causal(q[:, cols], k[:, cols]), v[:, cols])


def gated_kernel(local, q, state, gain, attention, first, second):
    step, steps = pl.program_id(0), pl.num_programs(0)
    parts = []
    for i, cols in enumerate(head_slices(q)):
        value = local[:, cols] + mm(q[:, cols], state[i])
        attention[:, cols] = value
        rms = jnp.sqrt(jnp.mean(value * value, axis=-1, keepdims=True) + 1e-05)
        parts.append((value / rms * gain[:, cols]).astype(BF16))
    found = jnp.concatenate(parts, axis=1)

    @pl.when(step < steps // 2)
    def _():
        first[...] = found

    @pl.when(step >= steps // 2)
    def _():
        second[...] = found


def gated_grad_kernel(cot, weight, out):
    out[...] = mm_t(cot[...], weight[...])


def pre_kernel(gated_grad, attention, q, gain, pre, out, low):
    for i, cols in enumerate(head_slices(q)):
        value = attention[:, cols]
        rms = jnp.sqrt(jnp.mean(value * value, axis=-1, keepdims=True) + 1e-05)
        normed = value / rms
        scaled = gated_grad[:, cols] * gain[:, cols]
        inner = jnp.mean(scaled * normed, axis=-1, keepdims=True)
        grad = ((scaled - normed * inner) / rms).astype(BF16)
        pre[:, cols] = grad
        out[i] = t_mm(q[:, cols], grad)
        low[i] = out[i].astype(BF16)


def query_kernel(pre, k, v, state, first, second):
    step, steps = pl.program_id(0), pl.num_programs(0)
    parts = []
    for i, cols in enumerate(head_slices(k)):
        grad = pre[:, cols]
        parts.append((lower_mm(causal(grad, v[:, cols]), k[:, cols]) + mm_t(grad, state[i])).astype(BF16))
    found = jnp.concatenate(parts, axis=1)

    @pl.when(step < steps // 2)
    def _():
        first[...] = found

    @pl.when(step >= steps // 2)
    def _():
        second[...] = found


def own_kernel(pre, q, k, v, key_local, value_local):
    for cols in head_slices(q):
        grad, qh = pre[:, cols], q[:, cols]
        key_local[:, cols] = upper_mm(causal(grad, v[:, cols]), qh)
        value_local[:, cols] = upper_mm(causal(qh, k[:, cols]), grad)


def key_value_kernel(key_local, value_local, k, v, state, key_grad, value_grad):
    for i, cols in enumerate(head_slices(k)):
        key_grad[:, cols] = (key_local[:, cols] + mm_t(v[:, cols], state[i])).astype(BF16)
        value_grad[:, cols] = (value_local[:, cols] + mm(k[:, cols], state[i])).astype(BF16)


def without(kernel, first, count):
    return lambda *refs: kernel(*refs[:first], *refs[first + count :])


def by_heads(kernel, args, outs, waits=()):
    tokens = args[0][1].shape[0]
    width = args[1][1].shape[0 if args[1][0] == "weight" else 1]
    pair = 2 * HEAD_DIM
    count = width // pair
    half = count // 2
    specs = {
        "rows": pl.BlockSpec((tokens, pair), lambda i: (0, i)),
        "first": pl.BlockSpec((tokens, pair), lambda i: (0, jnp.minimum(i, half - 1))),
        "second": pl.BlockSpec((tokens, pair), lambda i: (0, jnp.maximum(i - half, 0))),
        "heads": pl.BlockSpec((2, HEAD_DIM, HEAD_DIM), lambda i: (i, 0, 0)),
        "gain": pl.BlockSpec((1, pair), lambda i: (0, i)),
    }
    for kind, a in args:
        if kind == "whole":
            specs[kind] = pl.BlockSpec(a.shape, lambda i: (0, 0))
        if kind == "weight":
            specs[kind] = pl.BlockSpec((pair, a.shape[1]), lambda i: (i, 0))
    shapes = {
        "rows": (tokens, width),
        "first": (tokens, width // 2),
        "second": (tokens, width // 2),
        "heads": (2 * count, HEAD_DIM, HEAD_DIM),
    }
    return pl.pallas_call(
        without(kernel, len(args), len(waits)),
        grid=(count,),
        in_specs=[specs[kind] for kind, _ in args] + [pl.BlockSpec(memory_space=pl.ANY)] * len(waits),
        out_specs=[specs[kind] for kind, _ in outs],
        out_shape=[jax.ShapeDtypeStruct(shapes[kind], dtype) for kind, dtype in outs],
        compiler_params=PARAMS,
        cost_estimate=COST,
    )(*[a for _, a in args], *waits)


def term_kernel(turned, adds, index, mine, theirs, grad, other, *rest):
    out = rest[-1]
    if turned:
        total = t_mm(grad[...], mine[...]) + t_mm(other[...], theirs[...])
    else:
        total = t_mm(mine[...], grad[...]) + t_mm(theirs[...], other[...])
    for ref in rest[:adds]:
        total = total + ref[...].astype(F32)
    out[...] = total.astype(out.dtype)


def term(features, grads, block, cols, turned, owned, start, count, received, waits, target=None):
    mine, theirs, index = features
    grad, other = grads
    tokens, chunks = grad.shape[0], index.shape[0] // 2

    def tile(offset):
        if turned:
            return pl.BlockSpec((cols, owned), lambda r, ix: (0, r + offset))
        return pl.BlockSpec((owned, cols), lambda r, ix: (r + offset, 0))

    rows = pl.BlockSpec((tokens, cols), lambda r, ix: (0, block))
    in_specs = [
        pl.BlockSpec((tokens, owned), lambda r, ix: (0, ix[start + r])),
        pl.BlockSpec((tokens, owned), lambda r, ix: (0, ix[chunks + start + r])),
        rows,
        rows,
    ]
    in_specs += [tile(start - begun) for _, begun in received]
    in_specs += [pl.BlockSpec(memory_space=pl.ANY)] * len(waits)
    operands = [index, mine, theirs, grad, other, *[a for a, _ in received], *waits]
    aliases = {}
    if target is None:
        out_spec, dtype = tile(0), BF16
        shape = (cols, count * owned) if turned else (count * owned, cols)
    else:
        old, shape, place = target
        dtype = F32
        out_spec = pl.BlockSpec((None,) * (len(shape) - 2) + ((cols, owned) if turned else (owned, cols)), lambda r, ix: place)
        if old is not None:
            aliases = {len(operands): 0}
            operands.append(old)
            in_specs.append(pl.BlockSpec(memory_space=pl.ANY))
    return pl.pallas_call(
        functools.partial(term_kernel, turned, len(received)),
        grid_spec=pltpu.PrefetchScalarGridSpec(
            num_scalar_prefetch=1, grid=(count,), in_specs=in_specs, out_specs=out_spec
        ),
        out_shape=jax.ShapeDtypeStruct(shape, dtype),
        input_output_aliases=aliases,
        compiler_params=PARAMS,
        cost_estimate=COST,
    )(*operands)


def body(layer_input, query_rows, key_rows, value_rows, out_weight, norm_gain, cotangent):
    size, position = lax.axis_size("seq"), lax.axis_index("seq")
    head_size, head_place = lax.axis_size("head"), lax.axis_index("head")
    bits = size.bit_length() - 1
    gather_bit = 1
    halving = [bit for bit in range(bits) if bit != gather_bit]
    tokens, width = query_rows.shape
    model = out_weight.shape[1]
    owned = model // size

    chunks = 1 << len(halving)
    order = []
    for j in range(chunks):
        toggled = 0
        for i, bit in enumerate(halving):
            if not (j >> (len(halving) - 1 - i)) & 1:
                toggled |= 1 << bit
        order.append(position ^ toggled)
    there = jnp.stack(order).astype(jnp.int32)
    packed = jnp.arange(chunks, dtype=jnp.int32)

    paired = head_size == 4 and width == 2 * owned
    aligned = (head_place & 1) == ((position >> 1) & 1)

    def across(array, seq_toggle, head_toggle):
        pairs = [
            (s * head_size + h, (s ^ seq_toggle) * head_size + (h ^ head_toggle))
            for s in range(size)
            for h in range(head_size)
            if (h ^ (s >> 1)) & 1
        ]
        return lax.ppermute(array, ("seq", "head"), pairs)

    def both(gathered):
        share = chunks * owned // head_size
        send = jnp.concatenate(
            [lax.dynamic_slice_in_dim(gathered, (at ^ (1 << gather_bit)) * owned, owned, 1) for at in order], axis=1
        )
        send = lax.dynamic_slice_in_dim(send, head_place * share, share, 1)
        theirs = lax.all_gather(flip(send, gather_bit), "head", axis=1, tiled=True)
        return gathered, theirs, jnp.concatenate([there, packed])

    gain = norm_gain.reshape(1, width)
    q, k, v = ("rows", query_rows), ("rows", key_rows), ("rows", value_rows)

    gathered_cot = lax.all_gather(cotangent, "head", axis=1, tiled=True)

    block_state, block_low = by_heads(state_kernel, [k, v], [("heads", F32), ("heads", BF16)])
    state_parts, sent, came_in = entering(block_state, block_low, False)
    (local,) = by_heads(local_kernel, [q, k, v], [("rows", F32)], [sent[-1]])
    if paired:
        partner = after(across(cotangent, 2, 1), came_in[1])
        partner_half = across(partner[:, owned:], 0, 1)
    state_low = (state_parts[0] + after(state_parts[1], local).astype(F32)).astype(BF16)
    if paired:
        partner_half = jnp.where(aligned, after(partner_half, state_low), partner[:, :owned])
    attention, *gated = by_heads(
        gated_kernel,
        [("rows", local), q, ("heads", state_low), ("gain", gain)],
        [("rows", F32), ("first", BF16), ("second", BF16)],
    )
    if paired:
        partner_cot = lax.all_gather(partner_half, "head", axis=1, tiled=True)
        side = 1 ^ ((position >> 1) & 1) ^ (there & 1)
        both_cot = gathered_cot, partner_cot, jnp.concatenate([there, (there >> 2) * 2 + side])
    else:
        both_cot = both(gathered_cot)
    gated = [(part, flip(part, gather_bit)) for part in gated]

    (gated_grad,) = by_heads(
        gated_grad_kernel, [("whole", gathered_cot), ("weight", out_weight)], [("rows", F32)], [attention]
    )
    pre, grad_block, grad_block_low = by_heads(
        pre_kernel,
        [("rows", gated_grad), ("rows", attention), q, ("gain", gain)],
        [("rows", BF16), ("heads", F32), ("heads", BF16)],
    )
    grad_parts, sent, came = entering(grad_block, grad_block_low, True)
    if paired:
        swapped = across(after(layer_input, came_in[1]), 2, 1)
        swapped = jnp.where(aligned, layer_input, after(swapped, pre))
        gathered_input = lax.all_gather(swapped, "head", axis=1, tiled=True)
        both_input = gathered_input, gathered_input, jnp.concatenate([there, there ^ 2])
    else:
        both_input = both(lax.all_gather(layer_input, "head", axis=1, tiled=True))
    query_grad = by_heads(
        query_kernel,
        [("rows", pre), k, v, ("heads", state_low)],
        [("first", BF16), ("second", BF16)],
    )
    half = width // 2
    quarter = half // 2
    pieces = [(both_cot, gated[i], half, 0, True, (i, 0)) for i in range(2)]
    starts = [chunks - (chunks >> i) for i in range(len(halving) + 1)]
    shapes = {True: (width, owned), False: (3, owned, width)}
    targets = {True: None, False: None}
    received = {}
    last = [query_grad[0], sent[1]]

    def stage(i, n):
        features, (grad, other), cols, block, turned, place = pieces[i]
        came = received.setdefault(i, [])
        final = n == len(halving)
        target = (targets[turned], shapes[turned], place) if final else None
        count = 1 if final else chunks >> (n + 1)
        waits = [a for a in last if not final or a is not targets[turned]]
        out = term(features, (grad, other), block, cols, turned, owned, starts[n], count, came, waits, target)
        last[:] = [out]
        if final:
            targets[turned] = out
        else:
            came.append((flip(out, halving[n]), starts[n + 1]))

    stages = len(halving) + 1
    stage(0, 0)
    key_local, value_local = by_heads(
        own_kernel,
        [("rows", pre), q, k, v],
        [("rows", F32), ("rows", F32)],
        [*last, sent[1]],
    )
    last.append(key_local)
    stage(1, 0)
    first = [(part, flip(after(part, sent[1]), gather_bit)) for part in query_grad]
    pieces += [(both_input, first[i], half, 0, False, (0, 0, i)) for i in range(2)]
    count = 2 * len(gated) + 4
    for i in range(count):
        for n in range(1, stages - 1):
            stage(i, n)
        if i == 0:
            grad_low = (grad_parts[0] + grad_parts[1].astype(F32)).astype(BF16)
            late_grads = by_heads(
                key_value_kernel,
                [("rows", key_local), ("rows", value_local), k, v, ("heads", grad_low)],
                [("rows", BF16)] * 2,
                last,
            )
            key_grad = late_grads[0], flip(late_grads[0], gather_bit)
            pieces += [(both_input, key_grad, half, i, False, (1, 0, i)) for i in range(2)]
            last.append(late_grads[0])
        if i + 2 < count:
            stage(i + 2, 0)
            if i == 2:
                value_grad = late_grads[1], flip(after(late_grads[1], key_grad[1], last[0]), gather_bit)
                pieces += [(both_input, value_grad, half, j, False, (2, 0, j)) for j in range(2)]
        if i >= 1:
            stage(i - 1, stages - 1)
    stage(len(pieces) - 1, stages - 1)
    return (targets[False].transpose(1, 0, 2), targets[True])


def solution(mesh):
    placed = (
        P("seq", "head"),
        P("seq", "head"),
        P("seq", "head"),
        P("seq", "head"),
        P("head", None),
        P("head"),
        P("seq", "head"),
    )
    return jax.shard_map(
        body,
        mesh=mesh,
        in_specs=placed,
        out_specs=(P("seq", None, "head"), P("head", "seq")),
        check_vma=False,
    )
```

```python
import functools

import jax
import jax.numpy as jnp
from jax import lax
from jax.experimental import pallas as pl
from jax.experimental.pallas import tpu as pltpu
from jax.sharding import PartitionSpec as P

HEAD_DIM = 128
F32 = jnp.float32
BF16 = jnp.bfloat16
PARAMS = pltpu.CompilerParams(vmem_limit_bytes=48 * 1024 * 1024)


COST = pl.CostEstimate(flops=5*10**9, bytes_accessed=1, transcendentals=0)


def after(array, *others):
    return lax.optimization_barrier((array, *others))[0]


def flip(array, bit):
    size = lax.axis_size("seq")
    return lax.ppermute(array, "seq", [(i, i ^ (1 << bit)) for i in range(size)])


def entering(block, low, reverse, last=None):
    size, position = lax.axis_size("seq"), lax.axis_index("seq")
    bits = size.bit_length() - 1
    total, before = block, jnp.zeros_like(block)
    sent, came = [], []
    for bit in range(bits):
        step = 1 << bit
        if bit == bits - 1 and last is not None:
            low = after(low, last(came))
        sent.append(low)
        if bit < bits - 1:
            came.append(flip(low, bit))
            new = came[-1].astype(F32)
            mine = (position >> bit) & 1
            before = before + jnp.where(mine == (0 if reverse else 1), new, 0.0)
            total = total + new
            low = total.astype(BF16)
        else:
            pairs = [(i, i ^ step) for i in range(size) if bool(i & step) == reverse]
            came.append(lax.ppermute(low, "seq", pairs))
    return (before, came[-1]), sent, came


def mm(a, b):
    return lax.dot_general(a, b, (((1,), (0,)), ((), ())), preferred_element_type=F32)


def mm_t(a, b):
    return lax.dot_general(a, b, (((1,), (1,)), ((), ())), preferred_element_type=F32)


def t_mm(a, b):
    return lax.dot_general(a, b, (((0,), (0,)), ((), ())), preferred_element_type=F32)


def causal(a, b):
    half = a.shape[0] // 2
    rows = lax.broadcasted_iota(jnp.int32, (half, half), 0)
    cols = lax.broadcasted_iota(jnp.int32, (half, half), 1)
    lower = rows >= cols
    a0, a1, b0, b1 = a[:half], a[half:], b[:half], b[half:]
    first = jnp.where(lower, mm_t(a0, b0), 0.0).astype(BF16)
    cross = mm_t(a1, b0).astype(BF16)
    second = jnp.where(lower, mm_t(a1, b1), 0.0).astype(BF16)
    return first, cross, second


def lower_mm(tri, b):
    half = b.shape[0] // 2
    first, cross, second = tri
    return jnp.concatenate([mm(first, b[:half]), mm(cross, b[:half]) + mm(second, b[half:])], axis=0)


def upper_mm(tri, b):
    half = b.shape[0] // 2
    first, cross, second = tri
    return jnp.concatenate([t_mm(first, b[:half]) + t_mm(cross, b[half:]), t_mm(second, b[half:])], axis=0)


def head_slices(ref):
    return [slice(i * HEAD_DIM, (i + 1) * HEAD_DIM) for i in range(ref.shape[1] // HEAD_DIM)]


def state_kernel(k, v, out, low):
    for i, cols in enumerate(head_slices(k)):
        out[i] = t_mm(k[:, cols], v[:, cols])
        low[i] = out[i].astype(BF16)


def local_kernel(q, k, v, out):
    for cols in head_slices(q):
        out[:, cols] = lower_mm(causal(q[:, cols], k[:, cols]), v[:, cols])


def gated_kernel(local, q, state, gain, attention, first, second):
    step, steps = pl.program_id(0), pl.num_programs(0)
    parts = []
    for i, cols in enumerate(head_slices(q)):
        value = local[:, cols] + mm(q[:, cols], state[i])
        attention[:, cols] = value
        rms = jnp.sqrt(jnp.mean(value * value, axis=-1, keepdims=True) + 1e-05)
        parts.append((value / rms * gain[:, cols]).astype(BF16))
    found = jnp.concatenate(parts, axis=1)

    @pl.when(step < steps // 2)
    def _():
        first[...] = found

    @pl.when(step >= steps // 2)
    def _():
        second[...] = found


def gated_grad_kernel(cot, weight, out):
    out[...] = mm_t(cot[...], weight[...])


def pre_kernel(gated_grad, attention, q, gain, pre, out, low):
    for i, cols in enumerate(head_slices(q)):
        value = attention[:, cols]
        rms = jnp.sqrt(jnp.mean(value * value, axis=-1, keepdims=True) + 1e-05)
        normed = value / rms
        scaled = gated_grad[:, cols] * gain[:, cols]
        inner = jnp.mean(scaled * normed, axis=-1, keepdims=True)
        grad = ((scaled - normed * inner) / rms).astype(BF16)
        pre[:, cols] = grad
        out[i] = t_mm(q[:, cols], grad)
        low[i] = out[i].astype(BF16)


def query_kernel(pre, k, v, state, first, second):
    step, steps = pl.program_id(0), pl.num_programs(0)
    parts = []
    for i, cols in enumerate(head_slices(k)):
        grad = pre[:, cols]
        parts.append((lower_mm(causal(grad, v[:, cols]), k[:, cols]) + mm_t(grad, state[i])).astype(BF16))
    found = jnp.concatenate(parts, axis=1)

    @pl.when(step < steps // 2)
    def _():
        first[...] = found

    @pl.when(step >= steps // 2)
    def _():
        second[...] = found


def own_kernel(pre, q, k, v, key_local, value_local):
    for cols in head_slices(q):
        grad, qh = pre[:, cols], q[:, cols]
        key_local[:, cols] = upper_mm(causal(grad, v[:, cols]), qh)
        value_local[:, cols] = upper_mm(causal(qh, k[:, cols]), grad)


def key_value_kernel(key_local, value_local, k, v, state, key_grad, value_grad):
    for i, cols in enumerate(head_slices(k)):
        key_grad[:, cols] = (key_local[:, cols] + mm_t(v[:, cols], state[i])).astype(BF16)
        value_grad[:, cols] = (value_local[:, cols] + mm(k[:, cols], state[i])).astype(BF16)


def without(kernel, first, count):
    return lambda *refs: kernel(*refs[:first], *refs[first + count :])


def by_heads(kernel, args, outs, waits=()):
    tokens = args[0][1].shape[0]
    width = args[1][1].shape[0 if args[1][0] == "weight" else 1]
    pair = 2 * HEAD_DIM
    count = width // pair
    half = count // 2
    specs = {
        "rows": pl.BlockSpec((tokens, pair), lambda i: (0, i)),
        "first": pl.BlockSpec((tokens, pair), lambda i: (0, jnp.minimum(i, half - 1))),
        "second": pl.BlockSpec((tokens, pair), lambda i: (0, jnp.maximum(i - half, 0))),
        "heads": pl.BlockSpec((2, HEAD_DIM, HEAD_DIM), lambda i: (i, 0, 0)),
        "gain": pl.BlockSpec((1, pair), lambda i: (0, i)),
    }
    for kind, a in args:
        if kind == "whole":
            specs[kind] = pl.BlockSpec(a.shape, lambda i: (0, 0))
        if kind == "weight":
            specs[kind] = pl.BlockSpec((pair, a.shape[1]), lambda i: (i, 0))
    shapes = {
        "rows": (tokens, width),
        "first": (tokens, width // 2),
        "second": (tokens, width // 2),
        "heads": (2 * count, HEAD_DIM, HEAD_DIM),
    }
    return pl.pallas_call(
        without(kernel, len(args), len(waits)),
        grid=(count,),
        in_specs=[specs[kind] for kind, _ in args] + [pl.BlockSpec(memory_space=pl.ANY)] * len(waits),
        out_specs=[specs[kind] for kind, _ in outs],
        out_shape=[jax.ShapeDtypeStruct(shapes[kind], dtype) for kind, dtype in outs],
        compiler_params=PARAMS,
        cost_estimate=COST,
    )(*[a for _, a in args], *waits)


def term_kernel(turned, adds, index, mine, theirs, grad, other, *rest):
    out = rest[-1]
    if turned:
        total = t_mm(grad[...], mine[...]) + t_mm(other[...], theirs[...])
    else:
        total = t_mm(mine[...], grad[...]) + t_mm(theirs[...], other[...])
    for ref in rest[:adds]:
        total = total + ref[...].astype(F32)
    out[...] = total.astype(out.dtype)


def term(features, grads, block, cols, turned, owned, start, count, received, waits, target=None):
    mine, theirs, index = features
    grad, other = grads
    tokens, chunks = grad.shape[0], index.shape[0] // 2

    def tile(offset):
        if turned:
            return pl.BlockSpec((cols, owned), lambda r, ix: (0, r + offset))
        return pl.BlockSpec((owned, cols), lambda r, ix: (r + offset, 0))

    rows = pl.BlockSpec((tokens, cols), lambda r, ix: (0, block))
    in_specs = [
        pl.BlockSpec((tokens, owned), lambda r, ix: (0, ix[start + r])),
        pl.BlockSpec((tokens, owned), lambda r, ix: (0, ix[chunks + start + r])),
        rows,
        rows,
    ]
    in_specs += [tile(start - begun) for _, begun in received]
    in_specs += [pl.BlockSpec(memory_space=pl.ANY)] * len(waits)
    operands = [index, mine, theirs, grad, other, *[a for a, _ in received], *waits]
    aliases = {}
    if target is None:
        out_spec, dtype = tile(0), BF16
        shape = (cols, count * owned) if turned else (count * owned, cols)
    else:
        old, shape, place = target
        dtype = F32
        out_spec = pl.BlockSpec((None,) * (len(shape) - 2) + ((cols, owned) if turned else (owned, cols)), lambda r, ix: place)
        if old is not None:
            aliases = {len(operands): 0}
            operands.append(old)
            in_specs.append(pl.BlockSpec(memory_space=pl.ANY))
    return pl.pallas_call(
        functools.partial(term_kernel, turned, len(received)),
        grid_spec=pltpu.PrefetchScalarGridSpec(
            num_scalar_prefetch=1, grid=(count,), in_specs=in_specs, out_specs=out_spec
        ),
        out_shape=jax.ShapeDtypeStruct(shape, dtype),
        input_output_aliases=aliases,
        compiler_params=PARAMS,
        cost_estimate=COST,
    )(*operands)


def body(layer_input, query_rows, key_rows, value_rows, out_weight, norm_gain, cotangent):
    size, position = lax.axis_size("seq"), lax.axis_index("seq")
    head_size, head_place = lax.axis_size("head"), lax.axis_index("head")
    bits = size.bit_length() - 1
    gather_bit = 1
    halving = [bit for bit in range(bits) if bit != gather_bit]
    tokens, width = query_rows.shape
    model = out_weight.shape[1]
    owned = model // size

    chunks = 1 << len(halving)
    order = []
    for j in range(chunks):
        toggled = 0
        for i, bit in enumerate(halving):
            if not (j >> (len(halving) - 1 - i)) & 1:
                toggled |= 1 << bit
        order.append(position ^ toggled)
    there = jnp.stack(order).astype(jnp.int32)
    packed = jnp.arange(chunks, dtype=jnp.int32)

    paired = head_size == 4 and width == 2 * owned
    aligned = (head_place & 1) == ((position >> 1) & 1)

    def across(array, seq_toggle, head_toggle):
        pairs = [
            (s * head_size + h, (s ^ seq_toggle) * head_size + (h ^ head_toggle))
            for s in range(size)
            for h in range(head_size)
            if (h ^ (s >> 1)) & 1
        ]
        return lax.ppermute(array, ("seq", "head"), pairs)

    def both(gathered):
        share = chunks * owned // head_size
        send = jnp.concatenate(
            [lax.dynamic_slice_in_dim(gathered, (at ^ (1 << gather_bit)) * owned, owned, 1) for at in order], axis=1
        )
        send = lax.dynamic_slice_in_dim(send, head_place * share, share, 1)
        theirs = lax.all_gather(flip(send, gather_bit), "head", axis=1, tiled=True)
        return gathered, theirs, jnp.concatenate([there, packed])

    gain = norm_gain.reshape(1, width)
    q, k, v = ("rows", query_rows), ("rows", key_rows), ("rows", value_rows)

    gathered_cot = lax.all_gather(cotangent, "head", axis=1, tiled=True)

    block_state, block_low = by_heads(state_kernel, [k, v], [("heads", F32), ("heads", BF16)])
    state_parts, sent, came_in = entering(block_state, block_low, False)
    (local,) = by_heads(local_kernel, [q, k, v], [("rows", F32)], [sent[-1]])
    if paired:
        partner = after(across(cotangent, 2, 1), came_in[1])
        partner_half = across(partner[:, owned:], 0, 1)
    state_low = (state_parts[0] + after(state_parts[1], local).astype(F32)).astype(BF16)
    if paired:
        partner_half = jnp.where(aligned, after(partner_half, state_low), partner[:, :owned])
    attention, *gated = by_heads(
        gated_kernel,
        [("rows", local), q, ("heads", state_low), ("gain", gain)],
        [("rows", F32), ("first", BF16), ("second", BF16)],
    )
    if paired:
        partner_cot = lax.all_gather(partner_half, "head", axis=1, tiled=True)
        side = 1 ^ ((position >> 1) & 1) ^ (there & 1)
        both_cot = gathered_cot, partner_cot, jnp.concatenate([there, (there >> 2) * 2 + side])
    else:
        both_cot = both(gathered_cot)
    gated = [(part, flip(part, gather_bit)) for part in gated]

    (gated_grad,) = by_heads(
        gated_grad_kernel, [("whole", gathered_cot), ("weight", out_weight)], [("rows", F32)], [attention]
    )
    if paired:
        swapped = across(after(layer_input, came_in[1]), 2, 1)
        swapped = jnp.where(aligned, layer_input, after(swapped, gated_grad))
        gathered_input = lax.all_gather(swapped, "head", axis=1, tiled=True)
        both_input = gathered_input, gathered_input, jnp.concatenate([there, there ^ 2])
    else:
        both_input = both(lax.all_gather(layer_input, "head", axis=1, tiled=True))
    pre, grad_block, grad_block_low = by_heads(
        pre_kernel,
        [("rows", gated_grad), ("rows", attention), q, ("gain", gain)],
        [("rows", BF16), ("heads", F32), ("heads", BF16)],
    )
    grad_parts, sent, came = entering(grad_block, grad_block_low, True)
    query_grad = by_heads(
        query_kernel,
        [("rows", pre), k, v, ("heads", state_low)],
        [("first", BF16), ("second", BF16)],
    )
    half = width // 2
    quarter = half // 2
    pieces = [(both_cot, gated[i], half, 0, True, (i, 0)) for i in range(2)]
    starts = [chunks - (chunks >> i) for i in range(len(halving) + 1)]
    shapes = {True: (width, owned), False: (3, owned, width)}
    targets = {True: None, False: None}
    received = {}
    last = [query_grad[0], sent[1]]

    def stage(i, n):
        features, (grad, other), cols, block, turned, place = pieces[i]
        came = received.setdefault(i, [])
        final = n == len(halving)
        target = (targets[turned], shapes[turned], place) if final else None
        count = 1 if final else chunks >> (n + 1)
        waits = [a for a in last if not final or a is not targets[turned]]
        out = term(features, (grad, other), block, cols, turned, owned, starts[n], count, came, waits, target)
        last[:] = [out]
        if final:
            targets[turned] = out
        else:
            came.append((flip(out, halving[n]), starts[n + 1]))

    stages = len(halving) + 1
    stage(0, 0)
    key_local, value_local = by_heads(
        own_kernel,
        [("rows", pre), q, k, v],
        [("rows", F32), ("rows", F32)],
        [*last, sent[1]],
    )
    last.append(key_local)
    stage(1, 0)
    grad_low = (grad_parts[0] + grad_parts[1].astype(F32)).astype(BF16)
    late_grads = by_heads(
        key_value_kernel,
        [("rows", key_local), ("rows", value_local), k, v, ("heads", grad_low)],
        [("rows", BF16)] * 2,
    )
    first = [(part, flip(after(part, sent[1]), gather_bit)) for part in query_grad]
    pieces += [(both_input, first[i], half, 0, False, (0, 0, i)) for i in range(2)]
    count = 2 * len(gated) + 4
    for i in range(count):
        for n in range(1, stages - 1):
            stage(i, n)
        if i + 2 < count:
            if i == 0:
                last.append(late_grads[0])
            stage(i + 2, 0)
            if i == 0:
                key_grad = late_grads[0], flip(after(late_grads[0], last[0]), gather_bit)
                pieces += [(both_input, key_grad, half, j, False, (1, 0, j)) for j in range(2)]
            if i == 2:
                value_grad = late_grads[1], flip(after(late_grads[1], key_grad[1], last[0]), gather_bit)
                pieces += [(both_input, value_grad, half, j, False, (2, 0, j)) for j in range(2)]
        if i >= 1:
            stage(i - 1, stages - 1)
    stage(len(pieces) - 1, stages - 1)
    return (targets[False].transpose(1, 0, 2), targets[True])


def solution(mesh):
    placed = (
        P("seq", "head"),
        P("seq", "head"),
        P("seq", "head"),
        P("seq", "head"),
        P("head", None),
        P("head"),
        P("seq", "head"),
    )
    return jax.shard_map(
        body,
        mesh=mesh,
        in_specs=placed,
        out_specs=(P("seq", None, "head"), P("head", "seq")),
        check_vma=False,
    )
```
